128 devices in a mesh: dp: 16 (over z, x_lo, core), tensor: 8 (over y, x_hi).
Axes of the slice: x: 4 (x_hi: 2, x_lo: 2; x = x_hi * 2 + x_lo), y: 4, z: 4, core: 2. Of those that a mesh axis runs over, the one named last changes fastest.
Arguments:
- lm_grad: bfloat16 [8192, 3200], P(('dp', 'tensor')), may hold values from -6 to 6
- encoder_row: int32 [8192], P(('dp', 'tensor')), may hold values from 0 to 8191, as said below
- patch_count: int32 [16], replicated, may hold values from 256 to 512, as said below
- hidden_in: bfloat16 [8192, 3200], P(('dp', 'tensor'))
- norm_gain: float32 [3200], replicated, may hold values from 0.5 to 2
- layer_scale: float32 [3200], replicated, may hold values from 0.3 to 3
- up_weight: bfloat16 [3200, 12800], P(None, 'tensor'), may hold values from -0.109375 to 0.109375
- down_weight: bfloat16 [3200, 12800], P(None, 'tensor'), may hold values from -0.0546875 to 0.0546875
Outputs:
- input_grad: bfloat16 [8192, 3200], P(('dp', 'tensor'))
- up_grad: bfloat16 [3200, 12800], P('dp', 'tensor')
- down_grad: bfloat16 [3200, 12800], P('dp', 'tensor')
The draws below stay inside these ranges and needn't reach their ends.
Inputs may be any that keep to these rules, and one draw needn't show every extreme that they name: `encoder_row`: A permutation of the 8192 encoder rows. The 64 rows of one device hold exactly 4 rows of each image. `patch_count`: in every draw some image is full.
All inputs are finite; a program needn't handle non-finite values.
Results may differ from the reference program's by a relative error of at most 0.024.
Values may be sent and summed in bfloat16 or wider, within the bound.
No kernel may reach another device: no remote copies, remote signals or barrier semaphores. Data moves between devices by JAX's collectives and lax.ppermute only.
A program may use at most 192 MiB of HBM per device.

```python
import math
import jax
import jax.numpy as jnp
from jax import lax

D = 3200
FF = 12800
TOK_DEV = 64
GROUPS = 16
ROWS_GRP = 512
TOTAL = 8192
PER_GRP = 4


def draw_encoder_row(key, part):
    key = jax.random.fold_in(key, 11)
    first_key, second_key = jax.random.split(key)
    sources = TOTAL // TOK_DEV
    source_perm = jax.vmap(lambda one: jax.random.permutation(one, TOK_DEV))(jax.random.split(first_key, sources))
    target_perm = jax.vmap(lambda one: jax.random.permutation(one, ROWS_GRP))(jax.random.split(second_key, GROUPS))
    target_group = source_perm // PER_GRP
    within = source_perm % PER_GRP
    source_index = jnp.arange(sources, dtype=jnp.int32)[:, None]
    slot_index = source_index * PER_GRP + within
    slot = target_perm[target_group, slot_index]
    return (target_group * ROWS_GRP + slot).reshape(TOTAL).astype(jnp.int32)


def draw_patch_count(key, part):
    key = jax.random.fold_in(key, 23)
    first_key, second_key = jax.random.split(key)
    counts = jax.random.randint(first_key, (GROUPS,), ROWS_GRP // 2, ROWS_GRP + 1)
    full_image = jax.random.randint(second_key, (), 0, GROUPS)
    return counts.at[full_image].set(ROWS_GRP).astype(jnp.int32)


def draw_hidden_in(key, part):
    key = jax.random.fold_in(key, 37)
    base_key, row_key, column_key = jax.random.split(key, 3)
    row_scale = jnp.exp(jax.random.uniform(row_key, (TOTAL, 1), minval=math.log(0.3), maxval=math.log(3.0)))
    column_scale = jnp.exp(jax.random.uniform(column_key, (1, D), minval=math.log(0.5), maxval=math.log(2.0)))
    base = jax.random.normal(base_key, (TOTAL, D))
    return (base * row_scale * column_scale).astype(jnp.bfloat16)


def block_levels(rng, shape, cuts, least, top_value):
    loudness = 1.0
    for dim, parts in cuts:
        steps = jax.random.uniform(jax.random.fold_in(jax.random.fold_in(rng, 6), dim), (parts,), jnp.float32, least / len(cuts), top_value / len(cuts))
        loudness = loudness * jnp.repeat(jnp.exp(steps), shape[dim] // parts).reshape((-1,) + (1,) * (len(shape) - 1 - dim))
    return loudness


def normal_values(own_key, shape, spread, most, cuts=(), held_as=jnp.bfloat16):
    array = spread * jax.random.normal(own_key, shape, jnp.float32)
    if cuts:
        array = array * block_levels(own_key, shape, cuts, -0.22, 0.18)
    return jnp.clip(array, -most, most).astype(held_as)


def setup_inputs(seed: int = 0) -> dict:
    splits = jax.random.split(jax.random.key(seed), 9)
    lm_grad = normal_values(splits[0], (TOTAL, D), 1.0, 6.0, ((0, 128),))
    encoder_row = draw_encoder_row(jax.random.fold_in(splits[8], 71), 0)
    patch_count = draw_patch_count(jax.random.fold_in(splits[8], 71), 0)
    hidden_in = draw_hidden_in(jax.random.fold_in(splits[8], 71), 0)
    norm_gain = jnp.clip(jnp.exp(jax.random.uniform(splits[4], (D,), jnp.float32, math.log(0.5), math.log(2.0))), 0.5, 2.0)
    layer_scale = jnp.clip(jnp.exp(jax.random.uniform(splits[5], (D,), jnp.float32, math.log(0.3), math.log(3.0))), 0.3, 3.0)
    up_weight = normal_values(splits[6], (D, FF), D ** -0.5, 0.109375, ((1, 8),))
    down_weight = normal_values(splits[7], (D, FF), FF ** -0.5, 0.0546875, ((1, 8),))
    return {"lm_grad": lm_grad, "encoder_row": encoder_row, "patch_count": patch_count, "hidden_in": hidden_in, "norm_gain": norm_gain, "layer_scale": layer_scale, "up_weight": up_weight, "down_weight": down_weight}


def gelu_slope(value):
    return 0.5 * (1.0 + lax.erf(value * 0.7071067811865476)) + value * jnp.exp(-0.5 * value * value) * 0.3989422804014327

def reference(lm_grad, encoder_row, patch_count, hidden_in, norm_gain, layer_scale, up_weight, down_weight):
    grad_rows = jnp.zeros((TOTAL, D), jnp.bfloat16).at[encoder_row].set(lm_grad)
    grad_groups = grad_rows.reshape(GROUPS, ROWS_GRP, D)
    input_groups = hidden_in.reshape(GROUPS, ROWS_GRP, D)
    positions = jnp.arange(ROWS_GRP, dtype=jnp.int32)
    dims = (((0,), (0,)), ((), ()))

    def group_step(carry, packed):
        up_sum, down_sum = carry
        grad_group, input_group, limit = packed
        valid = (positions < limit)[:, None]
        scaled_grad = jnp.where(valid, layer_scale * grad_group.astype(jnp.float32), 0.0).astype(jnp.bfloat16)
        inputs = input_group.astype(jnp.float32)
        inverse_rms = lax.rsqrt(lax.optimization_barrier(jnp.mean(inputs * inputs, -1, keepdims=True)) + 1e-06)
        normed = (inputs * inverse_rms * norm_gain).astype(jnp.bfloat16)
        pre_act = jnp.dot(normed, up_weight, preferred_element_type=jnp.float32)
        activation = jax.nn.gelu(pre_act, approximate=False).astype(jnp.bfloat16)
        act_grad = jnp.dot(scaled_grad, down_weight, preferred_element_type=jnp.float32)
        pre_grad = (act_grad * gelu_slope(pre_act)).astype(jnp.bfloat16)
        normed_grad = lax.dot_general(pre_grad, up_weight, (((1,), (1,)), ((), ())), preferred_element_type=jnp.float32)
        weighted = norm_gain * normed_grad
        input_grad = (jnp.where(valid, grad_group.astype(jnp.float32), 0.0) + inverse_rms * weighted - inputs * inverse_rms ** 3 * lax.optimization_barrier(jnp.mean(weighted * inputs, -1, keepdims=True))).astype(jnp.bfloat16)
        up_part = lax.optimization_barrier(lax.dot_general(normed, pre_grad, dims, preferred_element_type=jnp.float32).astype(jnp.bfloat16))
        down_part = lax.optimization_barrier(lax.dot_general(scaled_grad, activation, dims, preferred_element_type=jnp.float32).astype(jnp.bfloat16))
        return ((up_sum + up_part.astype(jnp.float32), down_sum + down_part.astype(jnp.float32)), input_grad)
    start = (jnp.zeros((D, FF), jnp.float32), jnp.zeros((D, FF), jnp.float32))
    (up_sum, down_sum), input_grads = lax.scan(group_step, start, (grad_groups, input_groups, patch_count))
    grad_scale = 1.0 / jnp.sqrt(jnp.float32(TOTAL))
    return (input_grads.reshape(TOTAL, D), (up_sum * grad_scale).astype(jnp.bfloat16), (down_sum * grad_scale).astype(jnp.bfloat16))
```

```python
import math

import jax
import jax.numpy as jnp
from jax import lax
from jax.sharding import Mesh, PartitionSpec as P

F32 = jnp.float32
BF16 = jnp.bfloat16
Z, XL, CORE, Y, XH = 4, 2, 2, 4, 2
AXES = ("z", "xl", "core", "y", "xh")
ID_COLS = 128
ID_BASE = 32


def gelu_slope(value):
    return (
        0.5 * (1.0 + lax.erf(value * 0.7071067811865476))
        + value * jnp.exp(-0.5 * value * value) * 0.3989422804014327
    )


def shift(value, axis, size, step):
    return lax.ppermute(value, axis, [(i, (i + step) % size) for i in range(size)])


def add(*terms):
    total = terms[0].astype(F32)
    for term in terms[1:]:
        total = total + term.astype(F32)
    return total.astype(BF16)


def column_term(left_side, right_side):
    return lax.dot_general(
        left_side, right_side, (((0,), (0,)), ((), ())), preferred_element_type=F32
    ).astype(BF16)


def gather_rows(own):
    half = own.shape[0] // 2
    from_prev = shift(own, "y", Y, 1)
    from_next = shift(own, "y", Y, -1)
    other = shift(own, "xh", XH, 1)
    far = jnp.concatenate(
        [shift(from_prev[:half], "y", Y, 1), shift(from_next[half:], "y", Y, -1)], 0
    )
    other_prev = shift(other, "y", Y, 1)
    other_next = shift(other, "y", Y, -1)
    other_far = shift(far, "xh", XH, 1)
    return jnp.concatenate(
        [own, other, from_next, other_next, far, other_far, from_prev, other_prev], 0
    )


def scatter_rows(parts):
    rows = parts.shape[0] // 8
    half = rows // 2
    own, other, nxt, other_nxt, far, other_far, prev, other_prev = (
        parts[i * rows : (i + 1) * rows] for i in range(8)
    )
    got_far = shift(other_far, "xh", XH, 1)
    got_other_prev = shift(other_nxt, "y", Y, 1)
    got_other_next = shift(other_prev, "y", Y, -1)
    far = add(far, got_far)
    pass_prev = shift(far[:half], "y", Y, 1)
    pass_next = shift(far[half:], "y", Y, -1)
    got_other = shift(add(other, got_other_prev, got_other_next), "xh", XH, 1)
    nxt = jnp.concatenate([add(nxt[:half], pass_prev), nxt[half:]], 0)
    prev = jnp.concatenate([prev[:half], add(prev[half:], pass_next)], 0)
    got_prev = shift(nxt, "y", Y, 1)
    got_next = shift(prev, "y", Y, -1)
    return own.astype(F32) + got_prev.astype(F32) + got_next.astype(F32) + got_other.astype(F32)


def add_cores(grad):
    core = lax.axis_index("core")
    rows = grad.shape[0] // (Z * XL * CORE)
    view = grad.reshape(Z, XL, CORE, rows, grad.shape[1])
    give = lax.dynamic_index_in_dim(view, 1 - core, 2, keepdims=False)
    keep = lax.dynamic_index_in_dim(view, core, 2, keepdims=False)
    return add(keep, shift(give, "core", CORE, 1))


def z_first(grad):
    z, xl = lax.axis_index("z"), lax.axis_index("xl")
    total = add_cores(grad)

    def part(dz, x):
        return lax.dynamic_index_in_dim(total, (z + dz) % Z, 0, keepdims=False)[x]

    from_prev = shift(jnp.stack([part(2, 0), part(1, 1)]), "z", Z, 1)
    from_next = shift(jnp.stack([part(2, 1), part(3, 0)]), "z", Z, -1)
    acc_prev = shift(add(part(1, 0), from_prev[0]), "z", Z, 1)
    acc_next = shift(add(part(3, 1), from_next[0]), "z", Z, -1)
    sums = (
        add(part(0, 0), from_next[1], acc_prev),
        add(part(0, 1), from_prev[1], acc_next),
    )
    give = jnp.where(xl == 0, sums[1], sums[0])
    keep = jnp.where(xl == 0, sums[0], sums[1])
    return keep.astype(F32) + shift(give, "xl", XL, 1).astype(F32)


def x_first(grad):
    z, xl = lax.axis_index("z"), lax.axis_index("xl")
    total = add_cores(grad)
    rows = total.shape[2]
    cut = -(-rows // 16) * 8

    def part(dz, x):
        both = lax.dynamic_index_in_dim(total, (z + dz) % Z, 0, keepdims=False)
        return lax.dynamic_index_in_dim(both, x, 0, keepdims=False)

    early = shift(jnp.stack([part(2, 1 - xl), part(1, 1 - xl)]), "xl", XL, 1)
    late = shift(jnp.stack([part(3, 1 - xl), part(0, 1 - xl)]), "xl", XL, 1)
    two = add(part(2, xl), early[0])
    one = add(part(1, xl), early[1])
    three = add(part(3, xl), late[0])
    here = part(0, xl).astype(F32) + late[1].astype(F32)
    from_prev = shift(jnp.concatenate([two[:cut], one[cut:]], 0), "z", Z, 1)
    from_next = shift(jnp.concatenate([three[:cut], two[cut:]], 0), "z", Z, -1)
    acc_prev = shift(add(one[:cut], from_prev[:cut]), "z", Z, 1)
    acc_next = shift(add(three[cut:], from_next[cut:]), "z", Z, -1)
    return jnp.concatenate(
        [
            here[:cut] + from_next[:cut].astype(F32) + acc_prev.astype(F32),
            here[cut:] + from_prev[cut:].astype(F32) + acc_next.astype(F32),
        ],
        0,
    )


def on_device(
    lm_grad, encoder_row, patch_count, hidden_in, norm_gain, layer_scale, up_weight, down_weight
):
    tok_rows, width = hidden_in.shape
    members = Y * XH
    groups = Z * XL * CORE
    group_len = tok_rows * members
    per_pair = tok_rows // groups
    z, xl, core = lax.axis_index("z"), lax.axis_index("xl"), lax.axis_index("core")
    y, xh = lax.axis_index("y"), lax.axis_index("xh")
    group = (z * XL + xl) * CORE + core

    inputs = hidden_in.astype(F32)
    inverse_rms = lax.rsqrt(jnp.mean(inputs * inputs, -1, keepdims=True) + 1e-06)
    normed_own = (inputs * inverse_rms * norm_gain).astype(BF16)

    image, place = encoder_row // group_len, encoder_row % group_len
    index = jnp.arange(tok_rows, dtype=jnp.int32)
    same = (image[:, None] == image[None, :]) & (index[None, :] < index[:, None])
    slot = image * per_pair + jnp.sum(same.astype(jnp.int32), 1)
    sorter = (slot[None, :] == index[:, None]).astype(BF16)
    column = jnp.arange(ID_COLS, dtype=jnp.int32)[None, :]
    tags = jnp.where(
        column == 0,
        (place // ID_BASE)[:, None],
        jnp.where(column == 1, (place % ID_BASE)[:, None], 0),
    ).astype(BF16)
    rows = jnp.concatenate([lm_grad, tags], 1)
    ordered = jnp.dot(sorter, rows, preferred_element_type=F32).astype(BF16)
    arrived = lax.all_to_all(
        ordered.reshape(groups, per_pair, width + ID_COLS),
        ("z", "xl", "core"),
        split_axis=0,
        concat_axis=0,
    ).reshape(tok_rows, width + ID_COLS)

    normed = gather_rows(normed_own)
    joined = gather_rows(arrived)

    block = jnp.arange(members, dtype=jnp.int32)
    member = ((block // XH + y) % Y) * XH + (block % XH + xh) % XH
    positions = (member[:, None] * tok_rows + index[None, :]).reshape(group_len)
    limit = lax.dynamic_index_in_dim(patch_count, group, 0, keepdims=False)
    places = (
        joined[:, width].astype(jnp.int32) * ID_BASE + joined[:, width + 1].astype(jnp.int32)
    )
    chooser = (
        (positions[:, None] == places[None, :]) & (positions < limit)[:, None]
    ).astype(BF16)
    grads = jnp.dot(chooser, joined[:, :width], preferred_element_type=F32)
    scaled_grad = (grads * layer_scale).astype(BF16)
    own_grad = jnp.dot(chooser[:tok_rows], joined[:, :width], preferred_element_type=F32)

    pre_act = jnp.dot(normed, up_weight, preferred_element_type=F32)
    activation = jax.nn.gelu(pre_act, approximate=False).astype(BF16)
    slope = gelu_slope(pre_act)
    cut = 896
    down_a = z_first(column_term(scaled_grad, activation[:, :cut]))
    down_b = x_first(column_term(scaled_grad, activation[:, cut:]))
    act_grad = jnp.dot(scaled_grad, down_weight, preferred_element_type=F32)
    pre_grad = (act_grad * slope).astype(BF16)
    up_a = z_first(column_term(normed, pre_grad[:, :cut]))
    up_b = x_first(column_term(normed, pre_grad[:, cut:]))

    normed_grad = scatter_rows(
        lax.dot_general(
            pre_grad, up_weight, (((1,), (1,)), ((), ())), preferred_element_type=F32
        ).astype(BF16)
    )
    weighted = norm_gain * normed_grad
    input_grad = (
        own_grad
        + inverse_rms * weighted
        - inputs * inverse_rms**3 * jnp.mean(weighted * inputs, -1, keepdims=True)
    ).astype(BF16)
    grad_scale = 1.0 / math.sqrt(group_len * groups)
    return (
        input_grad,
        (jnp.concatenate([up_a, up_b], 1) * grad_scale).astype(BF16),
        (jnp.concatenate([down_a, down_b], 1) * grad_scale).astype(BF16),
    )


def solution(mesh):
    fine = Mesh(mesh.devices.reshape(Z, XL, CORE, Y, XH), AXES)
    dp, tensor = ("z", "xl", "core"), ("y", "xh")
    in_specs = (
        P(AXES, None),
        P(AXES),
        P(),
        P(AXES, None),
        P(),
        P(),
        P(None, tensor),
        P(None, tensor),
    )
    out_specs = (P(AXES, None), P(dp, tensor), P(dp, tensor))
    return jax.shard_map(
        on_device, mesh=fine, in_specs=in_specs, out_specs=out_specs, check_vma=False
    )
```

```python
import math

import jax
import jax.numpy as jnp
from jax import lax
from jax.experimental import pallas as pl
from jax.experimental.pallas import tpu as pltpu
from jax.sharding import Mesh, PartitionSpec as P

F32 = jnp.float32
BF16 = jnp.bfloat16
Z, XL, CORE, Y, XH = 4, 2, 2, 4, 2
AXES = ("z", "xl", "core", "y", "xh")
ID_COLS = 128
ID_BASE = 32


def gelu_slope(value):
    return (
        0.5 * (1.0 + lax.erf(value * 0.7071067811865476))
        + value * jnp.exp(-0.5 * value * value) * 0.3989422804014327
    )


def shift(value, axis, size, step):
    return lax.ppermute(value, axis, [(i, (i + step) % size) for i in range(size)])


def add32(*terms):
    total = terms[0].astype(F32)
    for term in terms[1:]:
        total = total + term.astype(F32)
    return total


def add(*terms):
    return add32(*terms).astype(BF16)


def together(*values):
    return lax.optimization_barrier(values)


def z_order(z, xl, core):
    pairs = [(2, 0), (1, 1), (2, 1), (3, 0), (1, 0), (3, 1), (0, 0), (0, 1)]
    return [((z + dz) % Z) * XL + x for dz, x in pairs]


def x_order(z, xl, core):
    pairs = [(dz, dx) for dx in (1, 0) for dz in (2, 1, 3, 0)]
    return [((z + dz) % Z) * XL + (xl + dx) % XL for dz, dx in pairs]


def slots_of(order, core):
    order = jnp.stack(order).astype(jnp.int32)
    block = jnp.arange(order.shape[0] * CORE, dtype=jnp.int32)
    place = jnp.sum(
        jnp.where(
            order[None, :] == (block // CORE)[:, None],
            jnp.arange(order.shape[0], dtype=jnp.int32)[None, :],
            0,
        ),
        1,
    )
    return jnp.where(block % CORE == core, order.shape[0], 0) + place


def grad_kernel(slots, left, right, after, *refs):
    del after
    outs, stage, sems = refs[:4], refs[4], refs[5]
    blocks = Z * XL * CORE
    rows = left.shape[1] // blocks
    per_out = blocks // 4
    step = blocks // Z
    for z in range(Z):
        product = lax.dot_general(
            left[:, z * step * rows : (z + 1) * step * rows],
            right[...],
            (((0,), (0,)), ((), ())),
            preferred_element_type=F32,
        ).astype(BF16)
        for i in range(step):
            j = z * step + i
            stage[j] = product[i * rows : (i + 1) * rows]
            slot = slots[j]
            for k, out in enumerate(outs):

                @pl.when(slot // per_out == k)
                def _(out=out, j=j, slot=slot):
                    pltpu.make_async_copy(
                        stage.at[j], out.at[slot % per_out], sems.at[j]
                    ).start()
    for j in range(blocks):
        pltpu.make_async_copy(stage.at[j], outs[0].at[0], sems.at[j]).wait()


def grad_blocks(left, right, slots, after):
    width, cols = left.shape[1], right.shape[1]
    blocks = Z * XL * CORE
    rows = width // blocks
    return pl.pallas_call(
        grad_kernel,
        out_shape=[jax.ShapeDtypeStruct((blocks // 4, rows, cols), BF16)] * 4,
        in_specs=[
            pl.BlockSpec(memory_space=pltpu.SMEM),
            pl.BlockSpec(memory_space=pltpu.VMEM),
            pl.BlockSpec(memory_space=pltpu.VMEM),
            pl.BlockSpec(memory_space=pl.ANY),
        ],
        out_specs=[pl.BlockSpec(memory_space=pl.ANY)] * 4,
        scratch_shapes=[
            pltpu.VMEM((blocks, rows, cols), BF16),
            pltpu.SemaphoreType.DMA((blocks,)),
        ],
        compiler_params=pltpu.CompilerParams(vmem_limit_bytes=40 * 1024 * 1024),
        cost_estimate=pl.CostEstimate(
            flops=2 * left.shape[0] * width * cols,
            bytes_accessed=2 * width * cols,
            transcendentals=0,
        ),
    )(slots, left, right, after)


def on_device(
    lm_grad, encoder_row, patch_count, hidden_in, norm_gain, layer_scale, up_weight, down_weight
):
    tok_rows, width = hidden_in.shape
    members = Y * XH
    groups = Z * XL * CORE
    group_len = tok_rows * members
    per_pair = tok_rows // groups
    z, xl, core = lax.axis_index("z"), lax.axis_index("xl"), lax.axis_index("core")
    y, xh = lax.axis_index("y"), lax.axis_index("xh")
    group = (z * XL + xl) * CORE + core

    inputs = hidden_in.astype(F32)
    inverse_rms = lax.rsqrt(jnp.mean(inputs * inputs, -1, keepdims=True) + 1e-06)
    normed_own = (inputs * inverse_rms * norm_gain).astype(BF16)

    image, place = encoder_row // group_len, encoder_row % group_len
    index = jnp.arange(tok_rows, dtype=jnp.int32)
    same = (image[:, None] == image[None, :]) & (index[None, :] < index[:, None])
    slot = image * per_pair + jnp.sum(same.astype(jnp.int32), 1)
    sorter = (slot[None, :] == index[:, None]).astype(BF16)
    column = jnp.arange(ID_COLS, dtype=jnp.int32)[None, :]
    tags = jnp.where(
        column == 0,
        (place // ID_BASE)[:, None],
        jnp.where(column == 1, (place % ID_BASE)[:, None], 0),
    ).astype(BF16)
    rows = jnp.concatenate([lm_grad, tags], 1)
    ordered = jnp.dot(sorter, rows, preferred_element_type=F32).astype(BF16)
    arrived = lax.all_to_all(
        ordered.reshape(groups, per_pair, width + ID_COLS),
        ("z", "xl", "core"),
        split_axis=0,
        concat_axis=0,
    ).reshape(tok_rows, width + ID_COLS)

    half = tok_rows // 2

    n_prev = shift(normed_own, "y", Y, 1)
    n_next = shift(normed_own, "y", Y, -1)
    n_other = shift(normed_own, "xh", XH, 1)
    n_prev, n_next, n_other, arrived = together(n_prev, n_next, n_other, arrived)
    n_far_a = shift(n_prev[:half], "y", Y, 1)
    n_far_b = shift(n_next[half:], "y", Y, -1)
    n_other_prev = shift(n_other, "y", Y, 1)
    n_other_next = shift(n_other, "y", Y, -1)
    g_other = shift(arrived, "xh", XH, 1)
    n_far_a, n_far_b, n_other_prev, n_other_next, g_other, arrived = together(
        n_far_a, n_far_b, n_other_prev, n_other_next, g_other, arrived
    )
    n_other_far_a = shift(n_other_prev[:half], "y", Y, 1)
    n_other_far_b = shift(n_other_next[half:], "y", Y, -1)
    g_prev = shift(arrived, "y", Y, 1)
    g_next = shift(arrived, "y", Y, -1)
    g_other_prev = shift(g_other, "y", Y, 1)
    g_other_next = shift(g_other, "y", Y, -1)
    g_prev, g_next, g_other_prev, g_other_next = together(
        g_prev, g_next, g_other_prev, g_other_next
    )
    g_far_a = shift(g_prev[:half], "y", Y, 1)
    g_far_b = shift(g_next[half:], "y", Y, -1)
    g_other_far_a = shift(g_other_prev[:half], "y", Y, 1)
    g_other_far_b = shift(g_other_next[half:], "y", Y, -1)
    normed = jnp.concatenate(
        [normed_own, n_other, n_next, n_other_next]
        + [n_far_a, n_far_b, n_other_far_a, n_other_far_b, n_prev, n_other_prev],
        0,
    )
    cut = 896
    pre_act_a = jnp.dot(normed, up_weight[:, :cut], preferred_element_type=F32)
    pre_act_b = jnp.dot(normed, up_weight[:, cut:], preferred_element_type=F32)
    activation_a = jax.nn.gelu(pre_act_a, approximate=False).astype(BF16)
    activation_b = jax.nn.gelu(pre_act_b, approximate=False).astype(BF16)
    slope_a, slope_b = gelu_slope(pre_act_a), gelu_slope(pre_act_b)
    (
        g_far_a, g_far_b, g_other_far_a, g_other_far_b,
        activation_a, activation_b, slope_a, slope_b, normed,
    ) = together(
        g_far_a, g_far_b, g_other_far_a, g_other_far_b,
        activation_a, activation_b, slope_a, slope_b, normed,
    )
    joined = jnp.concatenate(
        [arrived, g_other, g_next, g_other_next]
        + [g_far_a, g_far_b, g_other_far_a, g_other_far_b, g_prev, g_other_prev],
        0,
    )

    block = jnp.arange(members, dtype=jnp.int32)
    member = ((block // XH + y) % Y) * XH + (block % XH + xh) % XH
    positions = (member[:, None] * tok_rows + index[None, :]).reshape(group_len)
    limit = lax.dynamic_index_in_dim(patch_count, group, 0, keepdims=False)
    places = (
        joined[:, width].astype(jnp.int32) * ID_BASE + joined[:, width + 1].astype(jnp.int32)
    )
    chooser = (
        (positions[:, None] == places[None, :]) & (positions < limit)[:, None]
    ).astype(BF16)
    grads = jnp.dot(chooser, joined[:, :width], preferred_element_type=F32)
    scaled_grad = (grads * layer_scale).astype(BF16)
    own_grad = jnp.dot(chooser[:tok_rows], joined[:, :width], preferred_element_type=F32)

    z_slots = slots_of(z_order(z, xl, core), core)
    x_slots = slots_of(x_order(z, xl, core), core)
    d_give_a1, d_give_a2, d_keep_a1, d_keep_a2 = grad_blocks(
        scaled_grad, activation_a, z_slots, z_slots
    )
    d_give_b1, d_give_b2, d_keep_b1, d_keep_b2 = grad_blocks(
        scaled_grad, activation_b, x_slots, d_keep_a1
    )

    d_got_a1, d_got_a2, d_got_b1, d_got_b2 = (
        shift(give, "core", CORE, 1) for give in (d_give_a1, d_give_a2, d_give_b1, d_give_b2)
    )
    act_grad_a = jnp.dot(scaled_grad, down_weight[:, :cut], preferred_element_type=F32)
    act_grad_b = jnp.dot(scaled_grad, down_weight[:, cut:], preferred_element_type=F32)
    pre_grad_a = (act_grad_a * slope_a).astype(BF16)
    pre_grad_b = (act_grad_b * slope_b).astype(BF16)
    (
        d_got_a1, d_got_a2, d_got_b1, d_got_b2, pre_grad_a, pre_grad_b,
    ) = together(d_got_a1, d_got_a2, d_got_b1, d_got_b2, pre_grad_a, pre_grad_b)

    d_prev = shift(add(d_keep_a1[:2], d_got_a1[:2]), "z", Z, 1)
    d_next = shift(add(d_keep_a1[2:], d_got_a1[2:]), "z", Z, -1)
    d_x = shift(add(d_keep_b1, d_got_b1), "xl", XL, 1)
    u_give_a1, u_give_a2, u_keep_a1, u_keep_a2 = grad_blocks(
        normed, pre_grad_a, z_slots, d_keep_b1
    )
    u_give_b1, u_give_b2, u_keep_b1, u_keep_b2 = grad_blocks(
        normed, pre_grad_b, x_slots, u_keep_a1
    )
    u_got_a1, u_got_a2, u_got_b1, u_got_b2 = (
        shift(give, "core", CORE, 1) for give in (u_give_a1, u_give_a2, u_give_b1, u_give_b2)
    )
    pre_grad = jnp.concatenate([pre_grad_a, pre_grad_b], 1)
    pre_grad, _ = together(pre_grad, u_keep_b1)
    parts = lax.dot_general(
        pre_grad, up_weight, (((1,), (1,)), ((), ())), preferred_element_type=F32
    ).astype(BF16)
    (
        d_prev, d_next, d_x, u_got_a1, u_got_a2, u_got_b1, u_got_b2, parts,
    ) = together(
        d_prev, d_next, d_x, u_got_a1, u_got_a2, u_got_b1, u_got_b2, parts
    )

    row_cut = -(-d_x.shape[1] // 16) * 8
    d_acc_prev = shift(add(d_keep_a2[0], d_got_a2[0], d_prev[0]), "z", Z, 1)
    d_acc_next = shift(add(d_keep_a2[1], d_got_a2[1], d_next[0]), "z", Z, -1)
    two, one, three = (add(d_keep_b2[i], d_got_b2[i], d_x[i]) for i in range(3))
    d_here = add32(d_keep_b2[3], d_got_b2[3], d_x[3])
    d_b_one, d_b_three = one[:row_cut], three[row_cut:]
    d_b_prev = shift(jnp.concatenate([two[:row_cut], one[row_cut:]], 0), "z", Z, 1)
    d_b_next = shift(jnp.concatenate([three[:row_cut], two[row_cut:]], 0), "z", Z, -1)
    u_prev = shift(add(u_keep_a1[:2], u_got_a1[:2]), "z", Z, 1)
    u_next = shift(add(u_keep_a1[2:], u_got_a1[2:]), "z", Z, -1)
    u_x = shift(add(u_keep_b1, u_got_b1), "xl", XL, 1)
    parts = parts.reshape(members, tok_rows, width)
    p_prev = shift(jnp.concatenate([parts[4][:half], parts[5][:half]], 0), "y", Y, 1)
    p_next = shift(jnp.concatenate([parts[4][half:], parts[5][half:]], 0), "y", Y, -1)
    (
        d_acc_prev, d_acc_next, d_b_prev, d_b_next, u_prev, u_next, u_x, p_prev, p_next,
    ) = together(
        d_acc_prev, d_acc_next, d_b_prev, d_b_next, u_prev, u_next, u_x, p_prev, p_next
    )

    sum_0 = add(d_keep_a2[2], d_got_a2[2], d_next[1], d_acc_prev)
    sum_1 = add(d_keep_a2[3], d_got_a2[3], d_prev[1], d_acc_next)
    d_own = jnp.where(xl == 0, sum_0, sum_1)
    d_other = shift(jnp.where(xl == 0, sum_1, sum_0), "xl", XL, 1)
    d_b_acc_prev = shift(add(d_b_one, d_b_prev[:row_cut]), "z", Z, 1)
    d_b_acc_next = shift(add(d_b_three, d_b_next[row_cut:]), "z", Z, -1)
    u_acc_prev = shift(add(u_keep_a2[0], u_got_a2[0], u_prev[0]), "z", Z, 1)
    u_acc_next = shift(add(u_keep_a2[1], u_got_a2[1], u_next[0]), "z", Z, -1)
    two, one, three = (add(u_keep_b2[i], u_got_b2[i], u_x[i]) for i in range(3))
    u_here = add32(u_keep_b2[3], u_got_b2[3], u_x[3])
    u_b_one, u_b_three = one[:row_cut], three[row_cut:]
    u_b_prev = shift(jnp.concatenate([two[:row_cut], one[row_cut:]], 0), "z", Z, 1)
    u_b_next = shift(jnp.concatenate([three[:row_cut], two[row_cut:]], 0), "z", Z, -1)
    r_prev = shift(
        jnp.concatenate(
            [add(parts[2][:half], p_prev[:half]), parts[2][half:]]
            + [add(parts[3][:half], p_prev[half:]), parts[3][half:]],
            0,
        ),
        "y", Y, 1,
    )
    r_next = shift(
        jnp.concatenate(
            [parts[6][:half], add(parts[6][half:], p_next[:half])]
            + [parts[7][:half], add(parts[7][half:], p_next[half:])],
            0,
        ),
        "y", Y, -1,
    )
    (
        d_other, d_b_acc_prev, d_b_acc_next, u_acc_prev, u_acc_next, u_b_prev, u_b_next,
        r_prev, r_next,
    ) = together(
        d_other, d_b_acc_prev, d_b_acc_next, u_acc_prev, u_acc_next, u_b_prev, u_b_next,
        r_prev, r_next,
    )

    sum_0 = add(u_keep_a2[2], u_got_a2[2], u_next[1], u_acc_prev)
    sum_1 = add(u_keep_a2[3], u_got_a2[3], u_prev[1], u_acc_next)
    u_own = jnp.where(xl == 0, sum_0, sum_1)
    r_other = shift(add(parts[1], r_prev[tok_rows:], r_next[tok_rows:]), "xh", XH, 1)
    u_other = shift(jnp.where(xl == 0, sum_1, sum_0), "xl", XL, 1)
    u_b_acc_prev = shift(add(u_b_one, u_b_prev[:row_cut]), "z", Z, 1)
    u_b_acc_next = shift(add(u_b_three, u_b_next[row_cut:]), "z", Z, -1)
    down_a, up_a = add32(d_own, d_other), add32(u_own, u_other)
    down_b = jnp.concatenate(
        [
            add32(d_here[:row_cut], d_b_next[:row_cut], d_b_acc_prev),
            add32(d_here[row_cut:], d_b_prev[row_cut:], d_b_acc_next),
        ],
        0,
    )
    up_b = jnp.concatenate(
        [
            add32(u_here[:row_cut], u_b_next[:row_cut], u_b_acc_prev),
            add32(u_here[row_cut:], u_b_prev[row_cut:], u_b_acc_next),
        ],
        0,
    )
    normed_grad = add32(parts[0], r_prev[:tok_rows], r_next[:tok_rows], r_other)
    weighted = norm_gain * normed_grad
    input_grad = (
        own_grad
        + inverse_rms * weighted
        - inputs * inverse_rms**3 * jnp.mean(weighted * inputs, -1, keepdims=True)
    ).astype(BF16)
    grad_scale = 1.0 / math.sqrt(group_len * groups)
    return (
        input_grad,
        (jnp.concatenate([up_a, up_b], 1) * grad_scale).astype(BF16),
        (jnp.concatenate([down_a, down_b], 1) * grad_scale).astype(BF16),
    )


def solution(mesh):
    fine = Mesh(mesh.devices.reshape(Z, XL, CORE, Y, XH), AXES)
    dp, tensor = ("z", "xl", "core"), ("y", "xh")
    in_specs = (
        P(AXES, None),
        P(AXES),
        P(),
        P(AXES, None),
        P(),
        P(),
        P(None, tensor),
        P(None, tensor),
    )
    out_specs = (P(AXES, None), P(dp, tensor), P(dp, tensor))
    return jax.shard_map(
        on_device, mesh=fine, in_specs=in_specs, out_specs=out_specs, check_vma=False
    )
```

```python
import math

import jax
import jax.numpy as jnp
from jax import lax
from jax.experimental import pallas as pl
from jax.experimental.pallas import tpu as pltpu
from jax.sharding import Mesh, PartitionSpec as P

F32 = jnp.float32
BF16 = jnp.bfloat16
Z, XL, CORE, Y, XH = 4, 2, 2, 4, 2
AXES = ("z", "xl", "core", "y", "xh")
MEMBERS = Y * XH
BLOCKS = Z * XL * CORE
ID_COLS = 128
ID_BASE = 32
TILE = 256
CUT = 4 * TILE
MIB = 1024 * 1024
VMEM = pl.BlockSpec(memory_space=pltpu.VMEM)
SMEM = pl.BlockSpec(memory_space=pltpu.SMEM)
ANY = pl.BlockSpec(memory_space=pl.ANY)


def params(mib):
    return pltpu.CompilerParams(vmem_limit_bytes=mib * MIB)


def cost(flops, moved, special=0):
    return pl.CostEstimate(flops=flops, bytes_accessed=moved, transcendentals=special)


def shift(value, axis, size, step):
    return lax.ppermute(value, axis, [(i, (i + step) % size) for i in range(size)])


def add32(*terms):
    total = terms[0].astype(F32)
    for term in terms[1:]:
        total = total + term.astype(F32)
    return total


def add(*terms):
    return add32(*terms).astype(BF16)


def together(*values):
    return lax.optimization_barrier(values)


def place_rows(pieces, out, cols):
    at = 0
    for ref, first, rows in pieces:
        out[at : at + rows, :] = ref[first : first + rows, :cols]
        at += rows


def split_parity(turned, core, keep, give):
    rows = turned.shape[0] // BLOCKS
    for pair in range(BLOCKS // 4):
        for out, parity in ((keep, core), (give, 1 - core)):
            two = [
                turned[pl.ds(pl.multiple_of((2 * b + parity) * rows, 8), rows), :]
                for b in (2 * pair, 2 * pair + 1)
            ]
            out[2 * pair * rows : (2 * pair + 2) * rows, :] = jnp.concatenate(two, 0).astype(BF16)


def normed_kernel(core, *refs):
    ins, (out, keep, give, turned) = refs[:7], refs[7:]
    own, other, nxt, prev, mix_prev, mix_next, far = ins
    half = own.shape[0] // 2
    full = 2 * half
    pieces = [(own, 0, full), (other, 0, full), (nxt, 0, full), (mix_next, 0, full)]
    pieces += [(mix_prev, full, half), (mix_next, full, half), (far, 0, full)]
    pieces += [(prev, 0, full), (mix_prev, 0, full)]
    place_rows(pieces, out, out.shape[1])
    for t in range(out.shape[1] // 128):
        cols = slice(t * 128, (t + 1) * 128)
        turned[cols, :] = out[:, cols].astype(F32).T
    split_parity(turned, core[0], keep, give)


def assemble_normed(core, ins):
    rows, width = ins[0].shape[0] * MEMBERS, ins[0].shape[1]
    turned = jax.ShapeDtypeStruct((width // 2, rows), BF16)
    return pl.pallas_call(
        normed_kernel,
        out_shape=[jax.ShapeDtypeStruct((rows, width), BF16), turned, turned],
        in_specs=[SMEM] + [VMEM] * len(ins),
        out_specs=[VMEM] * 3,
        scratch_shapes=[pltpu.VMEM((width, rows), F32)],
        compiler_params=params(40),
        cost_estimate=cost(rows * width, 6 * rows * width),
    )(core, *ins)


def route_kernel(core, positions, layer_scale, *refs):
    ins, (scaled, own_grad, keep, give, joined, turned) = refs[:6], refs[6:]
    own, other, prev, nxt, far_prev, far_next = ins
    full = own.shape[0]
    half = full // 2
    rows, width = scaled.shape
    pieces = [(own, 0, full), (other, 0, full), (nxt, 0, full), (nxt, full, full)]
    pieces += [(far_prev, 0, half), (far_next, 0, half), (far_prev, half, half), (far_next, half, half)]
    pieces += [(prev, 0, full), (prev, full, full)]
    place_rows(pieces, joined, width + ID_COLS)
    tags = joined[:, width : width + ID_COLS].astype(F32).T
    places = tags[0:1, :] * ID_BASE + tags[1:2, :]
    chooser = (positions[...] == places).astype(F32).astype(BF16)
    step = 5 * 128
    for t in range(width // step):
        cols = slice(t * step, (t + 1) * step)
        grads = jnp.dot(chooser, joined[:, cols], preferred_element_type=F32)
        own_grad[:, cols] = grads[:full].astype(BF16)
        part = (grads * layer_scale[:, cols]).astype(BF16)
        scaled[:, cols] = part
        turned[cols, :] = part.astype(F32).T
    split_parity(turned, core[0], keep, give)


def route(core, positions, layer_scale, ins):
    full, width = ins[0].shape[0], layer_scale.shape[1]
    rows = full * MEMBERS
    turned = jax.ShapeDtypeStruct((width // 2, rows), BF16)
    return pl.pallas_call(
        route_kernel,
        out_shape=[
            jax.ShapeDtypeStruct((rows, width), BF16),
            jax.ShapeDtypeStruct((full, width), BF16),
            turned,
            turned,
        ],
        in_specs=[SMEM] + [VMEM] * (2 + len(ins)),
        out_specs=[VMEM] * 4,
        scratch_shapes=[pltpu.VMEM((rows, width + ID_COLS), BF16), pltpu.VMEM((width, rows), F32)],
        compiler_params=params(44),
        cost_estimate=cost(2 * rows * rows * width, 8 * rows * width),
    )(core, positions, layer_scale, *ins)


def gelu_kernel(normed, weight, *refs):
    activation, slope = refs[-2:]
    value = jnp.dot(normed[...], weight[...], preferred_element_type=F32)
    below = 0.5 * (1.0 + lax.erf(value * 0.7071067811865476))
    activation[...] = (value * below).astype(BF16)
    slope[...] = below + value * jnp.exp(-0.5 * value * value) * 0.3989422804014327


def gelu_tiles(normed, weight, first, count, done, after):
    rows, width = normed.shape
    cols = weight.shape[1]
    tile = pl.BlockSpec((rows, TILE), lambda n: (0, n + first))
    return pl.pallas_call(
        gelu_kernel,
        grid=(count,),
        out_shape=[
            jax.ShapeDtypeStruct((rows, cols), BF16),
            jax.ShapeDtypeStruct((rows, cols), F32),
        ],
        in_specs=[
            pl.BlockSpec((rows, width), lambda n: (0, 0)),
            pl.BlockSpec((width, TILE), lambda n: (0, n + first)),
        ]
        + [ANY] * (len(done) + len(after)),
        out_specs=[tile, tile],
        input_output_aliases={2 + i: i for i in range(len(done))},
        compiler_params=params(32),
        cost_estimate=cost(
            2 * rows * width * TILE * count, 2 * width * TILE * count, rows * TILE * count
        ),
    )(normed, weight, *done, *after)


def slope_kernel(scaled, weight, slope, out):
    value = jnp.dot(scaled[...], weight[...], preferred_element_type=F32)
    out[...] = (value * slope[...]).astype(BF16)


def times_slope(scaled, weight, slope):
    rows, width = scaled.shape
    cols = weight.shape[1]
    tile = pl.BlockSpec((rows, TILE), lambda n: (0, n))
    return pl.pallas_call(
        slope_kernel,
        grid=(-(-cols // TILE),),
        out_shape=jax.ShapeDtypeStruct((rows, cols), BF16),
        in_specs=[
            pl.BlockSpec((rows, width), lambda n: (0, 0)),
            pl.BlockSpec((width, TILE), lambda n: (0, n)),
            tile,
        ],
        out_specs=tile,
        compiler_params=params(32),
        cost_estimate=cost(2 * rows * width * cols, 2 * width * cols),
    )(scaled, weight, slope)


def blocks_kernel(sizes, first, slots, left, left_got, right, right_got, *refs):
    outs = refs[-2 - len(sizes) : -2]
    stage, sems = refs[-2:]
    count, rows, cols = stage.shape
    group = 4
    for g in range(count // group):
        part = slice(g * group * rows, (g + 1) * group * rows)
        product = jnp.dot(
            left[part], right[:, first : first + cols], preferred_element_type=F32
        ) + jnp.dot(left_got[part], right_got[:, first : first + cols], preferred_element_type=F32)
        for i in range(group):
            j = g * group + i
            stage[j] = product[i * rows : (i + 1) * rows].astype(BF16)
            slot = slots[j]
            at = 0
            for out, size in zip(outs, sizes):

                @pl.when((slot >= at) & (slot < at + size))
                def _(out=out, at=at, j=j, slot=slot):
                    pltpu.make_async_copy(stage.at[j], out.at[slot - at], sems.at[j]).start()

                at += size
    for j in range(count):
        pltpu.make_async_copy(stage.at[j], outs[0].at[0], sems.at[j]).wait()


def grad_blocks(left, left_got, right, right_got, slots, sizes, first, cols, after):
    width, rows = left.shape
    count = BLOCKS // 2
    block = width // count

    def kernel(*refs):
        blocks_kernel(sizes, first, *refs)

    return pl.pallas_call(
        kernel,
        out_shape=[jax.ShapeDtypeStruct((size, block, cols), BF16) for size in sizes],
        in_specs=[SMEM] + [VMEM] * 4 + [ANY] * len(after),
        out_specs=[ANY] * len(sizes),
        scratch_shapes=[
            pltpu.VMEM((count, block, cols), BF16),
            pltpu.SemaphoreType.DMA((count,)),
        ],
        compiler_params=params(40),
        cost_estimate=cost(4 * rows * width * cols, 2 * width * cols),
    )(slots, left, left_got, right, right_got, *after)


def z_order(z, xl):
    pairs = [(2, 0), (1, 1), (2, 1), (3, 0), (1, 0), (3, 1), (0, 0), (0, 1)]
    return [((z + dz) % Z) * XL + x for dz, x in pairs]


def x_order(z, xl):
    pairs = [(dz, dx) for dx in (1, 0) for dz in (2, 1, 3, 0)]
    return [((z + dz) % Z) * XL + (xl + dx) % XL for dz, dx in pairs]


def slots_of(order):
    order = jnp.stack(order).astype(jnp.int32)
    index = jnp.arange(order.shape[0], dtype=jnp.int32)
    return jnp.sum(jnp.where(order[None, :] == index[:, None], index[None, :], 0), 1)


def beside(*parts):
    return jnp.concatenate(parts, 1)


def below(*parts):
    return jnp.concatenate(parts, 0)


def on_device(
    lm_grad, encoder_row, patch_count, hidden_in, norm_gain, layer_scale, up_weight, down_weight
):
    tok_rows, width = hidden_in.shape
    hidden = up_weight.shape[1]
    group_len = tok_rows * MEMBERS
    per_pair = tok_rows // BLOCKS
    half = tok_rows // 2
    z, xl, core = lax.axis_index("z"), lax.axis_index("xl"), lax.axis_index("core")
    y, xh = lax.axis_index("y"), lax.axis_index("xh")
    group = (z * XL + xl) * CORE + core
    core_at = core.reshape(1).astype(jnp.int32)
    z_slots, x_slots = slots_of(z_order(z, xl)), slots_of(x_order(z, xl))

    inputs = hidden_in.astype(F32)
    inverse_rms = lax.rsqrt(jnp.mean(inputs * inputs, -1, keepdims=True) + 1e-06)
    normed_own = (inputs * inverse_rms * norm_gain).astype(BF16)

    n_prev = shift(normed_own, "y", Y, 1)
    n_next = shift(normed_own, "y", Y, -1)
    n_other = shift(normed_own, "xh", XH, 1)

    image, place = encoder_row // group_len, encoder_row % group_len
    index = jnp.arange(tok_rows, dtype=jnp.int32)
    same = (image[:, None] == image[None, :]) & (index[None, :] < index[:, None])
    slot = image * per_pair + jnp.sum(same.astype(jnp.int32), 1)
    sorter = (slot[None, :] == index[:, None]).astype(BF16)
    column = jnp.arange(ID_COLS, dtype=jnp.int32)[None, :]
    tags = jnp.where(
        column == 0,
        (place // ID_BASE)[:, None],
        jnp.where(column == 1, (place % ID_BASE)[:, None], 0),
    ).astype(BF16)
    ordered = jnp.dot(sorter, beside(lm_grad, tags), preferred_element_type=F32).astype(BF16)
    arrived = lax.all_to_all(
        ordered.reshape(BLOCKS, per_pair, width + ID_COLS),
        ("z", "xl", "core"),
        split_axis=0,
        concat_axis=0,
    ).reshape(tok_rows, width + ID_COLS)

    n_prev, n_next, n_other = together(n_prev, n_next, n_other)
    mix_prev = shift(below(n_other, n_prev[:half]), "y", Y, 1)
    mix_next = shift(below(n_other, n_next[half:]), "y", Y, -1)
    g_other = shift(arrived, "xh", XH, 1)
    mix_prev, mix_next, g_other, arrived = together(mix_prev, mix_next, g_other, arrived)

    far = below(shift(mix_prev[:half], "y", Y, 1), shift(mix_next[half:tok_rows], "y", Y, -1))
    g_both = below(arrived, g_other)
    g_prev = shift(g_both, "y", Y, 1)
    g_next = shift(g_both, "y", Y, -1)
    normed, n_keep, n_give = assemble_normed(
        core_at, (normed_own, n_other, n_next, n_prev, mix_prev, mix_next, far)
    )
    low = CUT // TILE
    done = gelu_tiles(normed, up_weight, 0, low, (), ())
    g_prev, g_next = together(g_prev, g_next)

    g_far_prev = shift(
        below(g_prev[:half], g_prev[tok_rows : tok_rows + half]), "y", Y, 1
    )
    g_far_next = shift(
        below(g_next[half:tok_rows], g_next[tok_rows + half :]), "y", Y, -1
    )
    activation, slope = gelu_tiles(
        normed, up_weight, low, -(-hidden // TILE) - low, done, (g_next,)
    )
    n_got = shift(n_give, "core", CORE, 1)
    act_got = shift(activation, "core", CORE, 1)
    g_far_prev, g_far_next, n_got, act_got = together(g_far_prev, g_far_next, n_got, act_got)

    block = jnp.arange(MEMBERS, dtype=jnp.int32)
    member = ((block // XH + y) % Y) * XH + (block % XH + xh) % XH
    positions = (member[:, None] * tok_rows + index[None, :]).reshape(group_len, 1)
    limit = lax.dynamic_index_in_dim(patch_count, group, 0, keepdims=False)
    positions = jnp.where(positions < limit, positions, -1).astype(F32)
    scaled, own_grad, d_keep, d_give = route(
        core_at,
        positions,
        layer_scale.reshape(1, width),
        (arrived, g_other, g_prev, g_next, g_far_prev, g_far_next),
    )
    d_got = shift(d_give, "core", CORE, 1)
    pre_grad = times_slope(scaled, down_weight, slope)
    pre_got = shift(pre_grad, "core", CORE, 1)

    rest = hidden - CUT
    z_sizes, x_sizes = (2, 2, 4), (4, 4)
    d_up, d_down, d_kept = grad_blocks(
        d_keep, d_got, activation, act_got, z_slots, z_sizes, 0, CUT, (pre_grad,)
    )
    d_prev, d_next = shift(d_up, "z", Z, 1), shift(d_down, "z", Z, -1)
    d_out, d_mine = grad_blocks(
        d_keep, d_got, activation, act_got, x_slots, x_sizes, CUT, rest, (pre_got, d_kept)
    )
    d_x = shift(d_out, "xl", XL, 1)
    u_up, u_down, u_kept = grad_blocks(
        n_keep, n_got, pre_grad, pre_got, z_slots, z_sizes, 0, CUT, (d_mine,)
    )
    u_prev, u_next = shift(u_up, "z", Z, 1), shift(u_down, "z", Z, -1)
    u_out, u_mine = grad_blocks(
        n_keep, n_got, pre_grad, pre_got, x_slots, x_sizes, CUT, rest, (u_kept,)
    )
    pre_grad, _ = together(pre_grad, u_mine)
    parts = lax.dot_general(
        pre_grad, up_weight, (((1,), (1,)), ((), ())), preferred_element_type=F32
    ).astype(BF16)
    d_prev, d_next, d_x, u_prev, u_next, parts, u_out = together(
        d_prev, d_next, d_x, u_prev, u_next, parts, u_out
    )

    cut = -(-d_x.shape[1] // 16) * 8
    two, one, three = (add(d_mine[i], d_x[i]) for i in range(3))
    d_here = add32(d_mine[3], d_x[3])
    d_b_one, d_b_three = one[:cut], three[cut:]
    to_prev = beside(
        add(d_kept[1], d_next[0]), add(u_kept[1], u_next[0]), below(three[:cut], two[cut:])
    )
    to_next = beside(
        add(d_kept[0], d_prev[0]), add(u_kept[0], u_prev[0]), below(two[:cut], one[cut:])
    )
    m_prev, m_next = shift(to_next, "z", Z, 1), shift(to_prev, "z", Z, -1)
    u_x = shift(u_out, "xl", XL, 1)
    parts = parts.reshape(MEMBERS, tok_rows, width)
    p_prev = shift(below(parts[4][:half], parts[5][:half]), "y", Y, 1)
    p_next = shift(below(parts[4][half:], parts[5][half:]), "y", Y, -1)
    m_prev, m_next, u_x, p_prev, p_next = together(m_prev, m_next, u_x, p_prev, p_next)

    d_acc_prev, u_acc_prev, d_b_prev = m_prev[:, :CUT], m_prev[:, CUT : 2 * CUT], m_prev[:, 2 * CUT :]
    d_acc_next, u_acc_next, d_b_next = m_next[:, :CUT], m_next[:, CUT : 2 * CUT], m_next[:, 2 * CUT :]
    sum_0 = beside(add(d_kept[2], d_next[1], d_acc_prev), add(u_kept[2], u_next[1], u_acc_prev))
    sum_1 = beside(add(d_kept[3], d_prev[1], d_acc_next), add(u_kept[3], u_prev[1], u_acc_next))
    a_own = jnp.where(xl == 0, sum_0, sum_1)
    a_other = shift(jnp.where(xl == 0, sum_1, sum_0), "xl", XL, 1)
    two, one, three = (add(u_mine[i], u_x[i]) for i in range(3))
    u_here = add32(u_mine[3], u_x[3])
    u_b_one, u_b_three = one[:cut], three[cut:]
    b_prev = shift(below(add(d_b_one, d_b_prev[:cut]), two[:cut], one[cut:]), "z", Z, 1)
    b_next = shift(below(add(d_b_three, d_b_next[cut:]), three[:cut], two[cut:]), "z", Z, -1)
    r_prev = shift(
        below(
            add(parts[2][:half], p_prev[:half]), parts[2][half:],
            add(parts[3][:half], p_prev[half:]), parts[3][half:],
        ),
        "y", Y, 1,
    )
    r_next = shift(
        below(
            parts[6][:half], add(parts[6][half:], p_next[:half]),
            parts[7][:half], add(parts[7][half:], p_next[half:]),
        ),
        "y", Y, -1,
    )
    a_other, b_prev, b_next, r_prev, r_next = together(a_other, b_prev, b_next, r_prev, r_next)

    r_other = shift(add(parts[1], r_prev[tok_rows:], r_next[tok_rows:]), "xh", XH, 1)
    tail = d_here.shape[0] - cut
    u_b_prev, u_b_next = b_prev[cut:], b_next[tail:]
    c_prev = shift(add(u_b_one, u_b_prev[:cut]), "z", Z, 1)
    c_next = shift(add(u_b_three, u_b_next[cut:]), "z", Z, -1)
    a_total = add32(a_own, a_other)
    down_b = below(
        add32(d_here[:cut], d_b_next[:cut], b_prev[:cut]),
        add32(d_here[cut:], d_b_prev[cut:], b_next[:tail]),
    )
    up_b = below(
        add32(u_here[:cut], u_b_next[:cut], c_prev),
        add32(u_here[cut:], u_b_prev[cut:], c_next),
    )
    normed_grad = add32(parts[0], r_prev[:tok_rows], r_next[:tok_rows], r_other)
    weighted = norm_gain * normed_grad
    input_grad = (
        own_grad.astype(F32)
        + inverse_rms * weighted
        - inputs * inverse_rms**3 * jnp.mean(weighted * inputs, -1, keepdims=True)
    ).astype(BF16)
    grad_scale = 1.0 / math.sqrt(group_len * BLOCKS)
    return (
        input_grad,
        (beside(a_total[:, CUT:], up_b) * grad_scale).astype(BF16),
        (beside(a_total[:, :CUT], down_b) * grad_scale).astype(BF16),
    )


def solution(mesh):
    fine = Mesh(mesh.devices.reshape(Z, XL, CORE, Y, XH), AXES)
    dp, tensor = AXES[:3], AXES[3:]
    in_specs = (
        P(AXES, None),
        P(AXES),
        P(),
        P(AXES, None),
        P(),
        P(),
        P(None, tensor),
        P(None, tensor),
    )
    out_specs = (P(AXES, None), P(dp, tensor), P(dp, tensor))
    return jax.shard_map(
        on_device, mesh=fine, in_specs=in_specs, out_specs=out_specs, check_vma=False
    )
```

```python
import math

import jax
import jax.numpy as jnp
from jax import lax
from jax.experimental import pallas as pl
from jax.experimental.pallas import tpu as pltpu
from jax.sharding import Mesh, PartitionSpec as P

F32 = jnp.float32
BF16 = jnp.bfloat16
Z, XL, CORE, Y, XH = 4, 2, 2, 4, 2
AXES = ("z", "xl", "core", "y", "xh")
MEMBERS = Y * XH
BLOCKS = Z * XL * CORE
ID_COLS = 128
ID_BASE = 32
CUT = 1024
MIB = 1024 * 1024
VMEM = pl.BlockSpec(memory_space=pltpu.VMEM)
SMEM = pl.BlockSpec(memory_space=pltpu.SMEM)
ANY = pl.BlockSpec(memory_space=pl.ANY)


def params(mib):
    return pltpu.CompilerParams(vmem_limit_bytes=mib * MIB)


def cost(flops, moved, special=0):
    return pl.CostEstimate(flops=flops, bytes_accessed=moved, transcendentals=special)


def shift(value, axis, size, step):
    return lax.ppermute(value, axis, [(i, (i + step) % size) for i in range(size)])


def add32(*terms):
    total = terms[0].astype(F32)
    for term in terms[1:]:
        total = total + term.astype(F32)
    return total


def add(*terms):
    return add32(*terms).astype(BF16)


def together(*values):
    return lax.optimization_barrier(values)


def place_rows(pieces, out, cols):
    at = 0
    for ref, first, rows in pieces:
        out[at : at + rows, :] = ref[first : first + rows, :cols]
        at += rows


def split_parity(turned, core, keep, give):
    rows = turned.shape[0] // BLOCKS
    for pair in range(BLOCKS // 4):
        for out, parity in ((keep, core), (give, 1 - core)):
            two = [
                turned[pl.ds(pl.multiple_of((2 * b + parity) * rows, 8), rows), :]
                for b in (2 * pair, 2 * pair + 1)
            ]
            out[2 * pair * rows : (2 * pair + 2) * rows, :] = jnp.concatenate(two, 0).astype(BF16)


def normed_kernel(core, *refs):
    ins, (out, keep, give, turned) = refs[:7], refs[7:]
    own, other, nxt, prev, mix_prev, mix_next, far = ins
    half = own.shape[0] // 2
    full = 2 * half
    pieces = [(own, 0, full), (other, 0, full), (nxt, 0, full), (mix_next, 0, full)]
    pieces += [(mix_prev, full, half), (mix_next, full, half), (far, 0, full)]
    pieces += [(prev, 0, full), (mix_prev, 0, full)]
    place_rows(pieces, out, out.shape[1])
    for t in range(out.shape[1] // 128):
        cols = slice(t * 128, (t + 1) * 128)
        turned[cols, :] = out[:, cols].astype(F32).T
    split_parity(turned, core[0], keep, give)


def assemble_normed(core, ins):
    rows, width = ins[0].shape[0] * MEMBERS, ins[0].shape[1]
    turned = jax.ShapeDtypeStruct((width // 2, rows), BF16)
    return pl.pallas_call(
        normed_kernel,
        out_shape=[jax.ShapeDtypeStruct((rows, width), BF16), turned, turned],
        in_specs=[SMEM] + [VMEM] * len(ins),
        out_specs=[VMEM] * 3,
        scratch_shapes=[pltpu.VMEM((width, rows), F32)],
        compiler_params=params(12),
        cost_estimate=cost(10**8, 10**6),
    )(core, *ins)


def route_kernel(core, positions, layer_scale, *refs):
    ins, (scaled, own_grad, keep, give, joined, turned) = refs[:6], refs[6:]
    own, other, prev, nxt, far_prev, far_next = ins
    full = own.shape[0]
    half = full // 2
    rows, width = scaled.shape
    pieces = [(own, 0, full), (other, 0, full), (nxt, 0, full), (nxt, full, full)]
    pieces += [(far_prev, 0, half), (far_next, 0, half), (far_prev, half, half), (far_next, half, half)]
    pieces += [(prev, 0, full), (prev, full, full)]
    place_rows(pieces, joined, width + ID_COLS)
    tags = joined[:, width : width + ID_COLS].astype(F32).T
    places = tags[0:1, :] * ID_BASE + tags[1:2, :]
    chooser = (positions[...] == places).astype(F32).astype(BF16)
    step = 5 * 128
    for t in range(width // step):
        cols = slice(t * step, (t + 1) * step)
        grads = jnp.dot(chooser, joined[:, cols], preferred_element_type=F32)
        own_grad[:, cols] = grads[:full].astype(BF16)
        part = (grads * layer_scale[:, cols]).astype(BF16)
        scaled[:, cols] = part
        turned[cols, :] = part.astype(F32).T
    split_parity(turned, core[0], keep, give)


def route(core, positions, layer_scale, ins):
    full, width = ins[0].shape[0], layer_scale.shape[1]
    rows = full * MEMBERS
    turned = jax.ShapeDtypeStruct((width // 2, rows), BF16)
    return pl.pallas_call(
        route_kernel,
        out_shape=[
            jax.ShapeDtypeStruct((rows, width), BF16),
            jax.ShapeDtypeStruct((full, width), BF16),
            turned,
            turned,
        ],
        in_specs=[SMEM] + [VMEM] * (2 + len(ins)),
        out_specs=[VMEM] * 4,
        scratch_shapes=[pltpu.VMEM((rows, width + ID_COLS), BF16), pltpu.VMEM((width, rows), F32)],
        compiler_params=params(16),
        cost_estimate=cost(10**8, 10**6),
    )(core, positions, layer_scale, *ins)


def by_last(left, right):
    return lax.dot_general(
        left, right, (((1,), (1,)), ((), ())), preferred_element_type=F32
    )


def gelu_kernel(first, tile, normed, weight, *refs):
    activation, slope = refs[-2:]

    @pl.loop(0, activation.shape[0] // tile)
    def _(n):
        at = pl.multiple_of(n * tile, 16)
        value = by_last(weight[pl.ds(first + at, tile), :], normed[...])
        below = 0.5 * (1.0 + lax.erf(value * 0.7071067811865476))
        activation[pl.ds(at, tile), :] = (value * below).astype(BF16)
        slope[pl.ds(at, tile), :] = (
            below + value * jnp.exp(-0.5 * value * value) * 0.3989422804014327
        )


def gelu_part(normed, weight, first, count, tile, after):
    rows, width = normed.shape

    def kernel(*refs):
        gelu_kernel(first, tile, *refs)

    return pl.pallas_call(
        kernel,
        out_shape=[
            jax.ShapeDtypeStruct((count, rows), BF16),
            jax.ShapeDtypeStruct((count, rows), F32),
        ],
        in_specs=[VMEM, VMEM] + [ANY] * len(after),
        out_specs=[VMEM, VMEM],
        compiler_params=params(12),
        cost_estimate=cost(10**8, 10**6),
    )(normed, weight, *after)


def slope_kernel(first, tile, scaled, weight, slope, *refs):
    out = refs[-1]

    @pl.loop(0, out.shape[0] // tile)
    def _(n):
        at = pl.multiple_of(n * tile, 16)
        value = by_last(weight[pl.ds(first + at, tile), :], scaled[...])
        out[pl.ds(at, tile), :] = (value * slope[pl.ds(at, tile), :]).astype(BF16)


def times_slope(scaled, weight, slope, first, tile, after):
    rows, width = scaled.shape
    count = slope.shape[0]

    def kernel(*refs):
        slope_kernel(first, tile, *refs)

    return pl.pallas_call(
        kernel,
        out_shape=jax.ShapeDtypeStruct((count, rows), BF16),
        in_specs=[VMEM, VMEM, VMEM] + [ANY] * len(after),
        out_specs=VMEM,
        compiler_params=params(12),
        cost_estimate=cost(10**8, 10**6),
    )(scaled, weight, slope, *after)


def blocks_kernel(sizes, slots, left, left_got, right, right_got, *refs):
    outs = refs[-2 - len(sizes) : -2]
    stage, sems = refs[-2:]
    count, rows, cols = stage.shape
    group = 4
    for g in range(count // group):
        part = slice(g * group * rows, (g + 1) * group * rows)
        product = by_last(
            jnp.concatenate([left[part], left_got[part]], 1),
            jnp.concatenate([right[...], right_got[...]], 1),
        )
        for i in range(group):
            j = g * group + i
            stage[j] = product[i * rows : (i + 1) * rows].astype(BF16)
            slot = slots[j]
            at = 0
            for out, size in zip(outs, sizes):

                @pl.when((slot >= at) & (slot < at + size))
                def _(out=out, at=at, j=j, slot=slot):
                    pltpu.make_async_copy(stage.at[j], out.at[slot - at], sems.at[j]).start()

                at += size
    for j in range(count):
        pltpu.make_async_copy(stage.at[j], outs[0].at[0], sems.at[j]).wait()


def grad_blocks(left, left_got, right, right_got, slots, sizes, after):
    width, rows = left.shape
    cols = right.shape[0]
    count = BLOCKS // 2
    block = width // count

    def kernel(*refs):
        blocks_kernel(sizes, *refs)

    return pl.pallas_call(
        kernel,
        out_shape=[jax.ShapeDtypeStruct((size, block, cols), BF16) for size in sizes],
        in_specs=[SMEM] + [VMEM] * 4 + [ANY] * len(after),
        out_specs=[ANY] * len(sizes),
        scratch_shapes=[
            pltpu.VMEM((count, block, cols), BF16),
            pltpu.SemaphoreType.DMA((count,)),
        ],
        compiler_params=params(16),
        cost_estimate=cost(10**8, 10**6),
    )(slots, left, left_got, right, right_got, *after)


def z_order(z, xl):
    pairs = [(2, 0), (1, 1), (2, 1), (3, 0), (1, 0), (3, 1), (0, 0), (0, 1)]
    return [((z + dz) % Z) * XL + x for dz, x in pairs]


def x_order(z, xl):
    pairs = [(dz, dx) for dx in (1, 0) for dz in (2, 1, 3, 0)]
    return [((z + dz) % Z) * XL + (xl + dx) % XL for dz, dx in pairs]


def slots_of(order):
    order = jnp.stack(order).astype(jnp.int32)
    index = jnp.arange(order.shape[0], dtype=jnp.int32)
    return jnp.sum(jnp.where(order[None, :] == index[:, None], index[None, :], 0), 1)


def beside(*parts):
    return jnp.concatenate(parts, 1)


def below(*parts):
    return jnp.concatenate(parts, 0)


def on_device(
    lm_grad, encoder_row, patch_count, hidden_in, norm_gain, layer_scale, up_weight, down_weight
):
    tok_rows, width = hidden_in.shape
    rest = up_weight.shape[1] - CUT
    up_turned, down_turned = up_weight.T, down_weight.T
    group_len = tok_rows * MEMBERS
    per_pair = tok_rows // BLOCKS
    half = tok_rows // 2
    z, xl, core = lax.axis_index("z"), lax.axis_index("xl"), lax.axis_index("core")
    y, xh = lax.axis_index("y"), lax.axis_index("xh")
    group = (z * XL + xl) * CORE + core
    core_at = core.reshape(1).astype(jnp.int32)
    z_slots, x_slots = slots_of(z_order(z, xl)), slots_of(x_order(z, xl))

    inputs = hidden_in.astype(F32)
    inverse_rms = lax.rsqrt(jnp.mean(inputs * inputs, -1, keepdims=True) + 1e-06)
    normed_own = (inputs * inverse_rms * norm_gain).astype(BF16)

    n_prev = shift(normed_own, "y", Y, 1)
    n_next = shift(normed_own, "y", Y, -1)
    n_other = shift(normed_own, "xh", XH, 1)

    image, place = encoder_row // group_len, encoder_row % group_len
    index = jnp.arange(tok_rows, dtype=jnp.int32)
    same = (image[:, None] == image[None, :]) & (index[None, :] < index[:, None])
    slot = image * per_pair + jnp.sum(same.astype(jnp.int32), 1)
    sorter = (slot[None, :] == index[:, None]).astype(BF16)
    column = jnp.arange(ID_COLS, dtype=jnp.int32)[None, :]
    tags = jnp.where(
        column == 0,
        (place // ID_BASE)[:, None],
        jnp.where(column == 1, (place % ID_BASE)[:, None], 0),
    ).astype(BF16)
    ordered = jnp.dot(sorter, beside(lm_grad, tags), preferred_element_type=F32).astype(BF16)
    arrived = lax.all_to_all(
        ordered.reshape(BLOCKS, per_pair, width + ID_COLS),
        ("z", "xl", "core"),
        split_axis=0,
        concat_axis=0,
    ).reshape(tok_rows, width + ID_COLS)

    n_prev, n_next, n_other = together(n_prev, n_next, n_other)
    mix_prev = shift(below(n_other, n_prev[:half]), "y", Y, 1)
    mix_next = shift(below(n_other, n_next[half:]), "y", Y, -1)
    g_other = shift(arrived, "xh", XH, 1)
    mix_prev, mix_next, g_other, arrived = together(mix_prev, mix_next, g_other, arrived)

    far = below(shift(mix_prev[:half], "y", Y, 1), shift(mix_next[half:tok_rows], "y", Y, -1))
    g_both = below(arrived, g_other)
    g_prev = shift(g_both, "y", Y, 1)
    g_next = shift(g_both, "y", Y, -1)
    normed, n_keep, n_give = assemble_normed(
        core_at, (normed_own, n_other, n_next, n_prev, mix_prev, mix_next, far)
    )
    act_a, slope_a = gelu_part(normed, up_turned, 0, CUT, 256, ())
    n_got = shift(n_give, "core", CORE, 1)
    g_prev, g_next = together(g_prev, g_next)

    g_far_prev = shift(
        below(g_prev[:half], g_prev[tok_rows : tok_rows + half]), "y", Y, 1
    )
    g_far_next = shift(
        below(g_next[half:tok_rows], g_next[tok_rows + half :]), "y", Y, -1
    )
    act_b, slope_b = gelu_part(normed, up_turned, CUT, rest, rest // 2, (g_next,))
    act_a_got = shift(act_a, "core", CORE, 1)
    act_b_got = shift(act_b, "core", CORE, 1)
    g_far_prev, g_far_next, n_got, act_a_got, act_b_got = together(
        g_far_prev, g_far_next, n_got, act_a_got, act_b_got
    )

    block = jnp.arange(MEMBERS, dtype=jnp.int32)
    member = ((block // XH + y) % Y) * XH + (block % XH + xh) % XH
    positions = (member[:, None] * tok_rows + index[None, :]).reshape(group_len, 1)
    limit = lax.dynamic_index_in_dim(patch_count, group, 0, keepdims=False)
    positions = jnp.where(positions < limit, positions, -1).astype(F32)
    scaled, own_grad, d_keep, d_give = route(
        core_at,
        positions,
        layer_scale.reshape(1, width),
        (arrived, g_other, g_prev, g_next, g_far_prev, g_far_next),
    )
    d_got = shift(d_give, "core", CORE, 1)
    pre_a = times_slope(scaled, down_turned, slope_a, 0, 256, ())
    pre_a_got = shift(pre_a, "core", CORE, 1)

    z_sizes, x_sizes = (2, 2, 4), (4, 4)
    d_up, d_down, d_kept = grad_blocks(
        d_keep, d_got, act_a, act_a_got, z_slots, z_sizes, (pre_a,)
    )
    d_prev, d_next = shift(d_up, "z", Z, 1), shift(d_down, "z", Z, -1)
    u_up, u_down, u_kept = grad_blocks(
        n_keep, n_got, pre_a, pre_a_got, z_slots, z_sizes, (d_kept,)
    )
    u_prev, u_next = shift(u_up, "z", Z, 1), shift(u_down, "z", Z, -1)
    pre_b = times_slope(scaled, down_turned, slope_b, CUT, rest // 2, (u_kept,))
    pre_b_got = shift(pre_b, "core", CORE, 1)
    d_out, d_mine = grad_blocks(d_keep, d_got, act_b, act_b_got, x_slots, x_sizes, (pre_b,))
    d_x = shift(d_out, "xl", XL, 1)
    u_out, u_mine = grad_blocks(n_keep, n_got, pre_b, pre_b_got, x_slots, x_sizes, (d_mine,))
    pre_a, pre_b, d_prev, d_next, _ = together(pre_a, pre_b, d_prev, d_next, u_mine)
    parts = lax.dot_general(
        below(pre_a, pre_b), up_turned, (((0,), (0,)), ((), ())), preferred_element_type=F32
    ).astype(BF16)
    d_prev, d_next, d_x, u_prev, u_next, parts, u_out = together(
        d_prev, d_next, d_x, u_prev, u_next, parts, u_out
    )

    cut = -(-d_x.shape[1] // 16) * 8
    two, one, three = (add(d_mine[i], d_x[i]) for i in range(3))
    d_here = add32(d_mine[3], d_x[3])
    d_b_one, d_b_three = one[:cut], three[cut:]
    to_prev = beside(
        add(d_kept[1], d_next[0]), add(u_kept[1], u_next[0]), below(three[:cut], two[cut:])
    )
    to_next = beside(
        add(d_kept[0], d_prev[0]), add(u_kept[0], u_prev[0]), below(two[:cut], one[cut:])
    )
    m_prev, m_next = shift(to_next, "z", Z, 1), shift(to_prev, "z", Z, -1)
    u_x = shift(u_out, "xl", XL, 1)
    parts = parts.reshape(MEMBERS, tok_rows, width)
    p_prev = shift(below(parts[4][:half], parts[5][:half]), "y", Y, 1)
    p_next = shift(below(parts[4][half:], parts[5][half:]), "y", Y, -1)
    m_prev, m_next, u_x, p_prev, p_next = together(m_prev, m_next, u_x, p_prev, p_next)

    d_acc_prev, u_acc_prev, d_b_prev = m_prev[:, :CUT], m_prev[:, CUT : 2 * CUT], m_prev[:, 2 * CUT :]
    d_acc_next, u_acc_next, d_b_next = m_next[:, :CUT], m_next[:, CUT : 2 * CUT], m_next[:, 2 * CUT :]
    sum_0 = beside(add(d_kept[2], d_next[1], d_acc_prev), add(u_kept[2], u_next[1], u_acc_prev))
    sum_1 = beside(add(d_kept[3], d_prev[1], d_acc_next), add(u_kept[3], u_prev[1], u_acc_next))
    a_own = jnp.where(xl == 0, sum_0, sum_1)
    a_other = shift(jnp.where(xl == 0, sum_1, sum_0), "xl", XL, 1)
    two, one, three = (add(u_mine[i], u_x[i]) for i in range(3))
    u_here = add32(u_mine[3], u_x[3])
    u_b_one, u_b_three = one[:cut], three[cut:]
    b_prev = shift(below(add(d_b_one, d_b_prev[:cut]), two[:cut], one[cut:]), "z", Z, 1)
    b_next = shift(below(add(d_b_three, d_b_next[cut:]), three[:cut], two[cut:]), "z", Z, -1)
    r_prev = shift(
        below(
            add(parts[2][:half], p_prev[:half]), parts[2][half:],
            add(parts[3][:half], p_prev[half:]), parts[3][half:],
        ),
        "y", Y, 1,
    )
    r_next = shift(
        below(
            parts[6][:half], add(parts[6][half:], p_next[:half]),
            parts[7][:half], add(parts[7][half:], p_next[half:]),
        ),
        "y", Y, -1,
    )
    a_other, b_prev, b_next, r_prev, r_next = together(a_other, b_prev, b_next, r_prev, r_next)

    r_other = shift(add(parts[1], r_prev[tok_rows:], r_next[tok_rows:]), "xh", XH, 1)
    tail = d_here.shape[0] - cut
    u_b_prev, u_b_next = b_prev[cut:], b_next[tail:]
    c_prev = shift(add(u_b_one, u_b_prev[:cut]), "z", Z, 1)
    c_next = shift(add(u_b_three, u_b_next[cut:]), "z", Z, -1)
    a_total = add32(a_own, a_other)
    down_b = below(
        add32(d_here[:cut], d_b_next[:cut], b_prev[:cut]),
        add32(d_here[cut:], d_b_prev[cut:], b_next[:tail]),
    )
    up_b = below(
        add32(u_here[:cut], u_b_next[:cut], c_prev),
        add32(u_here[cut:], u_b_prev[cut:], c_next),
    )
    normed_grad = add32(parts[0], r_prev[:tok_rows], r_next[:tok_rows], r_other)
    weighted = norm_gain * normed_grad
    input_grad = (
        own_grad.astype(F32)
        + inverse_rms * weighted
        - inputs * inverse_rms**3 * jnp.mean(weighted * inputs, -1, keepdims=True)
    ).astype(BF16)
    grad_scale = 1.0 / math.sqrt(group_len * BLOCKS)
    return (
        input_grad,
        (beside(a_total[:, CUT:], up_b) * grad_scale).astype(BF16),
        (beside(a_total[:, :CUT], down_b) * grad_scale).astype(BF16),
    )


def solution(mesh):
    fine = Mesh(mesh.devices.reshape(Z, XL, CORE, Y, XH), AXES)
    dp, tensor = AXES[:3], AXES[3:]
    in_specs = (
        P(AXES, None),
        P(AXES),
        P(),
        P(AXES, None),
        P(),
        P(),
        P(None, tensor),
        P(None, tensor),
    )
    out_specs = (P(AXES, None), P(dp, tensor), P(dp, tensor))
    return jax.shard_map(
        on_device, mesh=fine, in_specs=in_specs, out_specs=out_specs, check_vma=False
    )
```

```python
import math

import jax
import jax.numpy as jnp
from jax import lax
from jax.experimental import pallas as pl
from jax.experimental.pallas import tpu as pltpu
from jax.sharding import Mesh, PartitionSpec as P

F32 = jnp.float32
BF16 = jnp.bfloat16
Z, XL, CORE, Y, XH = 4, 2, 2, 4, 2
AXES = ("z", "xl", "core", "y", "xh")
MEMBERS = Y * XH
BLOCKS = Z * XL * CORE
ID_COLS = 128
ID_BASE = 32
CUT = 1024
MIB = 1024 * 1024
VMEM = pl.BlockSpec(memory_space=pltpu.VMEM)
SMEM = pl.BlockSpec(memory_space=pltpu.SMEM)
ANY = pl.BlockSpec(memory_space=pl.ANY)


def params(mib):
    return pltpu.CompilerParams(vmem_limit_bytes=mib * MIB)


def cost(flops, moved, special=0):
    return pl.CostEstimate(flops=flops, bytes_accessed=moved, transcendentals=special)


def shift(value, axis, size, step):
    return lax.ppermute(value, axis, [(i, (i + step) % size) for i in range(size)])


def add32(*terms):
    total = terms[0].astype(F32)
    for term in terms[1:]:
        total = total + term.astype(F32)
    return total


def add(*terms):
    return add32(*terms).astype(BF16)


def together(*values):
    return lax.optimization_barrier(values)


def fetch(pieces, sem):
    copies = [pltpu.make_async_copy(src, dst, sem.at[i]) for i, (src, dst) in enumerate(pieces)]
    for copy in copies:
        copy.start()

    def wait():
        for copy in copies:
            copy.wait()

    return wait


def pieces_of(listed, out):
    at, pieces = 0, []
    for ref, first, rows in listed:
        pieces.append((ref.at[first : first + rows], out.at[at : at + rows]))
        at += rows
    return pieces


def split_parity(turned, core, pairs, keep, give):
    rows = keep.shape[0] // pairs
    for two in range(pairs // 2):
        for out, parity in ((keep, core), (give, 1 - core)):
            blocks = [
                turned[pl.ds(pl.multiple_of((2 * b + parity) * rows, 8), rows), :]
                for b in (2 * two, 2 * two + 1)
            ]
            out[2 * two * rows : (2 * two + 2) * rows, :] = jnp.concatenate(blocks, 0).astype(BF16)


def by_last(left, right):
    return lax.dot_general(left, right, (((1,), (1,)), ((), ())), preferred_element_type=F32)


def stream(weight, first, tile, count, held, sem, body):
    def copy(n):
        slot = lax.rem(n, 2)
        rows = pl.ds(pl.multiple_of(first + n * tile, 16), tile)
        return pltpu.make_async_copy(weight.at[rows], held.at[slot], sem.at[slot])

    copy(0).start()

    @pl.loop(0, count)
    def _(n):
        @pl.when(n + 1 < count)
        def _():
            copy(n + 1).start()

        copy(n).wait()
        body(n, held[lax.rem(n, 2)])


def normed_kernel(tile, core, *refs):
    ins, weight, (act, slope, keep, give) = refs[:7], refs[7], refs[8:12]
    normed, turned, held, act_s, slope_s, keep_s, give_s, in_sem, w_sem, out_sem = refs[12:]
    own, other, nxt, prev, mix_prev, mix_next, far = ins
    full = own.shape[0]
    half = full // 2
    listed = [(own, 0, full), (other, 0, full), (nxt, 0, full), (mix_next, 0, full)]
    listed += [(mix_prev, full, half), (mix_next, full, half), (far, 0, full)]
    listed += [(prev, 0, full), (mix_prev, 0, full)]
    fetch(pieces_of(listed, normed), in_sem)()
    for t in range(normed.shape[1] // 128):
        cols = slice(t * 128, (t + 1) * 128)
        turned[cols, :] = normed[:, cols].astype(F32).T
    split_parity(turned, core[0], BLOCKS // 2, keep_s, give_s)
    done = fetch([(keep_s, keep), (give_s, give)], out_sem)

    def body(n, rows):
        at = pl.ds(pl.multiple_of(n * tile, 16), tile)
        value = by_last(rows, normed[...])
        below = 0.5 * (1.0 + lax.erf(value * 0.7071067811865476))
        act_s[at, :] = (value * below).astype(BF16)
        slope_s[at, :] = below + value * jnp.exp(-0.5 * value * value) * 0.3989422804014327

    stream(weight, 0, tile, act.shape[0] // tile, held, w_sem, body)
    done()
    fetch([(act_s, act), (slope_s, slope)], out_sem)()


def assemble_normed(core, ins, weight):
    rows, width = ins[0].shape[0] * MEMBERS, ins[0].shape[1]
    hidden = weight.shape[0]
    tile = 320

    def kernel(*refs):
        normed_kernel(tile, *refs)

    outs = [((hidden, rows), BF16), ((hidden, rows), F32)] + [((width // 2, rows), BF16)] * 2
    return pl.pallas_call(
        kernel,
        out_shape=[jax.ShapeDtypeStruct(shape, kind) for shape, kind in outs],
        in_specs=[SMEM] + [ANY] * (len(ins) + 1),
        out_specs=[ANY] * 4,
        scratch_shapes=[
            pltpu.VMEM((rows, width), BF16),
            pltpu.VMEM((width, rows), F32),
            pltpu.VMEM((2, tile, width), BF16),
        ]
        + [pltpu.VMEM(shape, kind) for shape, kind in outs]
        + [pltpu.SemaphoreType.DMA((n,)) for n in (9, 2, 2)],
        compiler_params=params(32),
        cost_estimate=cost(10**8, 10**6),
    )(core, *ins, weight)


def prepare_kernel(order, own, other, first, second, rows_s, turned, sorted_s, *refs):
    outs_s, in_sem, sem = refs[:2], refs[2], refs[3]
    half = own.shape[0] // 2
    listed = [(own, 0, half), (other, 0, half), (own, half, half), (other, half, half)]
    fetch(pieces_of(listed, rows_s), in_sem)()
    width = turned.shape[0]
    pair = width // (BLOCKS // 2)
    for t in range(width // 128):
        cols = slice(t * 128, (t + 1) * 128)
        turned[cols, :] = rows_s[:, cols].astype(F32).T
    waits = []
    for h, out in enumerate((first, second)):
        for p in range(4):
            at = pl.ds(pl.multiple_of(order[4 * h + p] * pair, 8), pair)
            sorted_s[p * pair : (p + 1) * pair, :] = turned[at, :]
        cols = width // 2
        lead = 0 if h else ID_COLS
        for first_col in range(0, cols, 128):
            last = min(first_col + 128, cols)
            outs_s[h][:, lead + first_col : lead + last] = (
                sorted_s[first_col : first_col + 128, :].T[:, : last - first_col].astype(BF16)
            )
        if h == 0:
            outs_s[h][:, :lead] = rows_s[:, width : width + ID_COLS]
        waits.append(fetch([(outs_s[h], out)], sem.at[h]))
    for wait in waits:
        wait()


def prepare(order, own, other, width):
    rows = 2 * own.shape[0]
    cols = width // 2
    return pl.pallas_call(
        prepare_kernel,
        out_shape=[
            jax.ShapeDtypeStruct((rows, cols + ID_COLS), BF16),
            jax.ShapeDtypeStruct((rows, cols), BF16),
        ],
        in_specs=[SMEM, ANY, ANY],
        out_specs=[ANY, ANY],
        scratch_shapes=[
            pltpu.VMEM((rows, width + ID_COLS), BF16),
            pltpu.VMEM((width, rows), F32),
            pltpu.VMEM((-(-cols // 128) * 128, rows), F32),
            pltpu.VMEM((rows, cols + ID_COLS), BF16),
            pltpu.VMEM((rows, cols), BF16),
            pltpu.SemaphoreType.DMA((4,)),
            pltpu.SemaphoreType.DMA((2, 1)),
        ],
        compiler_params=params(12),
        cost_estimate=cost(10**8, 10**6),
    )(order, own, other)


def route_kernel(second, core, order, layer_scale, extra, *refs):
    ins, refs = refs[:5], refs[5:]
    if second:
        own_first, scaled, keep, give, own_grad = refs[:5]
    else:
        scaled, keep, give, own_turned, chooser_out = refs[:5]
    joined, turned, scaled_s, keep_s, give_s, chooser, own_s, own_rows, in_sem, sem = refs[5:]
    cols = scaled.shape[0]
    pair = cols // 4
    lead = 0 if second else ID_COLS
    at, pieces = 0, []
    for ref in ins:
        rows = ref.shape[0]
        pieces.append((ref, joined.at[at : at + rows]))
        at += rows
    if second:
        pieces += [(extra, chooser), (own_first, own_s.at[0])]
    fetch(pieces, in_sem)()
    if not second:
        tags = joined[:, :lead].astype(F32).T
        places = tags[0:1, :] * ID_BASE + tags[1:2, :]
        chooser[...] = (extra[...] == places).astype(F32).astype(BF16)
    step = 640
    for first in range(0, cols, step):
        last = min(first + step, cols)
        grads = jnp.dot(
            chooser[...], joined[:, lead + first : lead + last], preferred_element_type=F32
        )
        turned[first:last, :] = grads.T
    own_s[1 if second else 0] = turned[:cols, :128]
    for p in range(4):
        here = slice(p * pair, (p + 1) * pair)
        place = order[p + (4 if second else 0)]
        scale = layer_scale[pl.ds(pl.multiple_of(place * pair, 8), pair), :]
        value = turned[here, :] * scale
        turned[here, :] = value
        scaled_s[here, :] = value.astype(BF16)
    split_parity(turned, core[0], 4, keep_s, give_s)
    outs = [(scaled_s, scaled), (keep_s, keep), (give_s, give)]
    if not second:
        outs += [(own_s.at[0], own_turned), (chooser, chooser_out)]
    done = fetch(outs, sem)
    if second:
        for p in range(8):
            at = pl.ds(pl.multiple_of(order[p] * pair, 8), pair)
            own_rows[at, :] = own_s[p // 4, (p % 4) * pair : (p % 4 + 1) * pair, :]
        half = own_grad.shape[0]
        for t in range(own_rows.shape[0] // 128):
            here = slice(t * 128, (t + 1) * 128)
            own_grad[:, here] = own_rows[here, :].T[:half].astype(BF16)
    done()


def route(second, core, order, layer_scale, extra, ins, own_first=()):
    rows, width = 4 * ins[0].shape[0], layer_scale.shape[0]
    cols = width // 2

    def kernel(*refs):
        route_kernel(second, *refs)

    own = [((ins[0].shape[0] // 2, width), BF16)] if second else [((cols, 128), F32)]
    outs = [((cols, rows), BF16), ((cols // 2, rows), BF16), ((cols // 2, rows), BF16)] + own
    if not second:
        outs += [((rows, rows), BF16)]
    return pl.pallas_call(
        kernel,
        out_shape=[jax.ShapeDtypeStruct(shape, kind) for shape, kind in outs],
        in_specs=[SMEM, SMEM, VMEM, ANY if second else VMEM] + [ANY] * (len(ins) + len(own_first)),
        out_specs=[ANY] * 3 + ([VMEM] if second else [ANY] * 2),
        scratch_shapes=[
            pltpu.VMEM((rows, ins[0].shape[1]), BF16),
            pltpu.VMEM((cols, rows), F32),
            pltpu.VMEM((cols, rows), BF16),
            pltpu.VMEM((cols // 2, rows), BF16),
            pltpu.VMEM((cols // 2, rows), BF16),
            pltpu.VMEM((rows, rows), BF16),
            pltpu.VMEM((2, cols, 128), F32),
            pltpu.VMEM((width, 128), F32),
            pltpu.SemaphoreType.DMA((7,)),
            pltpu.SemaphoreType.DMA((5,)),
        ],
        compiler_params=params(24),
        cost_estimate=cost(10**8, 10**6),
    )(core, order, layer_scale, extra, *ins, *own_first)


def slope_kernel(first, tile, order, scaled_1, scaled_2, weight, slope, *refs):
    out, scaled, slope_s, held, out_s, in_sem, w_sem, sem = refs[-8:]
    count = out.shape[0]
    pair = scaled_1.shape[0] // 4
    pieces = [(slope.at[first : first + count], slope_s)]
    for p in range(8):
        source = (scaled_1, scaled_2)[p // 4].at[(p % 4) * pair : (p % 4 + 1) * pair]
        at = pl.ds(pl.multiple_of(order[p] * pair, 16), pair)
        pieces.append((source, scaled.at[at]))
    fetch(pieces, in_sem)()

    def body(n, rows):
        at = pl.ds(pl.multiple_of(n * tile, 16), tile)
        value = jnp.dot(rows, scaled[...], preferred_element_type=F32)
        out_s[at, :] = (value * slope_s[at, :]).astype(BF16)

    stream(weight, first, tile, count // tile, held, w_sem, body)
    fetch([(out_s, out)], sem)()


def times_slope(order, scaled, weight, slope, first, count, tile, after):
    width, rows = weight.shape[1], slope.shape[1]

    def kernel(*refs):
        slope_kernel(first, tile, *refs)

    return pl.pallas_call(
        kernel,
        out_shape=jax.ShapeDtypeStruct((count, rows), BF16),
        in_specs=[SMEM] + [ANY] * (4 + len(after)),
        out_specs=ANY,
        scratch_shapes=[
            pltpu.VMEM((width, rows), BF16),
            pltpu.VMEM((count, rows), F32),
            pltpu.VMEM((2, tile, width), BF16),
            pltpu.VMEM((count, rows), BF16),
        ]
        + [pltpu.SemaphoreType.DMA((n,)) for n in (9, 2, 1)],
        compiler_params=params(24),
        cost_estimate=cost(10**8, 10**6),
    )(order, *scaled, weight, slope, *after)


def blocks_kernel(parts, slots, left, left_got, right, right_got, *refs):
    total = sum(len(sizes) for _, _, sizes in parts)
    n = len(parts)
    tail = 2 * n + 4
    outs, refs = refs[-tail - total : -tail], refs[-tail:]
    left_s, rights, stages = refs[0], refs[1 : 1 + n], refs[1 + n : 1 + 2 * n]
    l_sem, r_sem, sem = refs[1 + 2 * n :]
    rows_in = left.shape[1]
    group = 800
    count = left.shape[0] // group
    waits_r = []
    for k, (first, cols, _) in enumerate(parts):
        here = slice(first, first + cols)
        waits_r.append(
            fetch(
                [
                    (right.at[here], rights[k].at[:cols, :rows_in]),
                    (right_got.at[here], rights[k].at[:cols, rows_in:]),
                ],
                r_sem.at[k],
            )
        )
    waits_l = []
    for g in range(count):
        here = slice(g * group, (g + 1) * group)
        waits_l.append(
            fetch(
                [
                    (left.at[here], left_s.at[here, :rows_in]),
                    (left_got.at[here], left_s.at[here, rows_in:]),
                ],
                l_sem.at[g],
            )
        )
    base = 0
    for k, (first, cols, sizes) in enumerate(parts):
        waits_r[k]()
        stage = stages[k]
        block = stage.shape[1]
        each = group // block
        for g in range(count):
            if k == 0:
                waits_l[g]()
            product = by_last(left_s[g * group : (g + 1) * group, :], rights[k][...])
            for i in range(each):
                j = g * each + i
                stage[j] = product[i * block : (i + 1) * block, :cols].astype(BF16)
                slot = slots[k, j]
                at = 0
                for out, size in zip(outs[base : base + len(sizes)], sizes):

                    @pl.when((slot >= at) & (slot < at + size))
                    def _(out=out, at=at, j=j, k=k, slot=slot, stage=stage):
                        pltpu.make_async_copy(
                            stage.at[j], out.at[slot - at], sem.at[k, j]
                        ).start()

                    at += size
        base += len(sizes)
    base = 0
    for k, (_, _, sizes) in enumerate(parts):
        for j in range(stages[k].shape[0]):
            pltpu.make_async_copy(stages[k].at[j], outs[base].at[0], sem.at[k, j]).wait()
        base += len(sizes)


def grad_blocks(left, left_got, right, right_got, slots, parts, after):
    width, rows = left.shape
    block = 200
    count = width // block

    def kernel(*refs):
        blocks_kernel(parts, *refs)

    return pl.pallas_call(
        kernel,
        out_shape=[
            jax.ShapeDtypeStruct((size, block, cols), BF16)
            for _, cols, sizes in parts
            for size in sizes
        ],
        in_specs=[SMEM] + [ANY] * (4 + len(after)),
        out_specs=[ANY] * sum(len(sizes) for _, _, sizes in parts),
        scratch_shapes=[pltpu.VMEM((width, 2 * rows), BF16)]
        + [pltpu.VMEM((-(-cols // 256) * 256, 2 * rows), BF16) for _, cols, _ in parts]
        + [pltpu.VMEM((count, block, cols), BF16) for _, cols, _ in parts]
        + [
            pltpu.SemaphoreType.DMA((width // 800, 2)),
            pltpu.SemaphoreType.DMA((len(parts), 2)),
            pltpu.SemaphoreType.DMA((len(parts), count)),
        ],
        compiler_params=params(32),
        cost_estimate=cost(10**8, 10**6),
    )(slots, left, left_got, right, right_got, *after)


def z_order(z, xl):
    pairs = [(2, 0), (1, 1), (2, 1), (3, 0), (1, 0), (3, 1), (0, 0), (0, 1)]
    return [((z + dz) % Z) * XL + x for dz, x in pairs]


def x_order(z, xl):
    pairs = [(dz, dx) for dx in (1, 0) for dz in (2, 1, 3, 0)]
    return [((z + dz) % Z) * XL + (xl + dx) % XL for dz, dx in pairs]


def slots_of(order):
    order = jnp.stack(order).astype(jnp.int32)
    index = jnp.arange(order.shape[0], dtype=jnp.int32)
    return jnp.sum(jnp.where(order[None, :] == index[:, None], index[None, :], 0), 1)


def beside(*parts):
    return jnp.concatenate(parts, 1)


def below(*parts):
    return jnp.concatenate(parts, 0)


def on_device(
    lm_grad, encoder_row, patch_count, hidden_in, norm_gain, layer_scale, up_weight, down_weight
):
    tok_rows, width = hidden_in.shape
    rest = up_weight.shape[1] - CUT
    up_turned, down_turned = up_weight.T, down_weight.T
    group_len = tok_rows * MEMBERS
    per_pair = tok_rows // BLOCKS
    half = tok_rows // 2
    z, xl, core = lax.axis_index("z"), lax.axis_index("xl"), lax.axis_index("core")
    y, xh = lax.axis_index("y"), lax.axis_index("xh")
    group = (z * XL + xl) * CORE + core
    core_at = core.reshape(1).astype(jnp.int32)
    z_slots, x_slots = slots_of(z_order(z, xl)), slots_of(x_order(z, xl))

    inputs = hidden_in.astype(F32)
    inverse_rms = lax.rsqrt(jnp.mean(inputs * inputs, -1, keepdims=True) + 1e-06)
    normed_own = (inputs * inverse_rms * norm_gain).astype(BF16)

    n_prev = shift(normed_own, "y", Y, 1)
    n_next = shift(normed_own, "y", Y, -1)
    n_other = shift(normed_own, "xh", XH, 1)

    image, place = encoder_row // group_len, encoder_row % group_len
    index = jnp.arange(tok_rows, dtype=jnp.int32)
    same = (image[:, None] == image[None, :]) & (index[None, :] < index[:, None])
    slot = image * per_pair + jnp.sum(same.astype(jnp.int32), 1)
    sorter = (slot[None, :] == index[:, None]).astype(BF16)
    column = jnp.arange(ID_COLS, dtype=jnp.int32)[None, :]
    tags = jnp.where(
        column == 0,
        (place // ID_BASE)[:, None],
        jnp.where(column == 1, (place % ID_BASE)[:, None], 0),
    ).astype(BF16)
    ordered = jnp.dot(sorter, beside(lm_grad, tags), preferred_element_type=F32).astype(BF16)
    arrived = lax.all_to_all(
        ordered.reshape(BLOCKS, per_pair, width + ID_COLS),
        ("z", "xl", "core"),
        split_axis=0,
        concat_axis=0,
    ).reshape(tok_rows, width + ID_COLS)

    n_prev, n_next, n_other = together(n_prev, n_next, n_other)
    mix_prev = shift(below(n_other, n_prev[:half]), "y", Y, 1)
    mix_next = shift(below(n_other, n_next[half:]), "y", Y, -1)
    g_other = shift(arrived, "xh", XH, 1)
    mix_prev, mix_next, g_other, arrived = together(mix_prev, mix_next, g_other, arrived)

    far_a = shift(mix_prev[:half], "y", Y, 1)
    far_b = shift(mix_next[half:tok_rows], "y", Y, -1)
    order = jnp.stack(z_order(z, xl)).astype(jnp.int32)
    g_1, g_2 = prepare(order, arrived, g_other, width)
    far_a, far_b, g_1, g_2 = together(far_a, far_b, g_1, g_2)

    g_prev_1, g_next_1 = shift(g_1, "y", Y, 1), shift(g_1, "y", Y, -1)
    act, slope, n_keep, n_give = assemble_normed(
        core_at,
        (normed_own, n_other, n_next, n_prev, mix_prev, mix_next, below(far_a, far_b)),
        up_turned,
    )
    n_got = shift(n_give, "core", CORE, 1)
    act_got = shift(act, "core", CORE, 1)
    g_prev_1, g_next_1 = together(g_prev_1, g_next_1)

    f_prev_1 = shift(g_prev_1[:tok_rows], "y", Y, 1)
    f_next_1 = shift(g_next_1[tok_rows:], "y", Y, -1)
    f_prev_1, f_next_1, g_2, act = together(f_prev_1, f_next_1, g_2, act)
    g_prev_2, g_next_2 = shift(g_2, "y", Y, 1), shift(g_2, "y", Y, -1)

    block = jnp.arange(MEMBERS, dtype=jnp.int32)
    member = ((block // XH + y) % Y) * XH + (block % XH + xh) % XH
    positions = (member[:, None] * tok_rows + index[None, :]).reshape(group_len, 1)
    limit = lax.dynamic_index_in_dim(patch_count, group, 0, keepdims=False)
    positions = jnp.where(positions < limit, positions, -1).astype(F32)
    scale_column = layer_scale.reshape(width, 1)
    s_1, d_keep_1, d_give_1, own_first, chooser = route(
        False, core_at, order, scale_column, positions,
        (g_1, g_prev_1, g_next_1, f_prev_1, f_next_1),
    )
    d_got_1 = shift(d_give_1, "core", CORE, 1)
    g_prev_2, g_next_2, d_got_1 = together(g_prev_2, g_next_2, d_got_1)

    f_prev_2 = shift(g_prev_2[:tok_rows], "y", Y, 1)
    f_next_2 = shift(g_next_2[tok_rows:], "y", Y, -1)
    here = xl == 0
    straight = jnp.arange(4, dtype=jnp.int32)
    slots_1 = jnp.stack([straight, jnp.where(here, jnp.array([2, 1, 0, 3]), jnp.array([0, 3, 2, 1]))])
    slots_2 = jnp.stack([straight, jnp.where(here, jnp.array([2, 0, 3, 1]), jnp.array([0, 2, 1, 3]))])
    slots_1, slots_2 = slots_1.astype(jnp.int32), slots_2.astype(jnp.int32)
    d_up, d_down, d_out_1, d_mine_1 = grad_blocks(
        d_keep_1, d_got_1, act, act_got, slots_1,
        ((0, CUT, (2, 2)), (CUT, rest, (2, 2))), (g_next_2,),
    )
    d_prev, d_next = shift(d_up, "z", Z, 1), shift(d_down, "z", Z, -1)
    d_x_1 = shift(d_out_1, "xl", XL, 1)
    f_prev_2, f_next_2, _ = together(f_prev_2, f_next_2, d_out_1)
    s_2, d_keep_2, d_give_2, own_grad = route(
        True, core_at, order, scale_column, chooser,
        (g_2, g_prev_2, g_next_2, f_prev_2, f_next_2), (own_first,),
    )
    d_got_2 = shift(d_give_2, "core", CORE, 1)
    pre_a = times_slope(order, (s_1, s_2), down_turned, slope, 0, CUT, 256, ())
    pre_a_got = shift(pre_a, "core", CORE, 1)
    pre_b = times_slope(order, (s_1, s_2), down_turned, slope, CUT, rest, rest // 2, (pre_a,))
    pre_b_got = shift(pre_b, "core", CORE, 1)
    u_up, u_down, u_kept = grad_blocks(
        n_keep, n_got, pre_a, pre_a_got, z_slots[None], ((0, CUT, (2, 2, 4)),), (pre_b,)
    )
    u_prev, u_next = shift(u_up, "z", Z, 1), shift(u_down, "z", Z, -1)
    d_kept, d_out_2, d_mine_2 = grad_blocks(
        d_keep_2, d_got_2, act, act_got, slots_2,
        ((0, CUT, (4,)), (CUT, rest, (2, 2))), (u_kept,),
    )
    d_x_2 = shift(d_out_2, "xl", XL, 1)
    pre_all, _ = together(below(pre_a, pre_b), d_kept)
    parts = lax.dot_general(
        pre_all, up_turned, (((0,), (0,)), ((), ())), preferred_element_type=F32
    ).astype(BF16)
    u_out, u_mine = grad_blocks(
        n_keep, n_got, pre_b, pre_b_got, x_slots[None], ((0, rest, (4, 4)),), (parts,)
    )
    u_x = shift(u_out, "xl", XL, 1)
    d_prev, d_next, u_prev, u_next, d_x_1, d_x_2, parts = together(
        d_prev, d_next, u_prev, u_next, d_x_1, d_x_2, parts
    )

    cut = -(-d_x_1.shape[1] // 16) * 8
    two, side_1, side_2 = (
        add(d_mine_1[0], d_x_1[0]), add(d_mine_1[1], d_x_1[1]), add(d_mine_2[0], d_x_2[0])
    )
    one, three = jnp.where(here, side_2, side_1), jnp.where(here, side_1, side_2)
    d_here = add32(d_mine_2[1], d_x_2[1])
    d_b_one, d_b_three = one[:cut], three[cut:]
    to_prev = beside(
        add(d_kept[1], d_next[0]), add(u_kept[1], u_next[0]), below(three[:cut], two[cut:])
    )
    to_next = beside(
        add(d_kept[0], d_prev[0]), add(u_kept[0], u_prev[0]), below(two[:cut], one[cut:])
    )
    m_prev, m_next = shift(to_next, "z", Z, 1), shift(to_prev, "z", Z, -1)
    parts = parts.reshape(MEMBERS, tok_rows, width)
    p_prev = shift(below(parts[4][:half], parts[5][:half]), "y", Y, 1)
    p_next = shift(below(parts[4][half:], parts[5][half:]), "y", Y, -1)
    m_prev, m_next, u_x, p_prev, p_next = together(m_prev, m_next, u_x, p_prev, p_next)

    d_acc_prev, u_acc_prev, d_b_prev = m_prev[:, :CUT], m_prev[:, CUT : 2 * CUT], m_prev[:, 2 * CUT :]
    d_acc_next, u_acc_next, d_b_next = m_next[:, :CUT], m_next[:, CUT : 2 * CUT], m_next[:, 2 * CUT :]
    sum_0 = beside(add(d_kept[2], d_next[1], d_acc_prev), add(u_kept[2], u_next[1], u_acc_prev))
    sum_1 = beside(add(d_kept[3], d_prev[1], d_acc_next), add(u_kept[3], u_prev[1], u_acc_next))
    a_own = jnp.where(xl == 0, sum_0, sum_1)
    a_other = shift(jnp.where(xl == 0, sum_1, sum_0), "xl", XL, 1)
    two, one, three = (add(u_mine[i], u_x[i]) for i in range(3))
    u_here = add32(u_mine[3], u_x[3])
    u_b_one, u_b_three = one[:cut], three[cut:]
    b_prev = shift(below(add(d_b_one, d_b_prev[:cut]), two[:cut], one[cut:]), "z", Z, 1)
    b_next = shift(below(add(d_b_three, d_b_next[cut:]), three[:cut], two[cut:]), "z", Z, -1)
    r_prev = shift(
        below(
            add(parts[2][:half], p_prev[:half]), parts[2][half:],
            add(parts[3][:half], p_prev[half:]), parts[3][half:],
        ),
        "y", Y, 1,
    )
    r_next = shift(
        below(
            parts[6][:half], add(parts[6][half:], p_next[:half]),
            parts[7][:half], add(parts[7][half:], p_next[half:]),
        ),
        "y", Y, -1,
    )
    a_other, b_prev, b_next, r_prev, r_next = together(a_other, b_prev, b_next, r_prev, r_next)

    r_other = shift(add(parts[1], r_prev[tok_rows:], r_next[tok_rows:]), "xh", XH, 1)
    tail = d_here.shape[0] - cut
    u_b_prev, u_b_next = b_prev[cut:], b_next[tail:]
    c_prev = shift(add(u_b_one, u_b_prev[:cut]), "z", Z, 1)
    c_next = shift(add(u_b_three, u_b_next[cut:]), "z", Z, -1)
    a_total = add32(a_own, a_other)
    down_b = below(
        add32(d_here[:cut], d_b_next[:cut], b_prev[:cut]),
        add32(d_here[cut:], d_b_prev[cut:], b_next[:tail]),
    )
    up_b = below(
        add32(u_here[:cut], u_b_next[:cut], c_prev),
        add32(u_here[cut:], u_b_prev[cut:], c_next),
    )
    normed_grad = add32(parts[0], r_prev[:tok_rows], r_next[:tok_rows], r_other)
    weighted = norm_gain * normed_grad
    input_grad = (
        own_grad.astype(F32)
        + inverse_rms * weighted
        - inputs * inverse_rms**3 * jnp.mean(weighted * inputs, -1, keepdims=True)
    ).astype(BF16)
    grad_scale = 1.0 / math.sqrt(group_len * BLOCKS)
    return (
        input_grad,
        (beside(a_total[:, CUT:], up_b) * grad_scale).astype(BF16),
        (beside(a_total[:, :CUT], down_b) * grad_scale).astype(BF16),
    )


def solution(mesh):
    fine = Mesh(mesh.devices.reshape(Z, XL, CORE, Y, XH), AXES)
    dp, tensor = AXES[:3], AXES[3:]
    in_specs = (
        P(AXES, None),
        P(AXES),
        P(),
        P(AXES, None),
        P(),
        P(),
        P(None, tensor),
        P(None, tensor),
    )
    out_specs = (P(AXES, None), P(dp, tensor), P(dp, tensor))
    return jax.shard_map(
        on_device, mesh=fine, in_specs=in_specs, out_specs=out_specs, check_vma=False
    )
```

```python
import math

import jax
import jax.numpy as jnp
from jax import lax
from jax.experimental import pallas as pl
from jax.experimental.pallas import tpu as pltpu
from jax.sharding import Mesh, PartitionSpec as P

F32 = jnp.float32
BF16 = jnp.bfloat16
Z, XL, CORE, Y, XH = 4, 2, 2, 4, 2
AXES = ("z", "xl", "core", "y", "xh")
MEMBERS = Y * XH
BLOCKS = Z * XL * CORE
ID_COLS = 128
ID_BASE = 32
CUT = 1024
MIB = 1024 * 1024
VMEM = pl.BlockSpec(memory_space=pltpu.VMEM)
SMEM = pl.BlockSpec(memory_space=pltpu.SMEM)
ANY = pl.BlockSpec(memory_space=pl.ANY)
HBM = pl.BlockSpec(memory_space=pltpu.HBM)


def params(mib):
    return pltpu.CompilerParams(vmem_limit_bytes=mib * MIB)


def cost(flops, moved, special=0):
    return pl.CostEstimate(flops=flops, bytes_accessed=moved, transcendentals=special)


def shift(value, axis, size, step):
    return lax.ppermute(value, axis, [(i, (i + step) % size) for i in range(size)])


def add32(*terms):
    total = terms[0].astype(F32)
    for term in terms[1:]:
        total = total + term.astype(F32)
    return total


def add(*terms):
    return add32(*terms).astype(BF16)


def together(*values):
    return lax.optimization_barrier(values)


def fetch(pieces, sem):
    copies = [pltpu.make_async_copy(src, dst, sem.at[i]) for i, (src, dst) in enumerate(pieces)]
    for copy in copies:
        copy.start()

    def wait():
        for copy in copies:
            copy.wait()

    return wait


def pieces_of(listed, out):
    at, pieces = 0, []
    for ref, first, rows in listed:
        pieces.append((ref.at[first : first + rows], out.at[at : at + rows]))
        at += rows
    return pieces


def split_parity(turned, core, pairs, keep, give):
    rows = keep.shape[0] // pairs
    for two in range(pairs // 2):
        for out, parity in ((keep, core), (give, 1 - core)):
            blocks = [
                turned[pl.ds(pl.multiple_of((2 * b + parity) * rows, 8), rows), :]
                for b in (2 * two, 2 * two + 1)
            ]
            out[2 * two * rows : (2 * two + 2) * rows, :] = jnp.concatenate(blocks, 0).astype(BF16)


def by_last(left, right):
    return lax.dot_general(left, right, (((1,), (1,)), ((), ())), preferred_element_type=F32)


def stream(weight, first, tile, count, held, sem, body):
    def copy(n):
        slot = lax.rem(n, 2)
        rows = pl.ds(pl.multiple_of(first + n * tile, 16), tile)
        return pltpu.make_async_copy(weight.at[rows], held.at[slot], sem.at[slot])

    copy(0).start()

    @pl.loop(0, count)
    def _(n):
        @pl.when(n + 1 < count)
        def _():
            copy(n + 1).start()

        copy(n).wait()
        body(n, held[lax.rem(n, 2)])


def normed_kernel(tile, core, *refs):
    ins, weight, (act, slope, keep, give) = refs[:7], refs[7], refs[8:12]
    normed, turned, held, act_s, slope_s, keep_s, give_s, in_sem, w_sem, out_sem = refs[12:]
    own, other, nxt, prev, mix_prev, mix_next, far = ins
    full = own.shape[0]
    half = full // 2
    listed = [(own, 0, full), (other, 0, full), (nxt, 0, full), (mix_next, 0, full)]
    listed += [(mix_prev, full, half), (mix_next, full, half), (far, 0, full)]
    listed += [(prev, 0, full), (mix_prev, 0, full)]
    fetch(pieces_of(listed, normed), in_sem)()
    for t in range(normed.shape[1] // 128):
        cols = slice(t * 128, (t + 1) * 128)
        turned[cols, :] = normed[:, cols].astype(F32).T
    split_parity(turned, core[0], BLOCKS // 2, keep_s, give_s)
    done = fetch([(keep_s, keep), (give_s, give)], out_sem)

    def body(n, rows):
        at = pl.ds(pl.multiple_of(n * tile, 16), tile)
        value = by_last(rows, normed[...])
        below = 0.5 * (1.0 + lax.erf(value * 0.7071067811865476))
        act_s[at, :] = (value * below).astype(BF16)
        slope_s[at, :] = below + value * jnp.exp(-0.5 * value * value) * 0.3989422804014327

    stream(weight, 0, tile, act.shape[0] // tile, held, w_sem, body)
    done()
    fetch([(act_s, act), (slope_s, slope)], out_sem)()


def assemble_normed(core, ins, weight):
    rows, width = ins[0].shape[0] * MEMBERS, ins[0].shape[1]
    hidden = weight.shape[0]
    tile = 320

    def kernel(*refs):
        normed_kernel(tile, *refs)

    outs = [((hidden, rows), BF16), ((hidden, rows), F32)] + [((width // 2, rows), BF16)] * 2
    return pl.pallas_call(
        kernel,
        out_shape=[jax.ShapeDtypeStruct(shape, kind) for shape, kind in outs],
        in_specs=[SMEM] + [HBM] * (len(ins) + 1),
        out_specs=[HBM] * 4,
        scratch_shapes=[
            pltpu.VMEM((rows, width), BF16),
            pltpu.VMEM((width, rows), F32),
            pltpu.VMEM((2, tile, width), BF16),
        ]
        + [pltpu.VMEM(shape, kind) for shape, kind in outs]
        + [pltpu.SemaphoreType.DMA((n,)) for n in (9, 2, 2)],
        compiler_params=params(52),
        cost_estimate=cost(10**8, 10**6),
    )(core, *ins, weight)


def prepare_kernel(order, own, other, first, second, rows_s, turned, sorted_s, *refs):
    outs_s, in_sem, sem = refs[:2], refs[2], refs[3]
    half = own.shape[0] // 2
    listed = [(own, 0, half), (other, 0, half), (own, half, half), (other, half, half)]
    fetch(pieces_of(listed, rows_s), in_sem)()
    width = turned.shape[0]
    pair = width // (BLOCKS // 2)
    for t in range(width // 128):
        cols = slice(t * 128, (t + 1) * 128)
        turned[cols, :] = rows_s[:, cols].astype(F32).T
    waits = []
    for h, out in enumerate((first, second)):
        for p in range(4):
            at = pl.ds(pl.multiple_of(order[4 * h + p] * pair, 8), pair)
            sorted_s[p * pair : (p + 1) * pair, :] = turned[at, :]
        cols = width // 2
        lead = 0 if h else ID_COLS
        for first_col in range(0, cols, 128):
            last = min(first_col + 128, cols)
            outs_s[h][:, lead + first_col : lead + last] = (
                sorted_s[first_col : first_col + 128, :].T[:, : last - first_col].astype(BF16)
            )
        if h == 0:
            outs_s[h][:, :lead] = rows_s[:, width : width + ID_COLS]
        waits.append(fetch([(outs_s[h], out)], sem.at[h]))
    for wait in waits:
        wait()


def prepare(order, own, other, width):
    rows = 2 * own.shape[0]
    cols = width // 2
    return pl.pallas_call(
        prepare_kernel,
        out_shape=[
            jax.ShapeDtypeStruct((rows, cols + ID_COLS), BF16),
            jax.ShapeDtypeStruct((rows, cols), BF16),
        ],
        in_specs=[SMEM, HBM, HBM],
        out_specs=[HBM, HBM],
        scratch_shapes=[
            pltpu.VMEM((rows, width + ID_COLS), BF16),
            pltpu.VMEM((width, rows), F32),
            pltpu.VMEM((-(-cols // 128) * 128, rows), F32),
            pltpu.VMEM((rows, cols + ID_COLS), BF16),
            pltpu.VMEM((rows, cols), BF16),
            pltpu.SemaphoreType.DMA((4,)),
            pltpu.SemaphoreType.DMA((2, 1)),
        ],
        compiler_params=params(52),
        cost_estimate=cost(10**8, 10**6),
    )(order, own, other)


def route_kernel(second, core, order, layer_scale, extra, *refs):
    ins, refs = refs[:5], refs[5:]
    if second:
        own_first, scaled, keep, give, own_grad = refs[:5]
    else:
        scaled, keep, give, own_turned, chooser_out = refs[:5]
    joined, turned, scaled_s, keep_s, give_s, chooser, own_s, own_rows, in_sem, sem = refs[5:]
    cols = scaled.shape[0]
    pair = cols // 4
    lead = 0 if second else ID_COLS
    at, pieces = 0, []
    for ref in ins:
        rows = ref.shape[0]
        pieces.append((ref, joined.at[at : at + rows]))
        at += rows
    if second:
        pieces += [(extra, chooser), (own_first, own_s.at[0])]
    fetch(pieces, in_sem)()
    if not second:
        tags = joined[:, :lead].astype(F32).T
        places = tags[0:1, :] * ID_BASE + tags[1:2, :]
        chooser[...] = (extra[...] == places).astype(F32).astype(BF16)
    step = 640
    for first in range(0, cols, step):
        last = min(first + step, cols)
        grads = jnp.dot(
            chooser[...], joined[:, lead + first : lead + last], preferred_element_type=F32
        )
        turned[first:last, :] = grads.T
    own_s[1 if second else 0] = turned[:cols, :128]
    for p in range(4):
        here = slice(p * pair, (p + 1) * pair)
        place = order[p + (4 if second else 0)]
        scale = layer_scale[pl.ds(pl.multiple_of(place * pair, 8), pair), :]
        value = turned[here, :] * scale
        turned[here, :] = value
        scaled_s[here, :] = value.astype(BF16)
    split_parity(turned, core[0], 4, keep_s, give_s)
    outs = [(scaled_s, scaled), (keep_s, keep), (give_s, give)]
    if not second:
        outs += [(own_s.at[0], own_turned), (chooser, chooser_out)]
    done = fetch(outs, sem)
    if second:
        for p in range(8):
            at = pl.ds(pl.multiple_of(order[p] * pair, 8), pair)
            own_rows[at, :] = own_s[p // 4, (p % 4) * pair : (p % 4 + 1) * pair, :]
        half = own_grad.shape[0]
        for t in range(own_rows.shape[0] // 128):
            here = slice(t * 128, (t + 1) * 128)
            own_grad[:, here] = own_rows[here, :].T[:half].astype(BF16)
    done()


def route(second, core, order, layer_scale, extra, ins, own_first=()):
    rows, width = 4 * ins[0].shape[0], layer_scale.shape[0]
    cols = width // 2

    def kernel(*refs):
        route_kernel(second, *refs)

    own = [((ins[0].shape[0] // 2, width), BF16)] if second else [((cols, 128), F32)]
    outs = [((cols, rows), BF16), ((cols // 2, rows), BF16), ((cols // 2, rows), BF16)] + own
    if not second:
        outs += [((rows, rows), BF16)]
    return pl.pallas_call(
        kernel,
        out_shape=[jax.ShapeDtypeStruct(shape, kind) for shape, kind in outs],
        in_specs=[SMEM, SMEM, VMEM, HBM if second else VMEM] + [HBM] * (len(ins) + len(own_first)),
        out_specs=[HBM] * 3 + ([VMEM] if second else [HBM] * 2),
        scratch_shapes=[
            pltpu.VMEM((rows, ins[0].shape[1]), BF16),
            pltpu.VMEM((cols, rows), F32),
            pltpu.VMEM((cols, rows), BF16),
            pltpu.VMEM((cols // 2, rows), BF16),
            pltpu.VMEM((cols // 2, rows), BF16),
            pltpu.VMEM((rows, rows), BF16),
            pltpu.VMEM((2, cols, 128), F32),
            pltpu.VMEM((width, 128), F32),
            pltpu.SemaphoreType.DMA((7,)),
            pltpu.SemaphoreType.DMA((5,)),
        ],
        compiler_params=params(52),
        cost_estimate=cost(10**8, 10**6),
    )(core, order, layer_scale, extra, *ins, *own_first)


def slope_kernel(first, tile, order, scaled_1, scaled_2, weight, slope, *refs):
    out, scaled, slope_s, held, out_s, in_sem, w_sem, sem = refs[-8:]
    count = out.shape[0]
    pair = scaled_1.shape[0] // 4
    pieces = [(slope.at[first : first + count], slope_s)]
    for p in range(8):
        source = (scaled_1, scaled_2)[p // 4].at[(p % 4) * pair : (p % 4 + 1) * pair]
        at = pl.ds(pl.multiple_of(order[p] * pair, 16), pair)
        pieces.append((source, scaled.at[at]))
    fetch(pieces, in_sem)()

    def body(n, rows):
        at = pl.ds(pl.multiple_of(n * tile, 16), tile)
        value = jnp.dot(rows, scaled[...], preferred_element_type=F32)
        out_s[at, :] = (value * slope_s[at, :]).astype(BF16)

    stream(weight, first, tile, count // tile, held, w_sem, body)
    fetch([(out_s, out)], sem)()


def times_slope(order, scaled, weight, slope, first, count, tile, after):
    width, rows = weight.shape[1], slope.shape[1]

    def kernel(*refs):
        slope_kernel(first, tile, *refs)

    return pl.pallas_call(
        kernel,
        out_shape=jax.ShapeDtypeStruct((count, rows), BF16),
        in_specs=[SMEM] + [HBM] * 4 + [ANY] * len(after),
        out_specs=HBM,
        scratch_shapes=[
            pltpu.VMEM((width, rows), BF16),
            pltpu.VMEM((count, rows), F32),
            pltpu.VMEM((2, tile, width), BF16),
            pltpu.VMEM((count, rows), BF16),
        ]
        + [pltpu.SemaphoreType.DMA((n,)) for n in (9, 2, 1)],
        compiler_params=params(52),
        cost_estimate=cost(10**8, 10**6),
    )(order, *scaled, weight, slope, *after)


def blocks_kernel(parts, slots, left, left_got, right, right_got, *refs):
    total = sum(len(sizes) for _, _, sizes in parts)
    n = len(parts)
    tail = 2 * n + 4
    outs, refs = refs[-tail - total : -tail], refs[-tail:]
    left_s, rights, stages = refs[0], refs[1 : 1 + n], refs[1 + n : 1 + 2 * n]
    l_sem, r_sem, sem = refs[1 + 2 * n :]
    rows_in = left.shape[1]
    group = 800
    count = left.shape[0] // group
    waits_r = []
    for k, (first, cols, _) in enumerate(parts):
        here = slice(first, first + cols)
        waits_r.append(
            fetch(
                [
                    (right.at[here], rights[k].at[:cols, :rows_in]),
                    (right_got.at[here], rights[k].at[:cols, rows_in:]),
                ],
                r_sem.at[k],
            )
        )
    waits_l = []
    for g in range(count):
        here = slice(g * group, (g + 1) * group)
        waits_l.append(
            fetch(
                [
                    (left.at[here], left_s.at[here, :rows_in]),
                    (left_got.at[here], left_s.at[here, rows_in:]),
                ],
                l_sem.at[g],
            )
        )
    base = 0
    for k, (first, cols, sizes) in enumerate(parts):
        waits_r[k]()
        stage = stages[k]
        block = stage.shape[1]
        each = group // block
        for g in range(count):
            if k == 0:
                waits_l[g]()
            product = by_last(left_s[g * group : (g + 1) * group, :], rights[k][...])
            for i in range(each):
                j = g * each + i
                stage[j] = product[i * block : (i + 1) * block, :cols].astype(BF16)
                slot = slots[k, j]
                at = 0
                for out, size in zip(outs[base : base + len(sizes)], sizes):

                    @pl.when((slot >= at) & (slot < at + size))
                    def _(out=out, at=at, j=j, k=k, slot=slot, stage=stage):
                        pltpu.make_async_copy(
                            stage.at[j], out.at[slot - at], sem.at[k, j]
                        ).start()

                    at += size
        base += len(sizes)
    base = 0
    for k, (_, _, sizes) in enumerate(parts):
        for j in range(stages[k].shape[0]):
            pltpu.make_async_copy(stages[k].at[j], outs[base].at[0], sem.at[k, j]).wait()
        base += len(sizes)


def grad_blocks(left, left_got, right, right_got, slots, parts, after):
    width, rows = left.shape
    block = 200
    count = width // block

    def kernel(*refs):
        blocks_kernel(parts, *refs)

    return pl.pallas_call(
        kernel,
        out_shape=[
            jax.ShapeDtypeStruct((size, block, cols), BF16)
            for _, cols, sizes in parts
            for size in sizes
        ],
        in_specs=[SMEM] + [HBM] * 4 + [ANY] * len(after),
        out_specs=[HBM] * sum(len(sizes) for _, _, sizes in parts),
        scratch_shapes=[pltpu.VMEM((width, 2 * rows), BF16)]
        + [pltpu.VMEM((-(-cols // 256) * 256, 2 * rows), BF16) for _, cols, _ in parts]
        + [pltpu.VMEM((count, block, cols), BF16) for _, cols, _ in parts]
        + [
            pltpu.SemaphoreType.DMA((width // 800, 2)),
            pltpu.SemaphoreType.DMA((len(parts), 2)),
            pltpu.SemaphoreType.DMA((len(parts), count)),
        ],
        compiler_params=params(52),
        cost_estimate=cost(10**8, 10**6),
    )(slots, left, left_got, right, right_got, *after)


def z_order(z, xl):
    pairs = [(2, 0), (1, 1), (2, 1), (3, 0), (1, 0), (3, 1), (0, 0), (0, 1)]
    return [((z + dz) % Z) * XL + x for dz, x in pairs]


def x_order(z, xl):
    pairs = [(dz, dx) for dx in (1, 0) for dz in (2, 1, 3, 0)]
    return [((z + dz) % Z) * XL + (xl + dx) % XL for dz, dx in pairs]


def slots_of(order):
    order = jnp.stack(order).astype(jnp.int32)
    index = jnp.arange(order.shape[0], dtype=jnp.int32)
    return jnp.sum(jnp.where(order[None, :] == index[:, None], index[None, :], 0), 1)


def beside(*parts):
    return jnp.concatenate(parts, 1)


def below(*parts):
    return jnp.concatenate(parts, 0)


def on_device(
    lm_grad, encoder_row, patch_count, hidden_in, norm_gain, layer_scale, up_weight, down_weight
):
    tok_rows, width = hidden_in.shape
    rest = up_weight.shape[1] - CUT
    up_turned, down_turned = up_weight.T, down_weight.T
    group_len = tok_rows * MEMBERS
    per_pair = tok_rows // BLOCKS
    half = tok_rows // 2
    z, xl, core = lax.axis_index("z"), lax.axis_index("xl"), lax.axis_index("core")
    y, xh = lax.axis_index("y"), lax.axis_index("xh")
    group = (z * XL + xl) * CORE + core
    core_at = core.reshape(1).astype(jnp.int32)
    z_slots, x_slots = slots_of(z_order(z, xl)), slots_of(x_order(z, xl))

    inputs = hidden_in.astype(F32)
    inverse_rms = lax.rsqrt(jnp.mean(inputs * inputs, -1, keepdims=True) + 1e-06)
    normed_own = (inputs * inverse_rms * norm_gain).astype(BF16)

    n_prev = shift(normed_own, "y", Y, 1)
    n_next = shift(normed_own, "y", Y, -1)
    n_other = shift(normed_own, "xh", XH, 1)

    image, place = encoder_row // group_len, encoder_row % group_len
    index = jnp.arange(tok_rows, dtype=jnp.int32)
    same = (image[:, None] == image[None, :]) & (index[None, :] < index[:, None])
    slot = image * per_pair + jnp.sum(same.astype(jnp.int32), 1)
    sorter = (slot[None, :] == index[:, None]).astype(BF16)
    column = jnp.arange(ID_COLS, dtype=jnp.int32)[None, :]
    tags = jnp.where(
        column == 0,
        (place // ID_BASE)[:, None],
        jnp.where(column == 1, (place % ID_BASE)[:, None], 0),
    ).astype(BF16)
    ordered = jnp.dot(sorter, beside(lm_grad, tags), preferred_element_type=F32).astype(BF16)
    arrived = lax.all_to_all(
        ordered.reshape(BLOCKS, per_pair, width + ID_COLS),
        ("z", "xl", "core"),
        split_axis=0,
        concat_axis=0,
    ).reshape(tok_rows, width + ID_COLS)

    n_prev, n_next, n_other = together(n_prev, n_next, n_other)
    mix_prev = shift(below(n_other, n_prev[:half]), "y", Y, 1)
    mix_next = shift(below(n_other, n_next[half:]), "y", Y, -1)
    g_other = shift(arrived, "xh", XH, 1)
    mix_prev, mix_next, g_other, arrived = together(mix_prev, mix_next, g_other, arrived)

    far_a = shift(mix_prev[:half], "y", Y, 1)
    far_b = shift(mix_next[half:tok_rows], "y", Y, -1)
    order = jnp.stack(z_order(z, xl)).astype(jnp.int32)
    g_1, g_2 = prepare(order, arrived, g_other, width)
    far_a, far_b, g_1, g_2 = together(far_a, far_b, g_1, g_2)

    g_prev_1, g_next_1 = shift(g_1, "y", Y, 1), shift(g_1, "y", Y, -1)
    act, slope, n_keep, n_give = assemble_normed(
        core_at,
        (normed_own, n_other, n_next, n_prev, mix_prev, mix_next, below(far_a, far_b)),
        up_turned,
    )
    n_got = shift(n_give, "core", CORE, 1)
    act_got = shift(act, "core", CORE, 1)
    g_prev_1, g_next_1 = together(g_prev_1, g_next_1)

    f_prev_1 = shift(g_prev_1[:tok_rows], "y", Y, 1)
    f_next_1 = shift(g_next_1[tok_rows:], "y", Y, -1)
    f_prev_1, f_next_1, g_2, act, act_got, n_got = together(
        f_prev_1, f_next_1, g_2, act, act_got, n_got
    )
    g_prev_2, g_next_2 = shift(g_2, "y", Y, 1), shift(g_2, "y", Y, -1)

    block = jnp.arange(MEMBERS, dtype=jnp.int32)
    member = ((block // XH + y) % Y) * XH + (block % XH + xh) % XH
    positions = (member[:, None] * tok_rows + index[None, :]).reshape(group_len, 1)
    limit = lax.dynamic_index_in_dim(patch_count, group, 0, keepdims=False)
    positions = jnp.where(positions < limit, positions, -1).astype(F32)
    scale_column = layer_scale.reshape(width, 1)
    s_1, d_keep_1, d_give_1, own_first, chooser = route(
        False, core_at, order, scale_column, positions,
        (g_1, g_prev_1, g_next_1, f_prev_1, f_next_1),
    )
    d_got_1 = shift(d_give_1, "core", CORE, 1)
    here = xl == 0
    straight = jnp.arange(4, dtype=jnp.int32)
    slots_1 = jnp.stack([straight, jnp.where(here, jnp.array([2, 1, 0, 3]), jnp.array([0, 3, 2, 1]))])
    slots_2 = jnp.stack([straight, jnp.where(here, jnp.array([2, 0, 3, 1]), jnp.array([0, 2, 1, 3]))])
    slots_1, slots_2 = slots_1.astype(jnp.int32), slots_2.astype(jnp.int32)
    d_up, d_down, d_out_1, d_mine_1 = grad_blocks(
        d_keep_1, d_got_1, act, act_got, slots_1,
        ((0, CUT, (2, 2)), (CUT, rest, (2, 2))), (),
    )

    g_prev_2, g_next_2, d_out_1 = together(g_prev_2, g_next_2, d_out_1)
    f_prev_2 = shift(g_prev_2[:tok_rows], "y", Y, 1)
    f_next_2 = shift(g_next_2[tok_rows:], "y", Y, -1)
    d_prev, d_next = shift(d_up, "z", Z, 1), shift(d_down, "z", Z, -1)
    d_x_1 = shift(d_out_1, "xl", XL, 1)
    s_2, d_keep_2, d_give_2, own_grad = route(
        True, core_at, order, scale_column, chooser,
        (g_2, g_prev_2, g_next_2, f_prev_2, f_next_2), (own_first,),
    )
    d_got_2 = shift(d_give_2, "core", CORE, 1)
    pre_a = times_slope(order, (s_1, s_2), down_turned, slope, 0, CUT, 256, ())
    pre_a_got = shift(pre_a, "core", CORE, 1)

    d_prev, d_next, d_x_1, d_got_2, pre_a = together(d_prev, d_next, d_x_1, d_got_2, pre_a)
    d_kept, d_out_2, d_mine_2 = grad_blocks(
        d_keep_2, d_got_2, act, act_got, slots_2,
        ((0, CUT, (4,)), (CUT, rest, (2, 2))), (pre_a,),
    )
    d_x_2 = shift(d_out_2, "xl", XL, 1)
    d_acc_prev = shift(add(d_kept[0], d_prev[0]), "z", Z, 1)
    d_acc_next = shift(add(d_kept[1], d_next[0]), "z", Z, -1)
    pre_b = times_slope(order, (s_1, s_2), down_turned, slope, CUT, rest, rest // 2, (d_kept,))
    pre_b_got = shift(pre_b, "core", CORE, 1)
    u_up, u_down, u_kept = grad_blocks(
        n_keep, n_got, pre_a, pre_a_got, z_slots[None], ((0, CUT, (2, 2, 4)),), (pre_b,)
    )
    u_prev, u_next = shift(u_up, "z", Z, 1), shift(u_down, "z", Z, -1)

    d_x_2, d_acc_prev, d_acc_next, pre_a, pre_b, pre_b_got, _ = together(
        d_x_2, d_acc_prev, d_acc_next, pre_a, pre_b, pre_b_got, u_kept
    )
    sum_0 = add(d_kept[2], d_next[1], d_acc_prev)
    sum_1 = add(d_kept[3], d_prev[1], d_acc_next)
    d_own = jnp.where(here, sum_0, sum_1)
    d_other = shift(jnp.where(here, sum_1, sum_0), "xl", XL, 1)
    cut = -(-d_x_1.shape[1] // 16) * 8
    two, side_1, side_2 = (
        add(d_mine_1[0], d_x_1[0]), add(d_mine_1[1], d_x_1[1]), add(d_mine_2[0], d_x_2[0])
    )
    one, three = jnp.where(here, side_2, side_1), jnp.where(here, side_1, side_2)
    d_here = add32(d_mine_2[1], d_x_2[1])
    d_b_one, d_b_three = one[:cut], three[cut:]
    d_b_prev = shift(below(two[:cut], one[cut:]), "z", Z, 1)
    d_b_next = shift(below(three[:cut], two[cut:]), "z", Z, -1)
    parts = lax.dot_general(
        below(pre_a, pre_b), up_turned, (((0,), (0,)), ((), ())), preferred_element_type=F32
    ).astype(BF16)
    d_other, d_b_prev, d_b_next, parts = together(d_other, d_b_prev, d_b_next, parts)
    blocks = parts.reshape(MEMBERS, tok_rows, width)
    p_prev = shift(below(blocks[4][:half], blocks[5][:half]), "y", Y, 1)
    p_next = shift(below(blocks[4][half:], blocks[5][half:]), "y", Y, -1)
    u_out, u_mine = grad_blocks(
        n_keep, n_got, pre_b, pre_b_got, x_slots[None], ((0, rest, (4, 4)),), (parts,)
    )
    u_x = shift(u_out, "xl", XL, 1)

    u_prev, u_next, p_prev, p_next, _ = together(u_prev, u_next, p_prev, p_next, u_mine)
    u_acc_prev = shift(add(u_kept[0], u_prev[0]), "z", Z, 1)
    u_acc_next = shift(add(u_kept[1], u_next[0]), "z", Z, -1)
    o_prev = shift(below(add(blocks[3][:half], p_prev[half:]), blocks[3][half:]), "y", Y, 1)
    o_next = shift(below(blocks[7][:half], add(blocks[7][half:], p_next[half:])), "y", Y, -1)
    u_acc_prev, u_acc_next, o_prev, o_next = together(u_acc_prev, u_acc_next, o_prev, o_next)

    sum_0 = add(u_kept[2], u_next[1], u_acc_prev)
    sum_1 = add(u_kept[3], u_prev[1], u_acc_next)
    u_own = jnp.where(here, sum_0, sum_1)
    u_other = shift(jnp.where(here, sum_1, sum_0), "xl", XL, 1)
    r_other = shift(add(blocks[1], o_prev, o_next), "xh", XH, 1)
    r_prev = shift(below(add(blocks[2][:half], p_prev[:half]), blocks[2][half:]), "y", Y, 1)
    r_next = shift(below(blocks[6][:half], add(blocks[6][half:], p_next[:half])), "y", Y, -1)
    u_x, u_other, r_other, r_prev, r_next = together(u_x, u_other, r_other, r_prev, r_next)

    two, one, three = (add(u_mine[i], u_x[i]) for i in range(3))
    u_here = add32(u_mine[3], u_x[3])
    b_prev = shift(
        below(add(d_b_one, d_b_prev[:cut]), two[:cut], one[cut:]), "z", Z, 1
    )
    b_next = shift(
        below(add(d_b_three, d_b_next[cut:]), three[:cut], two[cut:]), "z", Z, -1
    )
    tail = d_here.shape[0] - cut
    u_b_prev, u_b_next = b_prev[cut:], b_next[tail:]
    c_prev = shift(add(one[:cut], u_b_prev[:cut]), "z", Z, 1)
    c_next = shift(add(three[cut:], u_b_next[cut:]), "z", Z, -1)
    down_a, up_a = add32(d_own, d_other), add32(u_own, u_other)
    down_b = below(
        add32(d_here[:cut], d_b_next[:cut], b_prev[:cut]),
        add32(d_here[cut:], d_b_prev[cut:], b_next[:tail]),
    )
    up_b = below(
        add32(u_here[:cut], u_b_next[:cut], c_prev),
        add32(u_here[cut:], u_b_prev[cut:], c_next),
    )
    normed_grad = add32(blocks[0], r_prev, r_next, r_other)
    weighted = norm_gain * normed_grad
    input_grad = (
        own_grad.astype(F32)
        + inverse_rms * weighted
        - inputs * inverse_rms**3 * jnp.mean(weighted * inputs, -1, keepdims=True)
    ).astype(BF16)
    grad_scale = 1.0 / math.sqrt(group_len * BLOCKS)
    return (
        input_grad,
        (beside(up_a, up_b) * grad_scale).astype(BF16),
        (beside(down_a, down_b) * grad_scale).astype(BF16),
    )


def solution(mesh):
    fine = Mesh(mesh.devices.reshape(Z, XL, CORE, Y, XH), AXES)
    dp, tensor = AXES[:3], AXES[3:]
    in_specs = (
        P(AXES, None),
        P(AXES),
        P(),
        P(AXES, None),
        P(),
        P(),
        P(None, tensor),
        P(None, tensor),
    )
    out_specs = (P(AXES, None), P(dp, tensor), P(dp, tensor))
    return jax.shard_map(
        on_device, mesh=fine, in_specs=in_specs, out_specs=out_specs, check_vma=False
    )
```

```python
import math

import jax
import jax.numpy as jnp
from jax import lax
from jax.experimental import pallas as pl
from jax.experimental.pallas import tpu as pltpu
from jax.sharding import Mesh, PartitionSpec as P

F32 = jnp.float32
BF16 = jnp.bfloat16
Z, XL, CORE, Y, XH = 4, 2, 2, 4, 2
AXES = ("z", "xl", "core", "y", "xh")
MEMBERS = Y * XH
BLOCKS = Z * XL * CORE
ID_COLS = 128
ID_BASE = 32
CUT = 1280
MIB = 1024 * 1024
VMEM = pl.BlockSpec(memory_space=pltpu.VMEM)
SMEM = pl.BlockSpec(memory_space=pltpu.SMEM)
ANY = pl.BlockSpec(memory_space=pl.ANY)
HBM = pl.BlockSpec(memory_space=pltpu.HBM)


def params(mib):
    return pltpu.CompilerParams(vmem_limit_bytes=mib * MIB)


def cost(flops, moved, special=0):
    return pl.CostEstimate(flops=flops, bytes_accessed=moved, transcendentals=special)


def shift(value, axis, size, step):
    return lax.ppermute(value, axis, [(i, (i + step) % size) for i in range(size)])


def add32(*terms):
    total = terms[0].astype(F32)
    for term in terms[1:]:
        total = total + term.astype(F32)
    return total


def add(*terms):
    return add32(*terms).astype(BF16)


def together(*values):
    return lax.optimization_barrier(values)


def fetch(pieces, sem):
    copies = [pltpu.make_async_copy(src, dst, sem.at[i]) for i, (src, dst) in enumerate(pieces)]
    for copy in copies:
        copy.start()

    def wait():
        for copy in copies:
            copy.wait()

    return wait


def pieces_of(listed, out):
    at, pieces = 0, []
    for ref, first, rows in listed:
        pieces.append((ref.at[first : first + rows], out.at[at : at + rows]))
        at += rows
    return pieces


def split_parity(turned, core, pairs, keep, give):
    rows = keep.shape[0] // pairs
    for two in range(pairs // 2):
        for out, parity in ((keep, core), (give, 1 - core)):
            blocks = [
                turned[pl.ds(pl.multiple_of((2 * b + parity) * rows, 8), rows), :]
                for b in (2 * two, 2 * two + 1)
            ]
            out[2 * two * rows : (2 * two + 2) * rows, :] = jnp.concatenate(blocks, 0).astype(BF16)


def by_last(left, right):
    return lax.dot_general(left, right, (((1,), (1,)), ((), ())), preferred_element_type=F32)


def normed_kernel(core, *refs):
    ins, weight, (act, slope, keep, give) = refs[:8], refs[8], refs[9:13]
    normed, turned, held, act_s, slope_s, keep_s, give_s, in_sem, w_sem, out_sem, sem = refs[13:]
    own, other, nxt, prev, mix_prev, mix_next, far_a, far_b = ins
    full = own.shape[0]
    half = full // 2
    listed = [(own, 0, full), (other, 0, full), (nxt, 0, full), (mix_next, 0, full)]
    listed += [(mix_prev, full, half), (mix_next, full, half), (far_a, 0, half), (far_b, 0, half)]
    listed += [(prev, 0, full), (mix_prev, 0, full)]
    fetched = fetch(pieces_of(listed, normed), in_sem)
    tile = held.shape[1]
    count = held.shape[0]
    tiles = [slice(n * tile, (n + 1) * tile) for n in range(count)]
    weights = [fetch([(weight.at[tiles[n]], held.at[n])], w_sem.at[n]) for n in range(count)]
    fetched()
    for t in range(normed.shape[1] // 128):
        cols = slice(t * 128, (t + 1) * 128)
        turned[cols, :] = normed[:, cols].astype(F32).T
    split_parity(turned, core[0], BLOCKS // 2, keep_s, give_s)
    waits = [fetch([(give_s, give), (keep_s, keep)], out_sem)]
    for n, rows in enumerate(tiles):
        weights[n]()
        value = by_last(held[n], normed[...])
        below = 0.5 * (1.0 + lax.erf(value * 0.7071067811865476))
        act_s[rows, :] = (value * below).astype(BF16)
        slope_s[rows, :] = (
            below + value * jnp.exp(-0.5 * value * value) * 0.3989422804014327
        ).astype(BF16)
        waits.append(
            fetch([(act_s.at[rows], act.at[rows]), (slope_s.at[rows], slope.at[rows])], sem.at[n])
        )
    for wait in waits:
        wait()


def assemble_normed(core, ins, weight):
    rows, width = ins[0].shape[0] * MEMBERS, ins[0].shape[1]
    hidden = weight.shape[0]
    count = 4
    outs = [((hidden, rows), BF16)] * 2 + [((width // 2, rows), BF16)] * 2
    return pl.pallas_call(
        normed_kernel,
        out_shape=[jax.ShapeDtypeStruct(shape, kind) for shape, kind in outs],
        in_specs=[SMEM] + [HBM] * (len(ins) + 1),
        out_specs=[HBM] * 4,
        scratch_shapes=[
            pltpu.VMEM((rows, width), BF16),
            pltpu.VMEM((width, rows), F32),
            pltpu.VMEM((count, hidden // count, width), BF16),
        ]
        + [pltpu.VMEM(shape, kind) for shape, kind in outs]
        + [pltpu.SemaphoreType.DMA((n,)) for n in (10,)]
        + [pltpu.SemaphoreType.DMA((count, 1)), pltpu.SemaphoreType.DMA((2,))]
        + [pltpu.SemaphoreType.DMA((count, 2))],
        compiler_params=params(52),
        cost_estimate=cost(10**10, 10**7),
    )(core, *ins, weight)


def prepare_kernel(order, own, other, first, second, rows_s, turned, sorted_s, *refs):
    outs_s, in_sem, sem = refs[:2], refs[2], refs[3]
    half = own.shape[0] // 2
    listed = [(own, 0, half), (other, 0, half), (own, half, half), (other, half, half)]
    fetch(pieces_of(listed, rows_s), in_sem)()
    width = turned.shape[0]
    pair = width // (BLOCKS // 2)
    for t in range(width // 128):
        cols = slice(t * 128, (t + 1) * 128)
        turned[cols, :] = rows_s[:, cols].astype(F32).T
    waits = []
    for h, out in enumerate((first, second)):
        for p in range(4):
            at = pl.ds(pl.multiple_of(order[4 * h + p] * pair, 8), pair)
            sorted_s[p * pair : (p + 1) * pair, :] = turned[at, :]
        cols = width // 2
        lead = 0 if h else ID_COLS
        for first_col in range(0, cols, 128):
            last = min(first_col + 128, cols)
            outs_s[h][:, lead + first_col : lead + last] = (
                sorted_s[first_col : first_col + 128, :].T[:, : last - first_col].astype(BF16)
            )
        if h == 0:
            outs_s[h][:, :lead] = rows_s[:, width : width + ID_COLS]
        waits.append(fetch([(outs_s[h], out)], sem.at[h]))
    for wait in waits:
        wait()


def prepare(order, own, other, width):
    rows = 2 * own.shape[0]
    cols = width // 2
    return pl.pallas_call(
        prepare_kernel,
        out_shape=[
            jax.ShapeDtypeStruct((rows, cols + ID_COLS), BF16),
            jax.ShapeDtypeStruct((rows, cols), BF16),
        ],
        in_specs=[SMEM, HBM, HBM],
        out_specs=[HBM, HBM],
        scratch_shapes=[
            pltpu.VMEM((rows, width + ID_COLS), BF16),
            pltpu.VMEM((width, rows), F32),
            pltpu.VMEM((-(-cols // 128) * 128, rows), F32),
            pltpu.VMEM((rows, cols + ID_COLS), BF16),
            pltpu.VMEM((rows, cols), BF16),
            pltpu.SemaphoreType.DMA((4,)),
            pltpu.SemaphoreType.DMA((2, 1)),
        ],
        compiler_params=params(52),
        cost_estimate=cost(10**8, 10**6),
    )(order, own, other)


def joined_pieces(ins, joined):
    at, pieces = 0, []
    for ref in ins:
        rows = ref.shape[0]
        pieces.append((ref, joined.at[at : at + rows]))
        at += rows
    return pieces


def to_image_order(chooser, joined, lead, turned):
    cols = turned.shape[0]
    for first in range(0, cols, 640):
        last = min(first + 640, cols)
        grads = jnp.dot(
            chooser[...], joined[:, lead + first : lead + last], preferred_element_type=F32
        )
        turned[first:last, :] = grads.T


def first_kernel(core, order, scales, positions, *refs):
    ins, (scaled, keep, give, own_turned, chooser_out) = refs[:5], refs[5:10]
    joined, turned, scaled_s, keep_s, give_s, chooser, own_s, in_sem, sem, give_sem = refs[10:]
    cols = scaled.shape[0]
    pair = cols // 4
    fetch(joined_pieces(ins, joined), in_sem)()
    tags = joined[:, :ID_COLS].astype(F32).T
    places = tags[0:1, :] * ID_BASE + tags[1:2, :]
    chooser[...] = (positions[...] == places).astype(F32).astype(BF16)
    to_image_order(chooser, joined, ID_COLS, turned)
    own_s[...] = turned[:, :128]
    waits = [fetch([(own_s, own_turned), (chooser, chooser_out)], sem)]
    for p in range(4):
        here = slice(p * pair, (p + 1) * pair)
        turned[here, :] = turned[here, :] * scales[
            pl.ds(pl.multiple_of(order[p] * pair, 8), pair), :
        ]
        scaled_s[here, :] = turned[here, :].astype(BF16)
    split_parity(turned, core[0], 4, keep_s, give_s)
    waits.append(fetch([(give_s, give), (keep_s, keep), (scaled_s, scaled)], give_sem))
    for wait in waits:
        wait()


def route_first(core, order, scales, positions, ins):
    rows, cols = positions.shape[0], scales.shape[0] // 2
    turned = ((cols // 2, rows), BF16)
    outs = [((cols, rows), BF16), turned, turned, ((cols, 128), F32), ((rows, rows), BF16)]
    return pl.pallas_call(
        first_kernel,
        out_shape=[jax.ShapeDtypeStruct(shape, kind) for shape, kind in outs],
        in_specs=[SMEM, SMEM, VMEM, VMEM] + [HBM] * len(ins),
        out_specs=[HBM] * 5,
        scratch_shapes=[
            pltpu.VMEM((rows, cols + ID_COLS), BF16),
            pltpu.VMEM((cols, rows), F32),
            pltpu.VMEM((cols, rows), BF16),
            pltpu.VMEM((cols // 2, rows), BF16),
            pltpu.VMEM((cols // 2, rows), BF16),
            pltpu.VMEM((rows, rows), BF16),
            pltpu.VMEM((cols, 128), F32),
        ]
        + [pltpu.SemaphoreType.DMA((n,)) for n in (5, 2, 3)],
        compiler_params=params(52),
        cost_estimate=cost(10**9, 10**7),
    )(core, order, scales, positions, *ins)


def middle_kernel(core, order, *refs):
    scales, chooser_in, own_first, scaled_1, slope, down, up = refs[:7]
    ins, (keep, give, own_grad, pre, sums) = refs[7:12], refs[12:17]
    joined, turned, scaled, keep_s, give_s, chooser, own_s, own_rows, own_out = refs[17:26]
    slope_s, down_s, up_s, pre_s, sums_s, scales_s = refs[26:32]
    in_sem, s_sem, d_sem, u_sem, give_sem, own_sem, pre_sem, sum_sem = refs[32:]
    cols = joined.shape[1]
    pair = cols // 4
    got = fetch(
        joined_pieces(ins, joined)
        + [(chooser_in, chooser), (scales, scales_s), (own_first, own_s.at[0])],
        in_sem,
    )
    more = [(slope, slope_s)]
    for p in range(4):
        at = pl.ds(pl.multiple_of(order[p] * pair, 16), pair)
        more.append((scaled_1.at[p * pair : (p + 1) * pair], scaled.at[at]))
    got_more = fetch(more, s_sem)
    count = 2
    tile = down.shape[0] // count
    tiles = [slice(n * tile, (n + 1) * tile) for n in range(count)]
    got_down = [fetch([(down.at[rows], down_s.at[rows])], d_sem.at[n]) for n, rows in enumerate(tiles)]
    got_up = fetch([(up, up_s)], u_sem)
    got()
    to_image_order(chooser, joined, 0, turned)
    own_s[1] = turned[:, :128]
    got_more()
    for p in range(4):
        here = slice(p * pair, (p + 1) * pair)
        place = order[4 + p] * pair
        turned[here, :] = turned[here, :] * scales_s[pl.ds(pl.multiple_of(place, 8), pair), :]
        scaled[pl.ds(pl.multiple_of(place, 16), pair), :] = turned[here, :].astype(BF16)
    split_parity(turned, core[0], 4, keep_s, give_s)
    waits = [fetch([(give_s, give), (keep_s, keep)], give_sem)]
    for n, rows in enumerate(tiles):
        got_down[n]()
        value = jnp.dot(down_s[rows, :], scaled[...], preferred_element_type=F32)
        pre_s[rows, :] = (value * slope_s[rows, :].astype(F32)).astype(BF16)
        waits.append(fetch([(pre_s.at[rows], pre.at[rows])], pre_sem.at[n]))
    for p in range(8):
        at = pl.ds(pl.multiple_of(order[p] * pair, 8), pair)
        own_rows[at, :] = own_s[p // 4, (p % 4) * pair : (p % 4 + 1) * pair, :]
    for t in range(own_rows.shape[0] // 128):
        here = slice(t * 128, (t + 1) * 128)
        own_out[:, here] = own_rows[here, :].T[: own_out.shape[0]].astype(BF16)
    waits.append(fetch([(own_out, own_grad)], own_sem))
    got_up()
    width = sums.shape[1]
    for k, first in enumerate(range(0, width, 512)):
        here = slice(first, min(first + 512, width))
        sums_s[:, here] = lax.dot_general(
            pre_s[...], up_s[:, here], (((0,), (0,)), ((), ())), preferred_element_type=F32
        ).astype(BF16)
    waits.append(fetch([(sums_s, sums)], sum_sem))
    for wait in waits:
        wait()


def middle(core, order, scales, chooser, own_first, scaled_1, slope, down, up, ins):
    hidden, width = down.shape
    rows, cols = chooser.shape[0], width // 2
    turned = ((cols // 2, rows), BF16)
    outs = [turned, turned, ((rows // MEMBERS, width), BF16)]
    outs += [((hidden, rows), BF16), ((rows, width), BF16)]
    return pl.pallas_call(
        middle_kernel,
        out_shape=[jax.ShapeDtypeStruct(shape, kind) for shape, kind in outs],
        in_specs=[SMEM, SMEM] + [HBM] * (7 + len(ins)),
        out_specs=[HBM] * 5,
        scratch_shapes=[
            pltpu.VMEM((rows, cols), BF16),
            pltpu.VMEM((cols, rows), F32),
            pltpu.VMEM((width, rows), BF16),
            pltpu.VMEM((cols // 2, rows), BF16),
            pltpu.VMEM((cols // 2, rows), BF16),
            pltpu.VMEM((rows, rows), BF16),
            pltpu.VMEM((2, cols, 128), F32),
            pltpu.VMEM((width, 128), F32),
            pltpu.VMEM((rows // MEMBERS, width), BF16),
            pltpu.VMEM((hidden, rows), BF16),
            pltpu.VMEM((hidden, width), BF16),
            pltpu.VMEM((hidden, width), BF16),
            pltpu.VMEM((hidden, rows), BF16),
            pltpu.VMEM((rows, width), BF16),
            pltpu.VMEM((width, 1), F32),
        ]
        + [pltpu.SemaphoreType.DMA((n,)) for n in (8, 5)]
        + [pltpu.SemaphoreType.DMA((2, 1)), pltpu.SemaphoreType.DMA((1,))]
        + [pltpu.SemaphoreType.DMA((n,)) for n in (2, 1)]
        + [pltpu.SemaphoreType.DMA((2, 1)), pltpu.SemaphoreType.DMA((1,))],
        compiler_params=params(60),
        cost_estimate=cost(10**10, 10**7),
    )(core, order, scales, chooser, own_first, scaled_1, slope, down, up, *ins)


def blocks_kernel(jobs, *refs):
    group = 800
    count = len(jobs)
    ins, refs = refs[: 5 * count], refs[5 * count :]
    total = sum(len(sizes) for parts in jobs for _, _, sizes in parts)
    pieces = sum(len(parts) for parts in jobs)
    scratch = refs[-(3 * count + 3 * pieces) :]
    outs = refs[:total]
    todo = []
    at_out = at = 0
    for k, parts in enumerate(jobs):
        slots, left, left_got, right, right_got = ins[5 * k : 5 * k + 5]
        left_s, l_sem, r_sem = scratch[at : at + 3]
        at += 3
        rows_in = left.shape[1]
        waits_r = []
        each = []
        for i, (first, cols, sizes) in enumerate(parts):
            right_s, stage, sem = scratch[at : at + 3]
            at += 3
            here = slice(first, first + cols)
            waits_r.append(
                fetch(
                    [
                        (right.at[here], right_s.at[:cols, :rows_in]),
                        (right_got.at[here], right_s.at[:cols, rows_in:]),
                    ],
                    r_sem.at[i],
                )
            )
            each.append((i, cols, sizes, right_s, stage, sem, outs[at_out : at_out + len(sizes)]))
            at_out += len(sizes)
        waits_l = []
        for g in range(left.shape[0] // group):
            here = slice(g * group, (g + 1) * group)
            waits_l.append(
                fetch(
                    [
                        (left.at[here], left_s.at[here, :rows_in]),
                        (left_got.at[here], left_s.at[here, rows_in:]),
                    ],
                    l_sem.at[g],
                )
            )
        todo.append((slots, left_s, waits_l, waits_r, each))
    for slots, left_s, waits_l, waits_r, each in todo:
        for i, cols, sizes, right_s, stage, sem, targets in each:
            waits_r[i]()
            block = stage.shape[1]
            per = group // block
            for g in range(len(waits_l)):
                if i == 0:
                    waits_l[g]()
                product = by_last(left_s[g * group : (g + 1) * group, :], right_s[...])
                for b in range(per):
                    j = g * per + b
                    stage[j] = product[b * block : (b + 1) * block, :cols].astype(BF16)
                    slot = slots[i, j]
                    first = 0
                    for out, size in zip(targets, sizes):

                        @pl.when((slot >= first) & (slot < first + size))
                        def _(out=out, first=first, j=j, slot=slot, stage=stage, sem=sem):
                            pltpu.make_async_copy(
                                stage.at[j], out.at[slot - first], sem.at[j]
                            ).start()

                        first += size
    for _, _, _, _, each in todo:
        for _, _, _, _, stage, sem, targets in each:
            for j in range(stage.shape[0]):
                pltpu.make_async_copy(stage.at[j], targets[0].at[0], sem.at[j]).wait()


def grad_blocks(jobs):
    block = 200
    specs, ins, outs, scratch = [], [], [], []
    for slots, left, left_got, right, right_got, parts in jobs:
        width, rows = left.shape
        specs += [SMEM] + [HBM] * 4
        ins += [slots, left, left_got, right, right_got]
        scratch += [
            pltpu.VMEM((width, 2 * rows), BF16),
            pltpu.SemaphoreType.DMA((width // 800, 2)),
            pltpu.SemaphoreType.DMA((len(parts), 2)),
        ]
        for _, cols, sizes in parts:
            outs += [jax.ShapeDtypeStruct((size, block, cols), BF16) for size in sizes]
            scratch += [
                pltpu.VMEM((-(-cols // 256) * 256, 2 * rows), BF16),
                pltpu.VMEM((width // block, block, cols), BF16),
                pltpu.SemaphoreType.DMA((width // block,)),
            ]
    lists = [job[-1] for job in jobs]

    def kernel(*refs):
        blocks_kernel(lists, *refs)

    return pl.pallas_call(
        kernel,
        out_shape=outs,
        in_specs=specs,
        out_specs=[HBM] * len(outs),
        scratch_shapes=scratch,
        compiler_params=params(52),
        cost_estimate=cost(10**10, 10**7),
    )(*ins)


def z_order(z, xl):
    pairs = [(2, 0), (1, 1), (2, 1), (3, 0), (1, 0), (3, 1), (0, 0), (0, 1)]
    return [((z + dz) % Z) * XL + x for dz, x in pairs]


def x_order(z, xl):
    pairs = [(dz, dx) for dx in (1, 0) for dz in (2, 1, 3, 0)]
    return [((z + dz) % Z) * XL + (xl + dx) % XL for dz, dx in pairs]


def slots_of(order):
    order = jnp.stack(order).astype(jnp.int32)
    index = jnp.arange(order.shape[0], dtype=jnp.int32)
    return jnp.sum(jnp.where(order[None, :] == index[:, None], index[None, :], 0), 1)


def beside(*parts):
    return jnp.concatenate(parts, 1)


def below(*parts):
    return jnp.concatenate(parts, 0)


def on_device(
    lm_grad, encoder_row, patch_count, hidden_in, norm_gain, layer_scale, up_weight, down_weight
):
    tok_rows, width = hidden_in.shape
    rest = up_weight.shape[1] - CUT
    up_turned, down_turned = up_weight.T, down_weight.T
    group_len = tok_rows * MEMBERS
    per_pair = tok_rows // BLOCKS
    half = tok_rows // 2
    z, xl, core = lax.axis_index("z"), lax.axis_index("xl"), lax.axis_index("core")
    y, xh = lax.axis_index("y"), lax.axis_index("xh")
    group = (z * XL + xl) * CORE + core
    core_at = core.reshape(1).astype(jnp.int32)
    z_slots, x_slots = slots_of(z_order(z, xl)), slots_of(x_order(z, xl))

    inputs = hidden_in.astype(F32)
    inverse_rms = lax.rsqrt(jnp.mean(inputs * inputs, -1, keepdims=True) + 1e-06)
    normed_own = (inputs * inverse_rms * norm_gain).astype(BF16)

    n_prev = shift(normed_own, "y", Y, 1)
    n_next = shift(normed_own, "y", Y, -1)
    n_other = shift(normed_own, "xh", XH, 1)

    image, place = encoder_row // group_len, encoder_row % group_len
    index = jnp.arange(tok_rows, dtype=jnp.int32)
    same = (image[:, None] == image[None, :]) & (index[None, :] < index[:, None])
    slot = image * per_pair + jnp.sum(same.astype(jnp.int32), 1)
    sorter = (slot[None, :] == index[:, None]).astype(BF16)
    column = jnp.arange(ID_COLS, dtype=jnp.int32)[None, :]
    tags = jnp.where(
        column == 0,
        (place // ID_BASE)[:, None],
        jnp.where(column == 1, (place % ID_BASE)[:, None], 0),
    ).astype(BF16)
    ordered = jnp.dot(sorter, beside(lm_grad, tags), preferred_element_type=F32).astype(BF16)
    arrived = lax.all_to_all(
        ordered.reshape(BLOCKS, per_pair, width + ID_COLS),
        ("z", "xl", "core"),
        split_axis=0,
        concat_axis=0,
    ).reshape(tok_rows, width + ID_COLS)

    n_prev, n_next, n_other = together(n_prev, n_next, n_other)
    mix_prev = shift(below(n_other, n_prev[:half]), "y", Y, 1)
    mix_next = shift(below(n_other, n_next[half:]), "y", Y, -1)
    g_other = shift(arrived, "xh", XH, 1)
    mix_prev, mix_next, g_other, arrived = together(mix_prev, mix_next, g_other, arrived)

    far_a = shift(mix_prev[:half], "y", Y, 1)
    far_b = shift(mix_next[half:tok_rows], "y", Y, -1)
    order = jnp.stack(z_order(z, xl)).astype(jnp.int32)
    g_1, g_2 = prepare(order, arrived, g_other, width)
    far_a, far_b, g_1, g_2 = together(far_a, far_b, g_1, g_2)

    g_prev_1, g_next_1 = shift(g_1, "y", Y, 1), shift(g_1, "y", Y, -1)
    act, slope, n_keep, n_give = assemble_normed(
        core_at, (normed_own, n_other, n_next, n_prev, mix_prev, mix_next, far_a, far_b), up_turned
    )
    n_got = shift(n_give, "core", CORE, 1)
    act_got = shift(act, "core", CORE, 1)

    f_prev_1 = shift(g_prev_1[:tok_rows], "y", Y, 1)
    f_next_1 = shift(g_next_1[tok_rows:], "y", Y, -1)
    f_prev_1, f_next_1, g_2 = together(f_prev_1, f_next_1, g_2)
    g_prev_2, g_next_2 = shift(g_2, "y", Y, 1), shift(g_2, "y", Y, -1)

    block = jnp.arange(MEMBERS, dtype=jnp.int32)
    member = ((block // XH + y) % Y) * XH + (block % XH + xh) % XH
    positions = (member[:, None] * tok_rows + index[None, :]).reshape(group_len, 1)
    limit = lax.dynamic_index_in_dim(patch_count, group, 0, keepdims=False)
    positions = jnp.where(positions < limit, positions, -1).astype(F32)
    scale_column = layer_scale.reshape(width, 1)
    f_prev_1, n_got, act_got = together(f_prev_1, n_got, act_got)
    s_1, d_keep_1, d_give_1, own_first, chooser = route_first(
        core_at, order, scale_column, positions, (g_1, g_prev_1, g_next_1, f_prev_1, f_next_1)
    )
    d_got_1 = shift(d_give_1, "core", CORE, 1)

    g_prev_2, g_next_2, d_got_1 = together(g_prev_2, g_next_2, d_got_1)
    f_prev_2 = shift(g_prev_2[:tok_rows], "y", Y, 1)
    f_next_2 = shift(g_next_2[tok_rows:], "y", Y, -1)
    here = xl == 0
    straight = jnp.arange(4, dtype=jnp.int32)
    slots_1 = jnp.stack([straight, jnp.where(here, jnp.array([2, 1, 0, 3]), jnp.array([0, 3, 2, 1]))])
    slots_2 = jnp.stack([straight, jnp.where(here, jnp.array([2, 0, 3, 1]), jnp.array([0, 2, 1, 3]))])
    slots_1, slots_2 = slots_1.astype(jnp.int32), slots_2.astype(jnp.int32)
    d_up, d_down, d_out_1, d_mine_1 = grad_blocks(
        [(slots_1, d_keep_1, d_got_1, act, act_got, ((0, CUT, (2, 2)), (CUT, rest, (2, 2))))]
    )
    d_prev, d_next = shift(d_up, "z", Z, 1), shift(d_down, "z", Z, -1)
    d_x_1 = shift(d_out_1, "xl", XL, 1)
    f_prev_2, f_next_2, d_mine_1 = together(f_prev_2, f_next_2, d_mine_1)

    d_keep_2, d_give_2, own_grad, pre, parts = middle(
        core_at, order, scale_column, chooser, own_first, s_1, slope, down_turned, up_turned,
        (g_2, g_prev_2, g_next_2, f_prev_2, f_next_2),
    )
    pre_got = shift(pre, "core", CORE, 1)
    d_got_2 = shift(d_give_2, "core", CORE, 1)
    blocks = parts.reshape(MEMBERS, tok_rows, width)
    p_prev = shift(below(blocks[4][:half], blocks[5][:half]), "y", Y, 1)
    p_next = shift(below(blocks[4][half:], blocks[5][half:]), "y", Y, -1)
    pre_got, d_got_2, d_prev, d_next, d_x_1 = together(pre_got, d_got_2, d_prev, d_next, d_x_1)
    d_kept, d_out_2, d_mine_2, u_up, u_down, u_kept, u_out, u_mine = grad_blocks(
        [
            (slots_2, d_keep_2, d_got_2, act, act_got, ((0, CUT, (4,)), (CUT, rest, (2, 2)))),
            (
                jnp.stack([z_slots, x_slots]), n_keep, n_got, pre, pre_got,
                ((0, CUT, (2, 2, 4)), (CUT, rest, (4, 4))),
            ),
        ]
    )

    u_prev, u_next = shift(u_up, "z", Z, 1), shift(u_down, "z", Z, -1)
    d_x_2 = shift(d_out_2, "xl", XL, 1)
    p_prev, p_next, u_mine = together(p_prev, p_next, u_mine)
    o_prev = shift(below(add(blocks[3][:half], p_prev[half:]), blocks[3][half:]), "y", Y, 1)
    o_next = shift(below(blocks[7][:half], add(blocks[7][half:], p_next[half:])), "y", Y, -1)
    o_prev, o_next, d_x_2 = together(o_prev, o_next, d_x_2)
    u_x = shift(u_out, "xl", XL, 1)
    r_other = shift(add(blocks[1], o_prev, o_next), "xh", XH, 1)
    r_prev = shift(below(add(blocks[2][:half], p_prev[:half]), blocks[2][half:]), "y", Y, 1)
    r_next = shift(below(blocks[6][:half], add(blocks[6][half:], p_next[:half])), "y", Y, -1)
    u_prev, u_next, r_prev, r_next = together(u_prev, u_next, r_prev, r_next)

    cut = -(-d_x_1.shape[1] // 16) * 8
    two, side_1, side_2 = (
        add(d_mine_1[0], d_x_1[0]), add(d_mine_1[1], d_x_1[1]), add(d_mine_2[0], d_x_2[0])
    )
    one, three = jnp.where(here, side_2, side_1), jnp.where(here, side_1, side_2)
    d_here = add32(d_mine_2[1], d_x_2[1])
    d_b_one, d_b_three = one[:cut], three[cut:]
    u_acc_prev = shift(add(u_kept[0], u_prev[0]), "z", Z, 1)
    u_acc_next = shift(add(u_kept[1], u_next[0]), "z", Z, -1)
    to_next = beside(add(d_kept[0], d_prev[0]), below(two[:cut], one[cut:]))
    to_prev = beside(add(d_kept[1], d_next[0]), below(three[:cut], two[cut:]))
    m_prev, m_next = shift(to_next, "z", Z, 1), shift(to_prev, "z", Z, -1)
    u_acc_prev, u_acc_next, u_x, r_other = together(u_acc_prev, u_acc_next, u_x, r_other)

    sum_0 = add(u_kept[2], u_next[1], u_acc_prev)
    sum_1 = add(u_kept[3], u_prev[1], u_acc_next)
    u_own = jnp.where(here, sum_0, sum_1)
    u_other = shift(jnp.where(here, sum_1, sum_0), "xl", XL, 1)
    m_prev, m_next, u_own = together(m_prev, m_next, u_own)
    d_acc_prev, d_b_prev = m_prev[:, :CUT], m_prev[:, CUT:]
    d_acc_next, d_b_next = m_next[:, :CUT], m_next[:, CUT:]
    sum_0 = add(d_kept[2], d_next[1], d_acc_prev)
    sum_1 = add(d_kept[3], d_prev[1], d_acc_next)
    d_own = jnp.where(here, sum_0, sum_1)
    d_other = shift(jnp.where(here, sum_1, sum_0), "xl", XL, 1)
    two, one, three = (add(u_mine[i], u_x[i]) for i in range(3))
    u_here = add32(u_mine[3], u_x[3])
    b_prev = shift(
        below(add(d_b_one, d_b_prev[:cut]), two[:cut], one[cut:]), "z", Z, 1
    )
    b_next = shift(
        below(add(d_b_three, d_b_next[cut:]), three[:cut], two[cut:]), "z", Z, -1
    )
    tail = d_here.shape[0] - cut
    u_b_prev, u_b_next = b_prev[cut:], b_next[tail:]
    c_prev = shift(add(one[:cut], u_b_prev[:cut]), "z", Z, 1)
    c_next = shift(add(three[cut:], u_b_next[cut:]), "z", Z, -1)
    down_a, up_a = add32(d_own, d_other), add32(u_own, u_other)
    down_b = below(
        add32(d_here[:cut], d_b_next[:cut], b_prev[:cut]),
        add32(d_here[cut:], d_b_prev[cut:], b_next[:tail]),
    )
    up_b = below(
        add32(u_here[:cut], u_b_next[:cut], c_prev),
        add32(u_here[cut:], u_b_prev[cut:], c_next),
    )
    normed_grad = add32(blocks[0], r_prev, r_next, r_other)
    weighted = norm_gain * normed_grad
    input_grad = (
        own_grad.astype(F32)
        + inverse_rms * weighted
        - inputs * inverse_rms**3 * jnp.mean(weighted * inputs, -1, keepdims=True)
    ).astype(BF16)
    grad_scale = 1.0 / math.sqrt(group_len * BLOCKS)
    return (
        input_grad,
        (beside(up_a, up_b) * grad_scale).astype(BF16),
        (beside(down_a, down_b) * grad_scale).astype(BF16),
    )


def solution(mesh):
    fine = Mesh(mesh.devices.reshape(Z, XL, CORE, Y, XH), AXES)
    dp, tensor = AXES[:3], AXES[3:]
    in_specs = (
        P(AXES, None),
        P(AXES),
        P(),
        P(AXES, None),
        P(),
        P(),
        P(None, tensor),
        P(None, tensor),
    )
    out_specs = (P(AXES, None), P(dp, tensor), P(dp, tensor))
    return jax.shard_map(
        on_device, mesh=fine, in_specs=in_specs, out_specs=out_specs, check_vma=False
    )
```

```python
import math

import jax
import jax.numpy as jnp
from jax import lax
from jax.experimental import pallas as pl
from jax.experimental.pallas import tpu as pltpu
from jax.sharding import Mesh, PartitionSpec as P

F32 = jnp.float32
BF16 = jnp.bfloat16
Z, XL, CORE, Y, XH = 4, 2, 2, 4, 2
AXES = ("z", "xl", "core", "y", "xh")
MEMBERS = Y * XH
BLOCKS = Z * XL * CORE
ID_COLS = 128
ID_BASE = 32
CUT = 1152
MIB = 1024 * 1024
VMEM = pl.BlockSpec(memory_space=pltpu.VMEM)
SMEM = pl.BlockSpec(memory_space=pltpu.SMEM)
ANY = pl.BlockSpec(memory_space=pl.ANY)
HBM = pl.BlockSpec(memory_space=pltpu.HBM)


def params(mib):
    return pltpu.CompilerParams(vmem_limit_bytes=mib * MIB)


def cost(flops, moved, special=0):
    return pl.CostEstimate(flops=flops, bytes_accessed=moved, transcendentals=special)


def shift(value, axis, size, step):
    return lax.ppermute(value, axis, [(i, (i + step) % size) for i in range(size)])


def add32(*terms):
    total = terms[0].astype(F32)
    for term in terms[1:]:
        total = total + term.astype(F32)
    return total


def add(*terms):
    return add32(*terms).astype(BF16)


def together(*values):
    return lax.optimization_barrier(values)


def fetch(pieces, sem):
    copies = [pltpu.make_async_copy(src, dst, sem.at[i]) for i, (src, dst) in enumerate(pieces)]
    for copy in copies:
        copy.start()

    def wait():
        for copy in copies:
            copy.wait()

    return wait


def pieces_of(listed, out):
    at, pieces = 0, []
    for ref, first, rows in listed:
        pieces.append((ref.at[first : first + rows], out.at[at : at + rows]))
        at += rows
    return pieces


def split_parity(turned, core, pairs, keep, give):
    rows = keep.shape[0] // pairs
    for two in range(pairs // 2):
        for out, parity in ((keep, core), (give, 1 - core)):
            blocks = [
                turned[pl.ds(pl.multiple_of((2 * b + parity) * rows, 8), rows), :]
                for b in (2 * two, 2 * two + 1)
            ]
            out[2 * two * rows : (2 * two + 2) * rows, :] = jnp.concatenate(blocks, 0).astype(BF16)


def by_last(left, right):
    return lax.dot_general(left, right, (((1,), (1,)), ((), ())), preferred_element_type=F32)


def normed_kernel(core, *refs):
    ins, weight, (act, slope, keep, give) = refs[:8], refs[8], refs[9:13]
    normed, turned, held, act_s, slope_s, keep_s, give_s, in_sem, w_sem, out_sem, sem = refs[13:]
    own, other, nxt, prev, mix_prev, mix_next, far_a, far_b = ins
    full = own.shape[0]
    half = full // 2
    listed = [(own, 0, full), (other, 0, full), (nxt, 0, full), (mix_next, 0, full)]
    listed += [(mix_prev, full, half), (mix_next, full, half), (far_a, 0, half), (far_b, 0, half)]
    listed += [(prev, 0, full), (mix_prev, 0, full)]
    fetched = fetch(pieces_of(listed, normed), in_sem)
    tile = held.shape[1]
    count = held.shape[0]
    tiles = [slice(n * tile, (n + 1) * tile) for n in range(count)]
    weights = [fetch([(weight.at[tiles[n]], held.at[n])], w_sem.at[n]) for n in range(count)]
    fetched()
    for t in range(normed.shape[1] // 128):
        cols = slice(t * 128, (t + 1) * 128)
        turned[cols, :] = normed[:, cols].astype(F32).T
    split_parity(turned, core[0], BLOCKS // 2, keep_s, give_s)
    waits = [fetch([(give_s, give), (keep_s, keep)], out_sem)]
    for n, rows in enumerate(tiles):
        weights[n]()
        value = by_last(held[n], normed[...])
        below = 0.5 * (1.0 + lax.erf(value * 0.7071067811865476))
        act_s[rows, :] = (value * below).astype(BF16)
        slope_s[rows, :] = (
            below + value * jnp.exp(-0.5 * value * value) * 0.3989422804014327
        ).astype(BF16)
        waits.append(
            fetch([(act_s.at[rows], act.at[rows]), (slope_s.at[rows], slope.at[rows])], sem.at[n])
        )
    for wait in waits:
        wait()


def assemble_normed(core, ins, weight):
    rows, width = ins[0].shape[0] * MEMBERS, ins[0].shape[1]
    hidden = weight.shape[0]
    count = 4
    outs = [((hidden, rows), BF16)] * 2 + [((width // 2, rows), BF16)] * 2
    return pl.pallas_call(
        normed_kernel,
        out_shape=[jax.ShapeDtypeStruct(shape, kind) for shape, kind in outs],
        in_specs=[SMEM] + [HBM] * (len(ins) + 1),
        out_specs=[HBM] * 4,
        scratch_shapes=[
            pltpu.VMEM((rows, width), BF16),
            pltpu.VMEM((width, rows), F32),
            pltpu.VMEM((count, hidden // count, width), BF16),
        ]
        + [pltpu.VMEM(shape, kind) for shape, kind in outs]
        + [pltpu.SemaphoreType.DMA((n,)) for n in (10,)]
        + [pltpu.SemaphoreType.DMA((count, 1)), pltpu.SemaphoreType.DMA((2,))]
        + [pltpu.SemaphoreType.DMA((count, 2))],
        compiler_params=params(52),
        cost_estimate=cost(10**10, 10**7),
    )(core, *ins, weight)


def prepare_kernel(order, own, other, first, second, rows_s, turned, sorted_s, *refs):
    outs_s, in_sem, sem = refs[:2], refs[2], refs[3]
    half = own.shape[0] // 2
    listed = [(own, 0, half), (other, 0, half), (own, half, half), (other, half, half)]
    fetch(pieces_of(listed, rows_s), in_sem)()
    width = turned.shape[0]
    pair = width // (BLOCKS // 2)
    for t in range(width // 128):
        cols = slice(t * 128, (t + 1) * 128)
        turned[cols, :] = rows_s[:, cols].astype(F32).T
    waits = []
    for h, out in enumerate((first, second)):
        for p in range(4):
            at = pl.ds(pl.multiple_of(order[4 * h + p] * pair, 8), pair)
            sorted_s[p * pair : (p + 1) * pair, :] = turned[at, :]
        cols = width // 2
        lead = 0 if h else ID_COLS
        for first_col in range(0, cols, 128):
            last = min(first_col + 128, cols)
            outs_s[h][:, lead + first_col : lead + last] = (
                sorted_s[first_col : first_col + 128, :].T[:, : last - first_col].astype(BF16)
            )
        if h == 0:
            outs_s[h][:, :lead] = rows_s[:, width : width + ID_COLS]
        waits.append(fetch([(outs_s[h], out)], sem.at[h]))
    for wait in waits:
        wait()


def prepare(order, own, other, width):
    rows = 2 * own.shape[0]
    cols = width // 2
    return pl.pallas_call(
        prepare_kernel,
        out_shape=[
            jax.ShapeDtypeStruct((rows, cols + ID_COLS), BF16),
            jax.ShapeDtypeStruct((rows, cols), BF16),
        ],
        in_specs=[SMEM, HBM, HBM],
        out_specs=[HBM, HBM],
        scratch_shapes=[
            pltpu.VMEM((rows, width + ID_COLS), BF16),
            pltpu.VMEM((width, rows), F32),
            pltpu.VMEM((-(-cols // 128) * 128, rows), F32),
            pltpu.VMEM((rows, cols + ID_COLS), BF16),
            pltpu.VMEM((rows, cols), BF16),
            pltpu.SemaphoreType.DMA((4,)),
            pltpu.SemaphoreType.DMA((2, 1)),
        ],
        compiler_params=params(52),
        cost_estimate=cost(10**8, 10**6),
    )(order, own, other)


def joined_pieces(ins, joined):
    at, pieces = 0, []
    for ref in ins:
        rows = ref.shape[0]
        pieces.append((ref, joined.at[at : at + rows]))
        at += rows
    return pieces


def to_image_order(chooser, joined, lead, turned):
    cols = turned.shape[0]
    for first in range(0, cols, 640):
        last = min(first + 640, cols)
        grads = jnp.dot(
            chooser[...], joined[:, lead + first : lead + last], preferred_element_type=F32
        )
        turned[first:last, :] = grads.T


def first_kernel(core, order, scales, positions, *refs):
    ins, (scaled, keep, give, own_turned, chooser_out) = refs[:5], refs[5:10]
    joined, turned, scaled_s, keep_s, give_s, chooser, own_s, in_sem, sem, give_sem = refs[10:]
    cols = scaled.shape[0]
    pair = cols // 4
    fetch(joined_pieces(ins, joined), in_sem)()
    tags = joined[:, :ID_COLS].astype(F32).T
    places = tags[0:1, :] * ID_BASE + tags[1:2, :]
    chooser[...] = (positions[...] == places).astype(F32).astype(BF16)
    to_image_order(chooser, joined, ID_COLS, turned)
    own_s[...] = turned[:, :128]
    waits = [fetch([(own_s, own_turned), (chooser, chooser_out)], sem)]
    for p in range(4):
        here = slice(p * pair, (p + 1) * pair)
        turned[here, :] = turned[here, :] * scales[
            pl.ds(pl.multiple_of(order[p] * pair, 8), pair), :
        ]
        scaled_s[here, :] = turned[here, :].astype(BF16)
    split_parity(turned, core[0], 4, keep_s, give_s)
    waits.append(fetch([(give_s, give), (keep_s, keep), (scaled_s, scaled)], give_sem))
    for wait in waits:
        wait()


def route_first(core, order, scales, positions, ins):
    rows, cols = positions.shape[0], scales.shape[0] // 2
    turned = ((cols // 2, rows), BF16)
    outs = [((cols, rows), BF16), turned, turned, ((cols, 128), F32), ((rows, rows), BF16)]
    return pl.pallas_call(
        first_kernel,
        out_shape=[jax.ShapeDtypeStruct(shape, kind) for shape, kind in outs],
        in_specs=[SMEM, SMEM, VMEM, VMEM] + [HBM] * len(ins),
        out_specs=[HBM] * 5,
        scratch_shapes=[
            pltpu.VMEM((rows, cols + ID_COLS), BF16),
            pltpu.VMEM((cols, rows), F32),
            pltpu.VMEM((cols, rows), BF16),
            pltpu.VMEM((cols // 2, rows), BF16),
            pltpu.VMEM((cols // 2, rows), BF16),
            pltpu.VMEM((rows, rows), BF16),
            pltpu.VMEM((cols, 128), F32),
        ]
        + [pltpu.SemaphoreType.DMA((n,)) for n in (5, 2, 3)],
        compiler_params=params(52),
        cost_estimate=cost(10**9, 10**7),
    )(core, order, scales, positions, *ins)


def middle_kernel(core, order, *refs):
    scales, chooser_in, own_first, scaled_1, slope, down = refs[:6]
    ins, (keep, give, own_grad, pre) = refs[6:11], refs[11:15]
    joined, turned, scaled, keep_s, give_s, chooser, own_s, own_rows, own_out = refs[15:24]
    slope_s, down_s, pre_s, scales_s = refs[24:28]
    in_sem, s_sem, d_sem, give_sem, own_sem, pre_sem = refs[28:]
    cols = joined.shape[1]
    pair = cols // 4
    got = fetch(
        joined_pieces(ins, joined)
        + [(chooser_in, chooser), (scales, scales_s), (own_first, own_s.at[0])],
        in_sem,
    )
    more = [(slope, slope_s)]
    for p in range(4):
        at = pl.ds(pl.multiple_of(order[p] * pair, 16), pair)
        more.append((scaled_1.at[p * pair : (p + 1) * pair], scaled.at[at]))
    got_more = fetch(more, s_sem)
    count = 2
    tile = down.shape[0] // count
    tiles = [slice(n * tile, (n + 1) * tile) for n in range(count)]
    got_down = [fetch([(down.at[rows], down_s.at[rows])], d_sem.at[n]) for n, rows in enumerate(tiles)]
    got()
    to_image_order(chooser, joined, 0, turned)
    own_s[1] = turned[:, :128]
    got_more()
    for p in range(4):
        here = slice(p * pair, (p + 1) * pair)
        place = order[4 + p] * pair
        turned[here, :] = turned[here, :] * scales_s[pl.ds(pl.multiple_of(place, 8), pair), :]
        scaled[pl.ds(pl.multiple_of(place, 16), pair), :] = turned[here, :].astype(BF16)
    split_parity(turned, core[0], 4, keep_s, give_s)
    waits = [fetch([(give_s, give), (keep_s, keep)], give_sem)]
    for n, rows in enumerate(tiles):
        got_down[n]()
        value = jnp.dot(down_s[rows, :], scaled[...], preferred_element_type=F32)
        pre_s[rows, :] = (value * slope_s[rows, :].astype(F32)).astype(BF16)
        waits.append(fetch([(pre_s.at[rows], pre.at[rows])], pre_sem.at[n]))
    for p in range(8):
        at = pl.ds(pl.multiple_of(order[p] * pair, 8), pair)
        own_rows[at, :] = own_s[p // 4, (p % 4) * pair : (p % 4 + 1) * pair, :]
    for t in range(own_rows.shape[0] // 128):
        here = slice(t * 128, (t + 1) * 128)
        own_out[:, here] = own_rows[here, :].T[: own_out.shape[0]].astype(BF16)
    waits.append(fetch([(own_out, own_grad)], own_sem))
    for wait in waits:
        wait()


def middle(core, order, scales, chooser, own_first, scaled_1, slope, down, ins):
    hidden, width = down.shape
    rows, cols = chooser.shape[0], width // 2
    turned = ((cols // 2, rows), BF16)
    outs = [turned, turned, ((rows // MEMBERS, width), BF16), ((hidden, rows), BF16)]
    return pl.pallas_call(
        middle_kernel,
        out_shape=[jax.ShapeDtypeStruct(shape, kind) for shape, kind in outs],
        in_specs=[SMEM, SMEM] + [HBM] * (6 + len(ins)),
        out_specs=[HBM] * 4,
        scratch_shapes=[
            pltpu.VMEM((rows, cols), BF16),
            pltpu.VMEM((cols, rows), F32),
            pltpu.VMEM((width, rows), BF16),
            pltpu.VMEM((cols // 2, rows), BF16),
            pltpu.VMEM((cols // 2, rows), BF16),
            pltpu.VMEM((rows, rows), BF16),
            pltpu.VMEM((2, cols, 128), F32),
            pltpu.VMEM((width, 128), F32),
            pltpu.VMEM((rows // MEMBERS, width), BF16),
            pltpu.VMEM((hidden, rows), BF16),
            pltpu.VMEM((hidden, width), BF16),
            pltpu.VMEM((hidden, rows), BF16),
            pltpu.VMEM((width, 1), F32),
        ]
        + [pltpu.SemaphoreType.DMA((n,)) for n in (8, 5)]
        + [pltpu.SemaphoreType.DMA((2, 1))]
        + [pltpu.SemaphoreType.DMA((n,)) for n in (2, 1)]
        + [pltpu.SemaphoreType.DMA((2, 1))],
        compiler_params=params(52),
        cost_estimate=cost(10**10, 10**7),
    )(core, order, scales, chooser, own_first, scaled_1, slope, down, *ins)


def blocks_kernel(jobs, sums, *refs):
    group = 800
    count = len(jobs)
    if sums:
        refs, (pre_s, up_s, sums_s, up_sem, sums_sem) = refs[:-5], refs[-5:]
        pre, up = refs[5 * count : 5 * count + 2]
        refs = refs[: 5 * count] + refs[5 * count + 2 :]
    ins, refs = refs[: 5 * count], refs[5 * count :]
    total = sum(len(sizes) for parts in jobs for _, _, sizes in parts)
    pieces = sum(len(parts) for parts in jobs)
    scratch = refs[-(3 * count + 3 * pieces) :]
    outs, sums_out = refs[:total], refs[total] if sums else None
    todo = []
    at_out = at = 0
    for k, parts in enumerate(jobs):
        slots, left, left_got, right, right_got = ins[5 * k : 5 * k + 5]
        left_s, l_sem, r_sem = scratch[at : at + 3]
        at += 3
        rows_in = left.shape[1]
        waits_r = []
        each = []
        for i, (first, cols, sizes) in enumerate(parts):
            right_s, stage, sem = scratch[at : at + 3]
            at += 3
            here = slice(first, first + cols)
            waits_r.append(
                fetch(
                    [
                        (right.at[here], right_s.at[:cols, :rows_in]),
                        (right_got.at[here], right_s.at[:cols, rows_in:]),
                    ],
                    r_sem.at[i],
                )
            )
            each.append((i, cols, sizes, right_s, stage, sem, outs[at_out : at_out + len(sizes)]))
            at_out += len(sizes)
        waits_l = []
        for g in range(left.shape[0] // group):
            here = slice(g * group, (g + 1) * group)
            waits_l.append(
                fetch(
                    [
                        (left.at[here], left_s.at[here, :rows_in]),
                        (left_got.at[here], left_s.at[here, rows_in:]),
                    ],
                    l_sem.at[g],
                )
            )
        todo.append((slots, left_s, waits_l, waits_r, each))
    if sums:
        got_up = fetch([(pre, pre_s), (up, up_s)], up_sem)
    for slots, left_s, waits_l, waits_r, each in todo:
        for i, cols, sizes, right_s, stage, sem, targets in each:
            waits_r[i]()
            block = stage.shape[1]
            per = group // block
            for g in range(len(waits_l)):
                if i == 0:
                    waits_l[g]()
                product = by_last(left_s[g * group : (g + 1) * group, :], right_s[...])
                for b in range(per):
                    j = g * per + b
                    stage[j] = product[b * block : (b + 1) * block, :cols].astype(BF16)
                    slot = slots[i, j]
                    first = 0
                    for out, size in zip(targets, sizes):

                        @pl.when((slot >= first) & (slot < first + size))
                        def _(out=out, first=first, j=j, slot=slot, stage=stage, sem=sem):
                            pltpu.make_async_copy(
                                stage.at[j], out.at[slot - first], sem.at[j]
                            ).start()

                        first += size
    if sums:
        got_up()
        for first in range(0, up.shape[1], 512):
            here = slice(first, min(first + 512, up.shape[1]))
            sums_s[:, here] = lax.dot_general(
                pre_s[...], up_s[:, here], (((0,), (0,)), ((), ())), preferred_element_type=F32
            ).astype(BF16)
        fetch([(sums_s, sums_out)], sums_sem)()
    for _, _, _, _, each in todo:
        for _, _, _, _, stage, sem, targets in each:
            for j in range(stage.shape[0]):
                pltpu.make_async_copy(stage.at[j], targets[0].at[0], sem.at[j]).wait()


def grad_blocks(jobs, sums=()):
    block = 200
    specs, ins, outs, scratch = [], [], [], []
    for slots, left, left_got, right, right_got, parts in jobs:
        width, rows = left.shape
        specs += [SMEM] + [HBM] * 4
        ins += [slots, left, left_got, right, right_got]
        scratch += [
            pltpu.VMEM((width, 2 * rows), BF16),
            pltpu.SemaphoreType.DMA((width // 800, 2)),
            pltpu.SemaphoreType.DMA((len(parts), 2)),
        ]
        for _, cols, sizes in parts:
            outs += [jax.ShapeDtypeStruct((size, block, cols), BF16) for size in sizes]
            scratch += [
                pltpu.VMEM((-(-cols // 256) * 256, 2 * rows), BF16),
                pltpu.VMEM((width // block, block, cols), BF16),
                pltpu.SemaphoreType.DMA((width // block,)),
            ]
    lists = [job[-1] for job in jobs]
    if sums:
        (hidden, rows), width = sums[0].shape, sums[1].shape[1]
        specs += [HBM] * 2
        ins += list(sums)
        outs.append(jax.ShapeDtypeStruct((rows, width), BF16))
        scratch += [
            pltpu.VMEM((hidden, rows), BF16),
            pltpu.VMEM((hidden, width), BF16),
            pltpu.VMEM((rows, width), BF16),
            pltpu.SemaphoreType.DMA((2,)),
            pltpu.SemaphoreType.DMA((1,)),
        ]

    def kernel(*refs):
        blocks_kernel(lists, bool(sums), *refs)

    return pl.pallas_call(
        kernel,
        out_shape=outs,
        in_specs=specs,
        out_specs=[HBM] * len(outs),
        scratch_shapes=scratch,
        compiler_params=params(52),
        cost_estimate=cost(10**10, 10**7),
    )(*ins)


def z_order(z, xl):
    pairs = [(2, 0), (1, 1), (2, 1), (3, 0), (1, 0), (3, 1), (0, 0), (0, 1)]
    return [((z + dz) % Z) * XL + x for dz, x in pairs]


def x_order(z, xl):
    pairs = [(dz, dx) for dx in (1, 0) for dz in (2, 1, 3, 0)]
    return [((z + dz) % Z) * XL + (xl + dx) % XL for dz, dx in pairs]


def slots_of(order):
    order = jnp.stack(order).astype(jnp.int32)
    index = jnp.arange(order.shape[0], dtype=jnp.int32)
    return jnp.sum(jnp.where(order[None, :] == index[:, None], index[None, :], 0), 1)


def beside(*parts):
    return jnp.concatenate(parts, 1)


def below(*parts):
    return jnp.concatenate(parts, 0)


def on_device(
    lm_grad, encoder_row, patch_count, hidden_in, norm_gain, layer_scale, up_weight, down_weight
):
    tok_rows, width = hidden_in.shape
    rest = up_weight.shape[1] - CUT
    up_turned, down_turned = up_weight.T, down_weight.T
    group_len = tok_rows * MEMBERS
    per_pair = tok_rows // BLOCKS
    half = tok_rows // 2
    z, xl, core = lax.axis_index("z"), lax.axis_index("xl"), lax.axis_index("core")
    y, xh = lax.axis_index("y"), lax.axis_index("xh")
    group = (z * XL + xl) * CORE + core
    core_at = core.reshape(1).astype(jnp.int32)
    z_slots, x_slots = slots_of(z_order(z, xl)), slots_of(x_order(z, xl))

    inputs = hidden_in.astype(F32)
    inverse_rms = lax.rsqrt(jnp.mean(inputs * inputs, -1, keepdims=True) + 1e-06)
    normed_own = (inputs * inverse_rms * norm_gain).astype(BF16)

    n_prev = shift(normed_own, "y", Y, 1)
    n_next = shift(normed_own, "y", Y, -1)
    n_other = shift(normed_own, "xh", XH, 1)

    image, place = encoder_row // group_len, encoder_row % group_len
    index = jnp.arange(tok_rows, dtype=jnp.int32)
    same = (image[:, None] == image[None, :]) & (index[None, :] < index[:, None])
    slot = image * per_pair + jnp.sum(same.astype(jnp.int32), 1)
    sorter = (slot[None, :] == index[:, None]).astype(BF16)
    column = jnp.arange(ID_COLS, dtype=jnp.int32)[None, :]
    tags = jnp.where(
        column == 0,
        (place // ID_BASE)[:, None],
        jnp.where(column == 1, (place % ID_BASE)[:, None], 0),
    ).astype(BF16)
    ordered = jnp.dot(sorter, beside(lm_grad, tags), preferred_element_type=F32).astype(BF16)
    arrived = lax.all_to_all(
        ordered.reshape(BLOCKS, per_pair, width + ID_COLS),
        ("z", "xl", "core"),
        split_axis=0,
        concat_axis=0,
    ).reshape(tok_rows, width + ID_COLS)

    n_prev, n_next, n_other = together(n_prev, n_next, n_other)
    mix_prev = shift(below(n_other, n_prev[:half]), "y", Y, 1)
    mix_next = shift(below(n_other, n_next[half:]), "y", Y, -1)
    g_other = shift(arrived, "xh", XH, 1)
    mix_prev, mix_next, g_other, arrived = together(mix_prev, mix_next, g_other, arrived)

    far_a = shift(mix_prev[:half], "y", Y, 1)
    far_b = shift(mix_next[half:tok_rows], "y", Y, -1)
    order = jnp.stack(z_order(z, xl)).astype(jnp.int32)
    g_1, g_2 = prepare(order, arrived, g_other, width)
    far_a, far_b, g_1, g_2 = together(far_a, far_b, g_1, g_2)

    g_prev_1, g_next_1 = shift(g_1, "y", Y, 1), shift(g_1, "y", Y, -1)
    g_prev_2, g_next_2 = shift(g_2, "y", Y, 1), shift(g_2, "y", Y, -1)
    act, slope, n_keep, n_give = assemble_normed(
        core_at, (normed_own, n_other, n_next, n_prev, mix_prev, mix_next, far_a, far_b), up_turned
    )
    g_prev_1, g_next_1, g_prev_2, g_next_2, act, n_give = together(
        g_prev_1, g_next_1, g_prev_2, g_next_2, act, n_give
    )

    f_prev_1 = shift(g_prev_1[:tok_rows], "y", Y, 1)
    f_next_1 = shift(g_next_1[tok_rows:], "y", Y, -1)
    f_prev_2 = shift(g_prev_2[:tok_rows], "y", Y, 1)
    f_next_2 = shift(g_next_2[tok_rows:], "y", Y, -1)
    act_got = shift(act, "core", CORE, 1)

    block = jnp.arange(MEMBERS, dtype=jnp.int32)
    member = ((block // XH + y) % Y) * XH + (block % XH + xh) % XH
    positions = (member[:, None] * tok_rows + index[None, :]).reshape(group_len, 1)
    limit = lax.dynamic_index_in_dim(patch_count, group, 0, keepdims=False)
    positions = jnp.where(positions < limit, positions, -1).astype(F32)
    scale_column = layer_scale.reshape(width, 1)
    f_prev_1, f_next_1, act_got, n_give = together(f_prev_1, f_next_1, act_got, n_give)
    s_1, d_keep_1, d_give_1, own_first, chooser = route_first(
        core_at, order, scale_column, positions, (g_1, g_prev_1, g_next_1, f_prev_1, f_next_1)
    )
    d_got_1 = shift(d_give_1, "core", CORE, 1)
    here = xl == 0
    straight = jnp.arange(4, dtype=jnp.int32)
    slots_1 = jnp.stack([straight, jnp.where(here, jnp.array([2, 1, 0, 3]), jnp.array([0, 3, 2, 1]))])
    slots_2 = jnp.stack([straight, jnp.where(here, jnp.array([2, 0, 3, 1]), jnp.array([0, 2, 1, 3]))])
    slots_1, slots_2 = slots_1.astype(jnp.int32), slots_2.astype(jnp.int32)
    d_got_1, f_prev_2, f_next_2, n_give = together(d_got_1, f_prev_2, f_next_2, n_give)
    d_up, d_down, d_out_1, d_mine_1 = grad_blocks(
        [(slots_1, d_keep_1, d_got_1, act, act_got, ((0, CUT, (2, 2)), (CUT, rest, (2, 2))))]
    )
    d_prev, d_next = shift(d_up, "z", Z, 1), shift(d_down, "z", Z, -1)
    d_x_1 = shift(d_out_1, "xl", XL, 1)
    n_got = shift(n_give, "core", CORE, 1)
    f_prev_2, f_next_2, d_mine_1 = together(f_prev_2, f_next_2, d_mine_1)

    d_keep_2, d_give_2, own_grad, pre = middle(
        core_at, order, scale_column, chooser, own_first, s_1, slope, down_turned,
        (g_2, g_prev_2, g_next_2, f_prev_2, f_next_2),
    )
    d_got_2 = shift(d_give_2, "core", CORE, 1)
    d_got_2, d_prev, d_next, d_x_1, n_got = together(d_got_2, d_prev, d_next, d_x_1, n_got)
    pre_got = shift(pre, "core", CORE, 1)
    d_kept, d_out_2, d_mine_2, parts = grad_blocks(
        [(slots_2, d_keep_2, d_got_2, act, act_got, ((0, CUT, (4,)), (CUT, rest, (2, 2))))],
        (pre, up_turned),
    )
    pre_got, parts = together(pre_got, parts)

    blocks = parts.reshape(MEMBERS, tok_rows, width)
    p_prev = shift(below(blocks[4][:half], blocks[5][:half]), "y", Y, 1)
    p_next = shift(below(blocks[4][half:], blocks[5][half:]), "y", Y, -1)
    d_acc_prev = shift(add(d_kept[0], d_prev[0]), "z", Z, 1)
    d_acc_next = shift(add(d_kept[1], d_next[0]), "z", Z, -1)
    d_x_2 = shift(d_out_2, "xl", XL, 1)
    u_up, u_down, u_kept, u_out, u_mine = grad_blocks(
        [
            (
                jnp.stack([z_slots, x_slots]), n_keep, n_got, pre, pre_got,
                ((0, CUT, (2, 2, 4)), (CUT, rest, (4, 4))),
            )
        ]
    )
    p_prev, p_next, d_acc_prev, d_acc_next, d_x_2, u_mine = together(
        p_prev, p_next, d_acc_prev, d_acc_next, d_x_2, u_mine
    )

    u_prev, u_next = shift(u_up, "z", Z, 1), shift(u_down, "z", Z, -1)
    u_x = shift(u_out, "xl", XL, 1)
    o_prev = shift(below(add(blocks[3][:half], p_prev[half:]), blocks[3][half:]), "y", Y, 1)
    o_next = shift(below(blocks[7][:half], add(blocks[7][half:], p_next[half:])), "y", Y, -1)
    o_prev, o_next, p_prev, p_next = together(o_prev, o_next, p_prev, p_next)
    r_prev = shift(below(add(blocks[2][:half], p_prev[:half]), blocks[2][half:]), "y", Y, 1)
    r_next = shift(below(blocks[6][:half], add(blocks[6][half:], p_next[:half])), "y", Y, -1)
    u_prev, u_next, r_prev, r_next = together(u_prev, u_next, r_prev, r_next)

    cut = -(-d_x_1.shape[1] // 16) * 8
    two, side_1, side_2 = (
        add(d_mine_1[0], d_x_1[0]), add(d_mine_1[1], d_x_1[1]), add(d_mine_2[0], d_x_2[0])
    )
    one, three = jnp.where(here, side_2, side_1), jnp.where(here, side_1, side_2)
    d_here = add32(d_mine_2[1], d_x_2[1])
    d_b_one, d_b_three = one[:cut], three[cut:]
    to_next = beside(add(u_kept[0], u_prev[0]), below(two[:cut], one[cut:]))
    to_prev = beside(add(u_kept[1], u_next[0]), below(three[:cut], two[cut:]))
    m_prev, m_next = shift(to_next, "z", Z, 1), shift(to_prev, "z", Z, -1)
    r_other = shift(add(blocks[1], o_prev, o_next), "xh", XH, 1)
    sum_0 = add(d_kept[2], d_next[1], d_acc_prev)
    sum_1 = add(d_kept[3], d_prev[1], d_acc_next)
    d_own = jnp.where(here, sum_0, sum_1)
    d_other = shift(jnp.where(here, sum_1, sum_0), "xl", XL, 1)
    m_prev, m_next, u_x, r_other, d_other = together(m_prev, m_next, u_x, r_other, d_other)

    u_acc_prev, d_b_prev = m_prev[:, :CUT], m_prev[:, CUT:]
    u_acc_next, d_b_next = m_next[:, :CUT], m_next[:, CUT:]
    sum_0 = add(u_kept[2], u_next[1], u_acc_prev)
    sum_1 = add(u_kept[3], u_prev[1], u_acc_next)
    u_own = jnp.where(here, sum_0, sum_1)
    u_other = shift(jnp.where(here, sum_1, sum_0), "xl", XL, 1)
    two, one, three = (add(u_mine[i], u_x[i]) for i in range(3))
    u_here = add32(u_mine[3], u_x[3])
    b_prev = shift(
        below(add(d_b_one, d_b_prev[:cut]), two[:cut], one[cut:]), "z", Z, 1
    )
    b_next = shift(
        below(add(d_b_three, d_b_next[cut:]), three[:cut], two[cut:]), "z", Z, -1
    )
    tail = d_here.shape[0] - cut
    u_b_prev, u_b_next = b_prev[cut:], b_next[tail:]
    c_prev = shift(add(one[:cut], u_b_prev[:cut]), "z", Z, 1)
    c_next = shift(add(three[cut:], u_b_next[cut:]), "z", Z, -1)
    down_a, up_a = add32(d_own, d_other), add32(u_own, u_other)
    down_b = below(
        add32(d_here[:cut], d_b_next[:cut], b_prev[:cut]),
        add32(d_here[cut:], d_b_prev[cut:], b_next[:tail]),
    )
    up_b = below(
        add32(u_here[:cut], u_b_next[:cut], c_prev),
        add32(u_here[cut:], u_b_prev[cut:], c_next),
    )
    normed_grad = add32(blocks[0], r_prev, r_next, r_other)
    weighted = norm_gain * normed_grad
    input_grad = (
        own_grad.astype(F32)
        + inverse_rms * weighted
        - inputs * inverse_rms**3 * jnp.mean(weighted * inputs, -1, keepdims=True)
    ).astype(BF16)
    grad_scale = 1.0 / math.sqrt(group_len * BLOCKS)
    return (
        input_grad,
        (beside(up_a, up_b) * grad_scale).astype(BF16),
        (beside(down_a, down_b) * grad_scale).astype(BF16),
    )


def solution(mesh):
    fine = Mesh(mesh.devices.reshape(Z, XL, CORE, Y, XH), AXES)
    dp, tensor = AXES[:3], AXES[3:]
    in_specs = (
        P(AXES, None),
        P(AXES),
        P(),
        P(AXES, None),
        P(),
        P(),
        P(None, tensor),
        P(None, tensor),
    )
    out_specs = (P(AXES, None), P(dp, tensor), P(dp, tensor))
    return jax.shard_map(
        on_device, mesh=fine, in_specs=in_specs, out_specs=out_specs, check_vma=False
    )
```

```python
import math

import jax
import jax.numpy as jnp
from jax import lax
from jax.experimental import pallas as pl
from jax.experimental.pallas import tpu as pltpu
from jax.sharding import Mesh, PartitionSpec as P

F32 = jnp.float32
BF16 = jnp.bfloat16
Z, XL, CORE, Y, XH = 4, 2, 2, 4, 2
AXES = ("z", "xl", "core", "y", "xh")
MEMBERS = Y * XH
BLOCKS = Z * XL * CORE
ID_COLS = 128
ID_BASE = 32
CUT = 1152
MIB = 1024 * 1024
VMEM = pl.BlockSpec(memory_space=pltpu.VMEM)
SMEM = pl.BlockSpec(memory_space=pltpu.SMEM)
ANY = pl.BlockSpec(memory_space=pl.ANY)
HBM = pl.BlockSpec(memory_space=pltpu.HBM)


def params(mib):
    return pltpu.CompilerParams(vmem_limit_bytes=mib * MIB)


def cost(flops, moved, special=0):
    return pl.CostEstimate(flops=flops, bytes_accessed=moved, transcendentals=special)


def shift(value, axis, size, step):
    return lax.ppermute(value, axis, [(i, (i + step) % size) for i in range(size)])


def add32(*terms):
    total = terms[0].astype(F32)
    for term in terms[1:]:
        total = total + term.astype(F32)
    return total


def add(*terms):
    return add32(*terms).astype(BF16)


def together(*values):
    return lax.optimization_barrier(values)


def fetch(pieces, sem):
    copies = [pltpu.make_async_copy(src, dst, sem.at[i]) for i, (src, dst) in enumerate(pieces)]
    for copy in copies:
        copy.start()

    def wait():
        for copy in copies:
            copy.wait()

    return wait


def pieces_of(listed, out):
    at, pieces = 0, []
    for ref, first, rows in listed:
        pieces.append((ref.at[first : first + rows], out.at[at : at + rows]))
        at += rows
    return pieces


def split_parity(turned, core, pairs, keep, give):
    rows = keep.shape[0] // pairs
    for two in range(pairs // 2):
        for out, parity in ((keep, core), (give, 1 - core)):
            blocks = [
                turned[pl.ds(pl.multiple_of((2 * b + parity) * rows, 8), rows), :]
                for b in (2 * two, 2 * two + 1)
            ]
            out[2 * two * rows : (2 * two + 2) * rows, :] = jnp.concatenate(blocks, 0).astype(BF16)


def by_last(left, right):
    return lax.dot_general(left, right, (((1,), (1,)), ((), ())), preferred_element_type=F32)


def normed_kernel(core, *refs):
    ins, weight, (act, slope, keep, give) = refs[:8], refs[8], refs[9:13]
    normed, turned, held, act_s, slope_s, keep_s, give_s, in_sem, w_sem, out_sem, sem = refs[13:]
    own, other, nxt, prev, mix_prev, mix_next, far_a, far_b = ins
    full = own.shape[0]
    half = full // 2
    listed = [(own, 0, full), (other, 0, full), (nxt, 0, full), (mix_next, 0, full)]
    listed += [(mix_prev, full, half), (mix_next, full, half), (far_a, 0, half), (far_b, 0, half)]
    listed += [(prev, 0, full), (mix_prev, 0, full)]
    fetched = fetch(pieces_of(listed, normed), in_sem)
    tile = held.shape[1]
    count = held.shape[0]
    tiles = [slice(n * tile, (n + 1) * tile) for n in range(count)]
    weights = [fetch([(weight.at[tiles[n]], held.at[n])], w_sem.at[n]) for n in range(count)]
    fetched()
    for t in range(normed.shape[1] // 128):
        cols = slice(t * 128, (t + 1) * 128)
        turned[cols, :] = normed[:, cols].astype(F32).T
    split_parity(turned, core[0], BLOCKS // 2, keep_s, give_s)
    waits = [fetch([(give_s, give), (keep_s, keep)], out_sem)]
    for n, rows in enumerate(tiles):
        weights[n]()
        value = by_last(held[n], normed[...])
        below = 0.5 * (1.0 + lax.erf(value * 0.7071067811865476))
        act_s[rows, :] = (value * below).astype(BF16)
        slope_s[rows, :] = (
            below + value * jnp.exp(-0.5 * value * value) * 0.3989422804014327
        ).astype(BF16)
        waits.append(
            fetch([(act_s.at[rows], act.at[rows]), (slope_s.at[rows], slope.at[rows])], sem.at[n])
        )
    for wait in waits:
        wait()


def assemble_normed(core, ins, weight):
    rows, width = ins[0].shape[0] * MEMBERS, ins[0].shape[1]
    hidden = weight.shape[0]
    count = 4
    outs = [((hidden, rows), BF16)] * 2 + [((width // 2, rows), BF16)] * 2
    return pl.pallas_call(
        normed_kernel,
        out_shape=[jax.ShapeDtypeStruct(shape, kind) for shape, kind in outs],
        in_specs=[SMEM] + [HBM] * (len(ins) + 1),
        out_specs=[HBM] * 4,
        scratch_shapes=[
            pltpu.VMEM((rows, width), BF16),
            pltpu.VMEM((width, rows), F32),
            pltpu.VMEM((count, hidden // count, width), BF16),
        ]
        + [pltpu.VMEM(shape, kind) for shape, kind in outs]
        + [pltpu.SemaphoreType.DMA((n,)) for n in (10,)]
        + [pltpu.SemaphoreType.DMA((count, 1)), pltpu.SemaphoreType.DMA((2,))]
        + [pltpu.SemaphoreType.DMA((count, 2))],
        compiler_params=params(52),
        cost_estimate=cost(10**10, 10**7),
    )(core, *ins, weight)


def prepare_kernel(order, own, other, first, second, rows_s, turned, sorted_s, *refs):
    outs_s, in_sem, sem = refs[:2], refs[2], refs[3]
    half = own.shape[0] // 2
    listed = [(own, 0, half), (other, 0, half), (own, half, half), (other, half, half)]
    fetch(pieces_of(listed, rows_s), in_sem)()
    width = turned.shape[0]
    pair = width // (BLOCKS // 2)
    for t in range(width // 128):
        cols = slice(t * 128, (t + 1) * 128)
        turned[cols, :] = rows_s[:, cols].astype(F32).T
    waits = []
    for h, out in enumerate((first, second)):
        for p in range(4):
            at = pl.ds(pl.multiple_of(order[4 * h + p] * pair, 8), pair)
            sorted_s[p * pair : (p + 1) * pair, :] = turned[at, :]
        cols = width // 2
        lead = 0 if h else ID_COLS
        for first_col in range(0, cols, 128):
            last = min(first_col + 128, cols)
            outs_s[h][:, lead + first_col : lead + last] = (
                sorted_s[first_col : first_col + 128, :].T[:, : last - first_col].astype(BF16)
            )
        if h == 0:
            outs_s[h][:, :lead] = rows_s[:, width : width + ID_COLS]
        waits.append(fetch([(outs_s[h], out)], sem.at[h]))
    for wait in waits:
        wait()


def prepare(order, own, other, width):
    rows = 2 * own.shape[0]
    cols = width // 2
    return pl.pallas_call(
        prepare_kernel,
        out_shape=[
            jax.ShapeDtypeStruct((rows, cols + ID_COLS), BF16),
            jax.ShapeDtypeStruct((rows, cols), BF16),
        ],
        in_specs=[SMEM, HBM, HBM],
        out_specs=[HBM, HBM],
        scratch_shapes=[
            pltpu.VMEM((rows, width + ID_COLS), BF16),
            pltpu.VMEM((width, rows), F32),
            pltpu.VMEM((-(-cols // 128) * 128, rows), F32),
            pltpu.VMEM((rows, cols + ID_COLS), BF16),
            pltpu.VMEM((rows, cols), BF16),
            pltpu.SemaphoreType.DMA((4,)),
            pltpu.SemaphoreType.DMA((2, 1)),
        ],
        compiler_params=params(52),
        cost_estimate=cost(10**8, 10**6),
    )(order, own, other)


def joined_pieces(ins, joined):
    at, pieces = 0, []
    for ref in ins:
        rows = ref.shape[0]
        pieces.append((ref, joined.at[at : at + rows]))
        at += rows
    return pieces


def to_image_order(chooser, joined, lead, turned):
    cols = turned.shape[0]
    for first in range(0, cols, 640):
        last = min(first + 640, cols)
        grads = jnp.dot(
            chooser[...], joined[:, lead + first : lead + last], preferred_element_type=F32
        )
        turned[first:last, :] = grads.T


def first_kernel(core, order, scales, positions, *refs):
    ins, (scaled, keep, give, own_turned, chooser_out) = refs[:5], refs[5:10]
    joined, turned, scaled_s, keep_s, give_s, chooser, own_s, in_sem, sem, give_sem = refs[10:]
    cols = scaled.shape[0]
    pair = cols // 4
    fetch(joined_pieces(ins, joined), in_sem)()
    tags = joined[:, :ID_COLS].astype(F32).T
    places = tags[0:1, :] * ID_BASE + tags[1:2, :]
    chooser[...] = (positions[...] == places).astype(F32).astype(BF16)
    to_image_order(chooser, joined, ID_COLS, turned)
    own_s[...] = turned[:, :128]
    waits = [fetch([(own_s, own_turned), (chooser, chooser_out)], sem)]
    for p in range(4):
        here = slice(p * pair, (p + 1) * pair)
        turned[here, :] = turned[here, :] * scales[
            pl.ds(pl.multiple_of(order[p] * pair, 8), pair), :
        ]
        scaled_s[here, :] = turned[here, :].astype(BF16)
    split_parity(turned, core[0], 4, keep_s, give_s)
    waits.append(fetch([(give_s, give), (keep_s, keep), (scaled_s, scaled)], give_sem))
    for wait in waits:
        wait()


def route_first(core, order, scales, positions, ins):
    rows, cols = positions.shape[0], scales.shape[0] // 2
    turned = ((cols // 2, rows), BF16)
    outs = [((cols, rows), BF16), turned, turned, ((cols, 128), F32), ((rows, rows), BF16)]
    return pl.pallas_call(
        first_kernel,
        out_shape=[jax.ShapeDtypeStruct(shape, kind) for shape, kind in outs],
        in_specs=[SMEM, SMEM, VMEM, VMEM] + [HBM] * len(ins),
        out_specs=[HBM] * 5,
        scratch_shapes=[
            pltpu.VMEM((rows, cols + ID_COLS), BF16),
            pltpu.VMEM((cols, rows), F32),
            pltpu.VMEM((cols, rows), BF16),
            pltpu.VMEM((cols // 2, rows), BF16),
            pltpu.VMEM((cols // 2, rows), BF16),
            pltpu.VMEM((rows, rows), BF16),
            pltpu.VMEM((cols, 128), F32),
        ]
        + [pltpu.SemaphoreType.DMA((n,)) for n in (5, 2, 3)],
        compiler_params=params(52),
        cost_estimate=cost(10**9, 10**7),
    )(core, order, scales, positions, *ins)


def middle_kernel(core, order, *refs):
    scales, chooser_in, own_first, scaled_1, slope, down = refs[:6]
    ins, (keep, give, own_grad, pre) = refs[6:11], refs[11:15]
    joined, turned, scaled, keep_s, give_s, chooser, own_s, own_rows, own_out = refs[15:24]
    slope_s, down_s, pre_s, scales_s = refs[24:28]
    in_sem, s_sem, d_sem, give_sem, own_sem, pre_sem = refs[28:]
    cols = joined.shape[1]
    pair = cols // 4
    got = fetch(
        joined_pieces(ins, joined)
        + [(chooser_in, chooser), (scales, scales_s), (own_first, own_s.at[0])],
        in_sem,
    )
    more = [(slope, slope_s)]
    for p in range(4):
        at = pl.ds(pl.multiple_of(order[p] * pair, 16), pair)
        more.append((scaled_1.at[p * pair : (p + 1) * pair], scaled.at[at]))
    got_more = fetch(more, s_sem)
    count = 2
    tile = down.shape[0] // count
    tiles = [slice(n * tile, (n + 1) * tile) for n in range(count)]
    got_down = [fetch([(down.at[rows], down_s.at[rows])], d_sem.at[n]) for n, rows in enumerate(tiles)]
    got()
    to_image_order(chooser, joined, 0, turned)
    own_s[1] = turned[:, :128]
    got_more()
    for p in range(4):
        here = slice(p * pair, (p + 1) * pair)
        place = order[4 + p] * pair
        turned[here, :] = turned[here, :] * scales_s[pl.ds(pl.multiple_of(place, 8), pair), :]
        scaled[pl.ds(pl.multiple_of(place, 16), pair), :] = turned[here, :].astype(BF16)
    split_parity(turned, core[0], 4, keep_s, give_s)
    waits = [fetch([(give_s, give), (keep_s, keep)], give_sem)]
    for n, rows in enumerate(tiles):
        got_down[n]()
        value = jnp.dot(down_s[rows, :], scaled[...], preferred_element_type=F32)
        pre_s[rows, :] = (value * slope_s[rows, :].astype(F32)).astype(BF16)
        waits.append(fetch([(pre_s.at[rows], pre.at[rows])], pre_sem.at[n]))
    for p in range(8):
        at = pl.ds(pl.multiple_of(order[p] * pair, 8), pair)
        own_rows[at, :] = own_s[p // 4, (p % 4) * pair : (p % 4 + 1) * pair, :]
    for t in range(own_rows.shape[0] // 128):
        here = slice(t * 128, (t + 1) * 128)
        own_out[:, here] = own_rows[here, :].T[: own_out.shape[0]].astype(BF16)
    waits.append(fetch([(own_out, own_grad)], own_sem))
    for wait in waits:
        wait()


def middle(core, order, scales, chooser, own_first, scaled_1, slope, down, ins):
    hidden, width = down.shape
    rows, cols = chooser.shape[0], width // 2
    turned = ((cols // 2, rows), BF16)
    outs = [turned, turned, ((rows // MEMBERS, width), BF16), ((hidden, rows), BF16)]
    return pl.pallas_call(
        middle_kernel,
        out_shape=[jax.ShapeDtypeStruct(shape, kind) for shape, kind in outs],
        in_specs=[SMEM, SMEM] + [HBM] * (6 + len(ins)),
        out_specs=[HBM] * 4,
        scratch_shapes=[
            pltpu.VMEM((rows, cols), BF16),
            pltpu.VMEM((cols, rows), F32),
            pltpu.VMEM((width, rows), BF16),
            pltpu.VMEM((cols // 2, rows), BF16),
            pltpu.VMEM((cols // 2, rows), BF16),
            pltpu.VMEM((rows, rows), BF16),
            pltpu.VMEM((2, cols, 128), F32),
            pltpu.VMEM((width, 128), F32),
            pltpu.VMEM((rows // MEMBERS, width), BF16),
            pltpu.VMEM((hidden, rows), BF16),
            pltpu.VMEM((hidden, width), BF16),
            pltpu.VMEM((hidden, rows), BF16),
            pltpu.VMEM((width, 1), F32),
        ]
        + [pltpu.SemaphoreType.DMA((n,)) for n in (8, 5)]
        + [pltpu.SemaphoreType.DMA((2, 1))]
        + [pltpu.SemaphoreType.DMA((n,)) for n in (2, 1)]
        + [pltpu.SemaphoreType.DMA((2, 1))],
        compiler_params=params(52),
        cost_estimate=cost(10**10, 10**7),
    )(core, order, scales, chooser, own_first, scaled_1, slope, down, *ins)


def blocks_kernel(jobs, sums, *refs):
    group = 800
    count = len(jobs)
    if sums:
        refs, (pre_s, up_s, sums_s, up_sem, sums_sem) = refs[:-5], refs[-5:]
        pre, up = refs[5 * count : 5 * count + 2]
        refs = refs[: 5 * count] + refs[5 * count + 2 :]
    ins, refs = refs[: 5 * count], refs[5 * count :]
    total = sum(len(sizes) for parts in jobs for _, _, sizes in parts)
    pieces = sum(len(parts) for parts in jobs)
    scratch = refs[-(3 * count + 3 * pieces) :]
    outs, sums_out = refs[:total], refs[total] if sums else None
    todo = []
    at_out = at = 0
    for k, parts in enumerate(jobs):
        slots, left, left_got, right, right_got = ins[5 * k : 5 * k + 5]
        left_s, l_sem, r_sem = scratch[at : at + 3]
        at += 3
        rows_in = left.shape[1]
        waits_r = []
        each = []
        for i, (first, cols, sizes) in enumerate(parts):
            right_s, stage, sem = scratch[at : at + 3]
            at += 3
            here = slice(first, first + cols)
            waits_r.append(
                fetch(
                    [
                        (right.at[here], right_s.at[:cols, :rows_in]),
                        (right_got.at[here], right_s.at[:cols, rows_in:]),
                    ],
                    r_sem.at[i],
                )
            )
            each.append((i, cols, sizes, right_s, stage, sem, outs[at_out : at_out + len(sizes)]))
            at_out += len(sizes)
        waits_l = []
        for g in range(left.shape[0] // group):
            here = slice(g * group, (g + 1) * group)
            waits_l.append(
                fetch(
                    [
                        (left.at[here], left_s.at[here, :rows_in]),
                        (left_got.at[here], left_s.at[here, rows_in:]),
                    ],
                    l_sem.at[g],
                )
            )
        todo.append((slots, left_s, waits_l, waits_r, each))
    if sums:
        got_up = fetch([(pre, pre_s), (up, up_s)], up_sem)
    for slots, left_s, waits_l, waits_r, each in todo:
        for i, cols, sizes, right_s, stage, sem, targets in each:
            waits_r[i]()
            block = stage.shape[1]
            per = group // block
            for g in range(len(waits_l)):
                if i == 0:
                    waits_l[g]()
                product = by_last(left_s[g * group : (g + 1) * group, :], right_s[...])
                for b in range(per):
                    j = g * per + b
                    stage[j] = product[b * block : (b + 1) * block, :cols].astype(BF16)
                    slot = slots[i, j]
                    first = 0
                    for out, size in zip(targets, sizes):

                        @pl.when((slot >= first) & (slot < first + size))
                        def _(out=out, first=first, j=j, slot=slot, stage=stage, sem=sem):
                            pltpu.make_async_copy(
                                stage.at[j], out.at[slot - first], sem.at[j]
                            ).start()

                        first += size
    if sums:
        got_up()
        for first in range(0, up.shape[1], 512):
            here = slice(first, min(first + 512, up.shape[1]))
            sums_s[:, here] = lax.dot_general(
                pre_s[...], up_s[:, here], (((0,), (0,)), ((), ())), preferred_element_type=F32
            ).astype(BF16)
        fetch([(sums_s, sums_out)], sums_sem)()
    for _, _, _, _, each in todo:
        for _, _, _, _, stage, sem, targets in each:
            for j in range(stage.shape[0]):
                pltpu.make_async_copy(stage.at[j], targets[0].at[0], sem.at[j]).wait()


def grad_blocks(jobs, sums=()):
    block = 200
    specs, ins, outs, scratch = [], [], [], []
    for slots, left, left_got, right, right_got, parts in jobs:
        width, rows = left.shape
        specs += [SMEM] + [HBM] * 4
        ins += [slots, left, left_got, right, right_got]
        scratch += [
            pltpu.VMEM((width, 2 * rows), BF16),
            pltpu.SemaphoreType.DMA((width // 800, 2)),
            pltpu.SemaphoreType.DMA((len(parts), 2)),
        ]
        for _, cols, sizes in parts:
            outs += [jax.ShapeDtypeStruct((size, block, cols), BF16) for size in sizes]
            scratch += [
                pltpu.VMEM((-(-cols // 256) * 256, 2 * rows), BF16),
                pltpu.VMEM((width // block, block, cols), BF16),
                pltpu.SemaphoreType.DMA((width // block,)),
            ]
    lists = [job[-1] for job in jobs]
    if sums:
        (hidden, rows), width = sums[0].shape, sums[1].shape[1]
        specs += [HBM] * 2
        ins += list(sums)
        outs.append(jax.ShapeDtypeStruct((rows, width), BF16))
        scratch += [
            pltpu.VMEM((hidden, rows), BF16),
            pltpu.VMEM((hidden, width), BF16),
            pltpu.VMEM((rows, width), BF16),
            pltpu.SemaphoreType.DMA((2,)),
            pltpu.SemaphoreType.DMA((1,)),
        ]

    def kernel(*refs):
        blocks_kernel(lists, bool(sums), *refs)

    return pl.pallas_call(
        kernel,
        out_shape=outs,
        in_specs=specs,
        out_specs=[HBM] * len(outs),
        scratch_shapes=scratch,
        compiler_params=params(52),
        cost_estimate=cost(10**10, 10**7),
    )(*ins)


def z_order(z, xl):
    pairs = [(2, 0), (1, 1), (2, 1), (3, 0), (1, 0), (3, 1), (0, 0), (0, 1)]
    return [((z + dz) % Z) * XL + x for dz, x in pairs]


def x_order(z, xl):
    pairs = [(dz, dx) for dx in (1, 0) for dz in (2, 1, 3, 0)]
    return [((z + dz) % Z) * XL + (xl + dx) % XL for dz, dx in pairs]


def slots_of(order):
    order = jnp.stack(order).astype(jnp.int32)
    index = jnp.arange(order.shape[0], dtype=jnp.int32)
    return jnp.sum(jnp.where(order[None, :] == index[:, None], index[None, :], 0), 1)


def beside(*parts):
    return jnp.concatenate(parts, 1)


def below(*parts):
    return jnp.concatenate(parts, 0)


def on_device(
    lm_grad, encoder_row, patch_count, hidden_in, norm_gain, layer_scale, up_weight, down_weight
):
    tok_rows, width = hidden_in.shape
    rest = up_weight.shape[1] - CUT
    up_turned, down_turned = up_weight.T, down_weight.T
    group_len = tok_rows * MEMBERS
    per_pair = tok_rows // BLOCKS
    half = tok_rows // 2
    z, xl, core = lax.axis_index("z"), lax.axis_index("xl"), lax.axis_index("core")
    y, xh = lax.axis_index("y"), lax.axis_index("xh")
    group = (z * XL + xl) * CORE + core
    core_at = core.reshape(1).astype(jnp.int32)
    z_slots, x_slots = slots_of(z_order(z, xl)), slots_of(x_order(z, xl))

    inputs = hidden_in.astype(F32)
    inverse_rms = lax.rsqrt(jnp.mean(inputs * inputs, -1, keepdims=True) + 1e-06)
    normed_own = (inputs * inverse_rms * norm_gain).astype(BF16)

    n_prev = shift(normed_own, "y", Y, 1)
    n_next = shift(normed_own, "y", Y, -1)
    n_other = shift(normed_own, "xh", XH, 1)

    image, place = encoder_row // group_len, encoder_row % group_len
    index = jnp.arange(tok_rows, dtype=jnp.int32)
    same = (image[:, None] == image[None, :]) & (index[None, :] < index[:, None])
    slot = image * per_pair + jnp.sum(same.astype(jnp.int32), 1)
    sorter = (slot[None, :] == index[:, None]).astype(BF16)
    column = jnp.arange(ID_COLS, dtype=jnp.int32)[None, :]
    tags = jnp.where(
        column == 0,
        (place // ID_BASE)[:, None],
        jnp.where(column == 1, (place % ID_BASE)[:, None], 0),
    ).astype(BF16)
    ordered = jnp.dot(sorter, beside(lm_grad, tags), preferred_element_type=F32).astype(BF16)
    arrived = lax.all_to_all(
        ordered.reshape(BLOCKS, per_pair, width + ID_COLS),
        ("z", "xl", "core"),
        split_axis=0,
        concat_axis=0,
    ).reshape(tok_rows, width + ID_COLS)

    n_prev, n_next, n_other = together(n_prev, n_next, n_other)
    mix_prev = shift(below(n_other, n_prev[:half]), "y", Y, 1)
    mix_next = shift(below(n_other, n_next[half:]), "y", Y, -1)
    g_other = shift(arrived, "xh", XH, 1)
    block = jnp.arange(MEMBERS, dtype=jnp.int32)
    member = ((block // XH + y) % Y) * XH + (block % XH + xh) % XH
    positions = (member[:, None] * tok_rows + index[None, :]).reshape(group_len, 1)
    limit = lax.dynamic_index_in_dim(patch_count, group, 0, keepdims=False)
    positions = jnp.where(positions < limit, positions, -1).astype(F32)
    scale_column = layer_scale.reshape(width, 1)
    mix_prev, mix_next, g_other, arrived, positions, scale_column = together(
        mix_prev, mix_next, g_other, arrived, positions, scale_column
    )

    far_a = shift(mix_prev[:half], "y", Y, 1)
    far_b = shift(mix_next[half:tok_rows], "y", Y, -1)
    order = jnp.stack(z_order(z, xl)).astype(jnp.int32)
    g_1, g_2 = prepare(order, arrived, g_other, width)
    far_a, far_b, g_1, g_2 = together(far_a, far_b, g_1, g_2)

    g_prev_1, g_next_1 = shift(g_1, "y", Y, 1), shift(g_1, "y", Y, -1)
    g_prev_2, g_next_2 = shift(g_2, "y", Y, 1), shift(g_2, "y", Y, -1)
    act, slope, n_keep, n_give = assemble_normed(
        core_at, (normed_own, n_other, n_next, n_prev, mix_prev, mix_next, far_a, far_b), up_turned
    )
    g_prev_1, g_next_1, g_prev_2, g_next_2, act, n_give = together(
        g_prev_1, g_next_1, g_prev_2, g_next_2, act, n_give
    )

    f_prev_1 = shift(g_prev_1[:tok_rows], "y", Y, 1)
    f_next_1 = shift(g_next_1[tok_rows:], "y", Y, -1)
    f_prev_2 = shift(g_prev_2[:tok_rows], "y", Y, 1)
    f_next_2 = shift(g_next_2[tok_rows:], "y", Y, -1)
    f_prev_1, f_next_1, act, n_give = together(f_prev_1, f_next_1, act, n_give)
    act_got = shift(act, "core", CORE, 1)
    s_1, d_keep_1, d_give_1, own_first, chooser = route_first(
        core_at, order, scale_column, positions, (g_1, g_prev_1, g_next_1, f_prev_1, f_next_1)
    )
    d_got_1 = shift(d_give_1, "core", CORE, 1)
    here = xl == 0
    straight = jnp.arange(4, dtype=jnp.int32)
    slots_1 = jnp.stack([straight, jnp.where(here, jnp.array([2, 1, 0, 3]), jnp.array([0, 3, 2, 1]))])
    slots_2 = jnp.stack([straight, jnp.where(here, jnp.array([2, 0, 3, 1]), jnp.array([0, 2, 1, 3]))])
    slots_1, slots_2 = slots_1.astype(jnp.int32), slots_2.astype(jnp.int32)
    d_got_1, act_got, n_give = together(d_got_1, act_got, n_give)
    d_up, d_down, d_out_1, d_mine_1 = grad_blocks(
        [(slots_1, d_keep_1, d_got_1, act, act_got, ((0, CUT, (2, 2)), (CUT, rest, (2, 2))))]
    )
    d_prev, d_next = shift(d_up, "z", Z, 1), shift(d_down, "z", Z, -1)
    d_x_1 = shift(d_out_1, "xl", XL, 1)
    n_got = shift(n_give, "core", CORE, 1)
    f_prev_2, f_next_2, d_mine_1 = together(f_prev_2, f_next_2, d_mine_1)

    d_keep_2, d_give_2, own_grad, pre = middle(
        core_at, order, scale_column, chooser, own_first, s_1, slope, down_turned,
        (g_2, g_prev_2, g_next_2, f_prev_2, f_next_2),
    )
    d_got_2 = shift(d_give_2, "core", CORE, 1)
    d_got_2, d_prev, d_next, d_x_1, n_got = together(d_got_2, d_prev, d_next, d_x_1, n_got)
    pre_got = shift(pre, "core", CORE, 1)
    d_kept, d_out_2, d_mine_2, parts = grad_blocks(
        [(slots_2, d_keep_2, d_got_2, act, act_got, ((0, CUT, (4,)), (CUT, rest, (2, 2))))],
        (pre, up_turned),
    )
    pre_got, parts = together(pre_got, parts)

    d_acc_prev = shift(add(d_kept[0], d_prev[0]), "z", Z, 1)
    d_acc_next = shift(add(d_kept[1], d_next[0]), "z", Z, -1)
    d_x_2 = shift(d_out_2, "xl", XL, 1)
    u_up, u_down, u_kept, u_out, u_mine = grad_blocks(
        [
            (
                jnp.stack([z_slots, x_slots]), n_keep, n_got, pre, pre_got,
                ((0, CUT, (2, 2, 4)), (CUT, rest, (4, 4))),
            )
        ]
    )
    d_acc_prev, d_acc_next, d_x_2, u_mine, parts = together(
        d_acc_prev, d_acc_next, d_x_2, u_mine, parts
    )

    u_prev, u_next = shift(u_up, "z", Z, 1), shift(u_down, "z", Z, -1)
    u_x = shift(u_out, "xl", XL, 1)
    blocks = parts.reshape(MEMBERS, tok_rows, width)
    p_prev = shift(below(blocks[4][:half], blocks[5][:half]), "y", Y, 1)
    p_next = shift(below(blocks[4][half:], blocks[5][half:]), "y", Y, -1)
    sum_0 = add(d_kept[2], d_next[1], d_acc_prev)
    sum_1 = add(d_kept[3], d_prev[1], d_acc_next)
    d_own, d_give = jnp.where(here, sum_0, sum_1), jnp.where(here, sum_1, sum_0)
    o_prev, o_next = (
        below(add(blocks[3][:half], p_prev[half:]), blocks[3][half:]),
        below(blocks[7][:half], add(blocks[7][half:], p_next[half:])),
    )
    d_give, u_x, _, _ = together(d_give, u_x, o_prev, o_next)
    o_prev, o_next = shift(o_prev, "y", Y, 1), shift(o_next, "y", Y, -1)
    d_other = shift(d_give, "xl", XL, 1)

    m_prev = shift(add(u_kept[0], u_prev[0]), "z", Z, 1)
    m_next = shift(add(u_kept[1], u_next[0]), "z", Z, -1)
    d_other, p_prev, p_next, o_prev, o_next = together(d_other, p_prev, p_next, o_prev, o_next)
    r_other = shift(add(blocks[1], o_prev, o_next), "xh", XH, 1)
    r_prev = shift(below(add(blocks[2][:half], p_prev[:half]), blocks[2][half:]), "y", Y, 1)
    r_next = shift(below(blocks[6][:half], add(blocks[6][half:], p_next[:half])), "y", Y, -1)

    sum_0 = add(u_kept[2], u_next[1], m_prev)
    sum_1 = add(u_kept[3], u_prev[1], m_next)
    u_own, u_give = jnp.where(here, sum_0, sum_1), jnp.where(here, sum_1, sum_0)
    u_other = shift(u_give, "xl", XL, 1)
    cut = -(-d_x_1.shape[1] // 16) * 8
    u_x, d_x_2, r_prev, r_next, u_own, d_other = together(
        u_x, d_x_2, r_prev, r_next, u_own, d_other
    )
    two, side_1, side_2 = (
        add(d_mine_1[0], d_x_1[0]), add(d_mine_1[1], d_x_1[1]), add(d_mine_2[0], d_x_2[0])
    )
    one, three = jnp.where(here, side_2, side_1), jnp.where(here, side_1, side_2)
    two, one, three = (
        beside(both, add(u_mine[i], u_x[i])) for i, both in enumerate((two, one, three))
    )
    b_here = beside(add32(d_mine_2[1], d_x_2[1]), add32(u_mine[3], u_x[3]))
    b_prev = shift(below(two[:cut], one[cut:]), "z", Z, 1)
    b_next = shift(below(three[:cut], two[cut:]), "z", Z, -1)
    c_prev = shift(add(one[:cut], b_prev[:cut]), "z", Z, 1)
    c_next = shift(add(three[cut:], b_next[cut:]), "z", Z, -1)
    r_prev, r_next, r_other, b_prev = together(r_prev, r_next, r_other, b_prev)
    down_a, up_a = add32(d_own, d_other), add32(u_own, u_other)
    b_total = below(
        add32(b_here[:cut], b_next[:cut], c_prev), add32(b_here[cut:], b_prev[cut:], c_next)
    )
    down_b, up_b = b_total[:, :rest], b_total[:, rest:]
    normed_grad = add32(blocks[0], r_prev, r_next, r_other)
    weighted = norm_gain * normed_grad
    input_grad = (
        own_grad.astype(F32)
        + inverse_rms * weighted
        - inputs * inverse_rms**3 * jnp.mean(weighted * inputs, -1, keepdims=True)
    ).astype(BF16)
    grad_scale = 1.0 / math.sqrt(group_len * BLOCKS)
    return (
        input_grad,
        (beside(up_a, up_b) * grad_scale).astype(BF16),
        (beside(down_a, down_b) * grad_scale).astype(BF16),
    )


def solution(mesh):
    fine = Mesh(mesh.devices.reshape(Z, XL, CORE, Y, XH), AXES)
    dp, tensor = AXES[:3], AXES[3:]
    in_specs = (
        P(AXES, None),
        P(AXES),
        P(),
        P(AXES, None),
        P(),
        P(),
        P(None, tensor),
        P(None, tensor),
    )
    out_specs = (P(AXES, None), P(dp, tensor), P(dp, tensor))
    return jax.shard_map(
        on_device, mesh=fine, in_specs=in_specs, out_specs=out_specs, check_vma=False
    )
```

```python
import math

import jax
import jax.numpy as jnp
from jax import lax
from jax.experimental import pallas as pl
from jax.experimental.pallas import tpu as pltpu
from jax.sharding import Mesh, PartitionSpec as P

F32 = jnp.float32
BF16 = jnp.bfloat16
Z, XL, CORE, Y, XH = 4, 2, 2, 4, 2
AXES = ("z", "xl", "core", "y", "xh")
MEMBERS = Y * XH
BLOCKS = Z * XL * CORE
ID_COLS = 128
ID_BASE = 32
CUT = 1152
UP_CUT = 1152
MIB = 1024 * 1024
VMEM = pl.BlockSpec(memory_space=pltpu.VMEM)
SMEM = pl.BlockSpec(memory_space=pltpu.SMEM)
ANY = pl.BlockSpec(memory_space=pl.ANY)
HBM = pl.BlockSpec(memory_space=pltpu.HBM)


def params(mib):
    return pltpu.CompilerParams(vmem_limit_bytes=mib * MIB)


def cost(flops, moved, special=0):
    return pl.CostEstimate(flops=flops, bytes_accessed=moved, transcendentals=special)


def shift(value, axis, size, step):
    return lax.ppermute(value, axis, [(i, (i + step) % size) for i in range(size)])


def add32(*terms):
    total = terms[0].astype(F32)
    for term in terms[1:]:
        total = total + term.astype(F32)
    return total


def add(*terms):
    return add32(*terms).astype(BF16)


def together(*values):
    return lax.optimization_barrier(values)


def fetch(pieces, sem):
    copies = [pltpu.make_async_copy(src, dst, sem.at[i]) for i, (src, dst) in enumerate(pieces)]
    for copy in copies:
        copy.start()

    def wait():
        for copy in copies:
            copy.wait()

    return wait


def pieces_of(listed, out):
    at, pieces = 0, []
    for ref, first, rows in listed:
        pieces.append((ref.at[first : first + rows], out.at[at : at + rows]))
        at += rows
    return pieces


def split_parity(turned, core, pairs, keep, give):
    rows = keep.shape[0] // pairs
    for two in range(pairs // 2):
        for out, parity in ((keep, core), (give, 1 - core)):
            blocks = [
                turned[pl.ds(pl.multiple_of((2 * b + parity) * rows, 8), rows), :]
                for b in (2 * two, 2 * two + 1)
            ]
            out[2 * two * rows : (2 * two + 2) * rows, :] = jnp.concatenate(blocks, 0).astype(BF16)


def by_last(left, right):
    return lax.dot_general(left, right, (((1,), (1,)), ((), ())), preferred_element_type=F32)


def normed_kernel(core, *refs):
    ins, weight, (act, slope, keep, give) = refs[:8], refs[8], refs[9:13]
    normed, turned, held, act_s, slope_s, keep_s, give_s, in_sem, w_sem, out_sem, sem = refs[13:]
    own, other, nxt, prev, mix_prev, mix_next, far_a, far_b = ins
    full = own.shape[0]
    half = full // 2
    listed = [(own, 0, full), (other, 0, full), (nxt, 0, full), (mix_next, 0, full)]
    listed += [(mix_prev, full, half), (mix_next, full, half), (far_a, 0, half), (far_b, 0, half)]
    listed += [(prev, 0, full), (mix_prev, 0, full)]
    fetched = fetch(pieces_of(listed, normed), in_sem)
    tile = held.shape[1]
    count = held.shape[0]
    tiles = [slice(n * tile, (n + 1) * tile) for n in range(count)]
    weights = [fetch([(weight.at[tiles[n]], held.at[n])], w_sem.at[n]) for n in range(count)]
    fetched()
    for t in range(normed.shape[1] // 128):
        cols = slice(t * 128, (t + 1) * 128)
        turned[cols, :] = normed[:, cols].astype(F32).T
    split_parity(turned, core[0], BLOCKS // 2, keep_s, give_s)
    waits = [fetch([(give_s, give), (keep_s, keep)], out_sem)]
    for n, rows in enumerate(tiles):
        weights[n]()
        value = by_last(held[n], normed[...])
        below = 0.5 * (1.0 + lax.erf(value * 0.7071067811865476))
        act_s[rows, :] = (value * below).astype(BF16)
        slope_s[rows, :] = (
            below + value * jnp.exp(-0.5 * value * value) * 0.3989422804014327
        ).astype(BF16)
        waits.append(
            fetch([(act_s.at[rows], act.at[rows]), (slope_s.at[rows], slope.at[rows])], sem.at[n])
        )
    for wait in waits:
        wait()


def assemble_normed(core, ins, weight):
    rows, width = ins[0].shape[0] * MEMBERS, ins[0].shape[1]
    hidden = weight.shape[0]
    count = 4
    outs = [((hidden, rows), BF16)] * 2 + [((width // 2, rows), BF16)] * 2
    return pl.pallas_call(
        normed_kernel,
        out_shape=[jax.ShapeDtypeStruct(shape, kind) for shape, kind in outs],
        in_specs=[SMEM] + [HBM] * (len(ins) + 1),
        out_specs=[HBM] * 4,
        scratch_shapes=[
            pltpu.VMEM((rows, width), BF16),
            pltpu.VMEM((width, rows), F32),
            pltpu.VMEM((count, hidden // count, width), BF16),
        ]
        + [pltpu.VMEM(shape, kind) for shape, kind in outs]
        + [pltpu.SemaphoreType.DMA((n,)) for n in (10,)]
        + [pltpu.SemaphoreType.DMA((count, 1)), pltpu.SemaphoreType.DMA((2,))]
        + [pltpu.SemaphoreType.DMA((count, 2))],
        compiler_params=params(52),
        cost_estimate=cost(10**10, 10**7),
    )(core, *ins, weight)


def prepare_kernel(order, own, other, first, second, rows_s, turned, sorted_s, *refs):
    outs_s, in_sem, sem = refs[:2], refs[2], refs[3]
    half = own.shape[0] // 2
    listed = [(own, 0, half), (other, 0, half), (own, half, half), (other, half, half)]
    fetch(pieces_of(listed, rows_s), in_sem)()
    width = turned.shape[0]
    pair = width // (BLOCKS // 2)
    for t in range(width // 128):
        cols = slice(t * 128, (t + 1) * 128)
        turned[cols, :] = rows_s[:, cols].astype(F32).T
    waits = []
    for h, out in enumerate((first, second)):
        for p in range(4):
            at = pl.ds(pl.multiple_of(order[4 * h + p] * pair, 8), pair)
            sorted_s[p * pair : (p + 1) * pair, :] = turned[at, :]
        cols = width // 2
        lead = 0 if h else ID_COLS
        for first_col in range(0, cols, 128):
            last = min(first_col + 128, cols)
            outs_s[h][:, lead + first_col : lead + last] = (
                sorted_s[first_col : first_col + 128, :].T[:, : last - first_col].astype(BF16)
            )
        if h == 0:
            outs_s[h][:, :lead] = rows_s[:, width : width + ID_COLS]
        waits.append(fetch([(outs_s[h], out)], sem.at[h]))
    for wait in waits:
        wait()


def prepare(order, own, other, width):
    rows = 2 * own.shape[0]
    cols = width // 2
    return pl.pallas_call(
        prepare_kernel,
        out_shape=[
            jax.ShapeDtypeStruct((rows, cols + ID_COLS), BF16),
            jax.ShapeDtypeStruct((rows, cols), BF16),
        ],
        in_specs=[SMEM, HBM, HBM],
        out_specs=[HBM, HBM],
        scratch_shapes=[
            pltpu.VMEM((rows, width + ID_COLS), BF16),
            pltpu.VMEM((width, rows), F32),
            pltpu.VMEM((-(-cols // 128) * 128, rows), F32),
            pltpu.VMEM((rows, cols + ID_COLS), BF16),
            pltpu.VMEM((rows, cols), BF16),
            pltpu.SemaphoreType.DMA((4,)),
            pltpu.SemaphoreType.DMA((2, 1)),
        ],
        compiler_params=params(52),
        cost_estimate=cost(10**8, 10**6),
    )(order, own, other)


def joined_pieces(ins, joined):
    at, pieces = 0, []
    for ref in ins:
        rows = ref.shape[0]
        pieces.append((ref, joined.at[at : at + rows]))
        at += rows
    return pieces


def to_image_order(chooser, joined, lead, turned):
    cols = turned.shape[0]
    for first in range(0, cols, 640):
        last = min(first + 640, cols)
        grads = jnp.dot(
            chooser[...], joined[:, lead + first : lead + last], preferred_element_type=F32
        )
        turned[first:last, :] = grads.T


def first_kernel(core, order, scales, positions, *refs):
    ins, (scaled, keep, give, own_turned, chooser_out) = refs[:5], refs[5:10]
    joined, turned, scaled_s, keep_s, give_s, chooser, own_s, in_sem, sem, give_sem = refs[10:]
    cols = scaled.shape[0]
    pair = cols // 4
    fetch(joined_pieces(ins, joined), in_sem)()
    tags = joined[:, :ID_COLS].astype(F32).T
    places = tags[0:1, :] * ID_BASE + tags[1:2, :]
    chooser[...] = (positions[...] == places).astype(F32).astype(BF16)
    to_image_order(chooser, joined, ID_COLS, turned)
    own_s[...] = turned[:, :128]
    waits = [fetch([(own_s, own_turned), (chooser, chooser_out)], sem)]
    for p in range(4):
        here = slice(p * pair, (p + 1) * pair)
        turned[here, :] = turned[here, :] * scales[
            pl.ds(pl.multiple_of(order[p] * pair, 8), pair), :1
        ]
        scaled_s[here, :] = turned[here, :].astype(BF16)
    split_parity(turned, core[0], 4, keep_s, give_s)
    waits.append(fetch([(give_s, give), (keep_s, keep), (scaled_s, scaled)], give_sem))
    for wait in waits:
        wait()


def route_first(core, order, scales, positions, ins):
    rows, cols = positions.shape[0], scales.shape[0] // 2
    turned = ((cols // 2, rows), BF16)
    outs = [((cols, rows), BF16), turned, turned, ((cols, 128), F32), ((rows, rows), BF16)]
    return pl.pallas_call(
        first_kernel,
        out_shape=[jax.ShapeDtypeStruct(shape, kind) for shape, kind in outs],
        in_specs=[SMEM, SMEM, VMEM, VMEM] + [HBM] * len(ins),
        out_specs=[HBM] * 5,
        scratch_shapes=[
            pltpu.VMEM((rows, cols + ID_COLS), BF16),
            pltpu.VMEM((cols, rows), F32),
            pltpu.VMEM((cols, rows), BF16),
            pltpu.VMEM((cols // 2, rows), BF16),
            pltpu.VMEM((cols // 2, rows), BF16),
            pltpu.VMEM((rows, rows), BF16),
            pltpu.VMEM((cols, 128), F32),
        ]
        + [pltpu.SemaphoreType.DMA((n,)) for n in (5, 2, 3)],
        compiler_params=params(52),
        cost_estimate=cost(10**9, 10**7),
    )(core, order, scales, positions, *ins)


def middle_kernel(core, order, *refs):
    scales, chooser_in, own_first, scaled_1, slope, down = refs[:6]
    ins, (keep, give, own_grad, pre) = refs[6:11], refs[11:15]
    joined, turned, scaled, keep_s, give_s, chooser, own_s, own_rows, own_out = refs[15:24]
    slope_s, down_s, pre_s, scales_s = refs[24:28]
    in_sem, s_sem, d_sem, give_sem, own_sem, pre_sem = refs[28:]
    cols = joined.shape[1]
    pair = cols // 4
    got = fetch(
        joined_pieces(ins, joined)
        + [(chooser_in, chooser), (scales, scales_s), (own_first, own_s.at[0])],
        in_sem,
    )
    more = [(slope, slope_s)]
    for p in range(4):
        at = pl.ds(pl.multiple_of(order[p] * pair, 16), pair)
        more.append((scaled_1.at[p * pair : (p + 1) * pair], scaled.at[at]))
    got_more = fetch(more, s_sem)
    count = 2
    tile = down.shape[0] // count
    tiles = [slice(n * tile, (n + 1) * tile) for n in range(count)]
    got_down = [fetch([(down.at[rows], down_s.at[rows])], d_sem.at[n]) for n, rows in enumerate(tiles)]
    got()
    to_image_order(chooser, joined, 0, turned)
    own_s[1] = turned[:, :128]
    got_more()
    for p in range(4):
        here = slice(p * pair, (p + 1) * pair)
        place = order[4 + p] * pair
        turned[here, :] = turned[here, :] * scales_s[pl.ds(pl.multiple_of(place, 8), pair), :1]
        scaled[pl.ds(pl.multiple_of(place, 16), pair), :] = turned[here, :].astype(BF16)
    split_parity(turned, core[0], 4, keep_s, give_s)
    waits = [fetch([(give_s, give), (keep_s, keep)], give_sem)]
    for n, rows in enumerate(tiles):
        got_down[n]()
        value = jnp.dot(down_s[rows, :], scaled[...], preferred_element_type=F32)
        pre_s[rows, :] = (value * slope_s[rows, :].astype(F32)).astype(BF16)
        waits.append(fetch([(pre_s.at[rows], pre.at[rows])], pre_sem.at[n]))
    for p in range(8):
        at = pl.ds(pl.multiple_of(order[p] * pair, 8), pair)
        own_rows[at, :] = own_s[p // 4, (p % 4) * pair : (p % 4 + 1) * pair, :]
    for t in range(own_rows.shape[0] // 128):
        here = slice(t * 128, (t + 1) * 128)
        own_out[:, here] = own_rows[here, :].T[: own_out.shape[0]].astype(BF16)
    waits.append(fetch([(own_out, own_grad)], own_sem))
    for wait in waits:
        wait()


def middle(core, order, scales, chooser, own_first, scaled_1, slope, down, ins):
    hidden, width = down.shape
    rows, cols = chooser.shape[0], width // 2
    turned = ((cols // 2, rows), BF16)
    outs = [turned, turned, ((rows // MEMBERS, width), BF16), ((hidden, rows), BF16)]
    return pl.pallas_call(
        middle_kernel,
        out_shape=[jax.ShapeDtypeStruct(shape, kind) for shape, kind in outs],
        in_specs=[SMEM, SMEM] + [HBM] * (6 + len(ins)),
        out_specs=[HBM] * 4,
        scratch_shapes=[
            pltpu.VMEM((rows, cols), BF16),
            pltpu.VMEM((cols, rows), F32),
            pltpu.VMEM((width, rows), BF16),
            pltpu.VMEM((cols // 2, rows), BF16),
            pltpu.VMEM((cols // 2, rows), BF16),
            pltpu.VMEM((rows, rows), BF16),
            pltpu.VMEM((2, cols, 128), F32),
            pltpu.VMEM((width, 128), F32),
            pltpu.VMEM((rows // MEMBERS, width), BF16),
            pltpu.VMEM((hidden, rows), BF16),
            pltpu.VMEM((hidden, width), BF16),
            pltpu.VMEM((hidden, rows), BF16),
            pltpu.VMEM((width, 128), F32),
        ]
        + [pltpu.SemaphoreType.DMA((n,)) for n in (8, 5)]
        + [pltpu.SemaphoreType.DMA((2, 1))]
        + [pltpu.SemaphoreType.DMA((n,)) for n in (2, 1)]
        + [pltpu.SemaphoreType.DMA((2, 1))],
        compiler_params=params(52),
        cost_estimate=cost(10**10, 10**7),
    )(core, order, scales, chooser, own_first, scaled_1, slope, down, *ins)


def blocks_kernel(jobs, sums, *refs):
    group = 800
    count = len(jobs)
    if sums:
        refs, (pre_s, up_s, sums_s, more_s, up_sem, sums_sem, more_sem) = refs[:-7], refs[-7:]
        pre, up, more_up, more_down = refs[5 * count : 5 * count + 4]
        refs = refs[: 5 * count] + refs[5 * count + 4 :]
    ins, refs = refs[: 5 * count], refs[5 * count :]
    total = sum(len(sizes) for parts in jobs for _, _, sizes in parts)
    pieces = sum(len(parts) for parts in jobs)
    scratch = refs[-(3 * count + 3 * pieces) :]
    outs, sums_outs = refs[:total], refs[total : total + 3]
    todo = []
    at_out = at = 0
    for k, parts in enumerate(jobs):
        slots, left, left_got, right, right_got = ins[5 * k : 5 * k + 5]
        left_s, l_sem, r_sem = scratch[at : at + 3]
        at += 3
        rows_in = left.shape[1]
        waits_r = []
        each = []
        for i, (first, cols, sizes) in enumerate(parts):
            right_s, stage, sem = scratch[at : at + 3]
            at += 3
            here = slice(first, first + cols)
            waits_r.append(
                fetch(
                    [
                        (right.at[here], right_s.at[:cols, :rows_in]),
                        (right_got.at[here], right_s.at[:cols, rows_in:]),
                    ],
                    r_sem.at[i],
                )
            )
            each.append((i, cols, sizes, right_s, stage, sem, outs[at_out : at_out + len(sizes)]))
            at_out += len(sizes)
        waits_l = []
        for g in range(left.shape[0] // group):
            here = slice(g * group, (g + 1) * group)
            waits_l.append(
                fetch(
                    [
                        (left.at[here], left_s.at[here, :rows_in]),
                        (left_got.at[here], left_s.at[here, rows_in:]),
                    ],
                    l_sem.at[g],
                )
            )
        todo.append((slots, left_s, waits_l, waits_r, each))
    if sums:
        got_more = fetch(
            [
                (more_up.at[0], more_s.at[0]),
                (more_down.at[0], more_s.at[1]),
                (more_down.at[1], more_s.at[2]),
                (more_up.at[1], more_s.at[3]),
            ],
            more_sem,
        )
        got_up = fetch([(pre, pre_s), (up, up_s)], up_sem)
    for slots, left_s, waits_l, waits_r, each in todo:
        for i, cols, sizes, right_s, stage, sem, targets in each:
            waits_r[i]()
            block = stage.shape[1]
            per = group // block
            for g in range(len(waits_l)):
                if i == 0:
                    waits_l[g]()
                product = by_last(left_s[g * group : (g + 1) * group, :], right_s[...])
                for b in range(per):
                    j = g * per + b
                    value = product[b * block : (b + 1) * block, :cols]
                    if sums and i == 0:
                        if j == 0:
                            got_more()
                        value = value + more_s[j].astype(F32)
                    stage[j] = value.astype(BF16)
                    slot = slots[i, j]
                    first = 0
                    for out, size in zip(targets, sizes):

                        @pl.when((slot >= first) & (slot < first + size))
                        def _(out=out, first=first, j=j, slot=slot, stage=stage, sem=sem):
                            pltpu.make_async_copy(
                                stage.at[j], out.at[slot - first], sem.at[j]
                            ).start()

                        first += size
    if sums:
        got_up()
        for first in range(0, up.shape[1], 512):
            here = slice(first, min(first + 512, up.shape[1]))
            sums_s[:, here] = lax.dot_general(
                pre_s[...], up_s[:, here], (((0,), (0,)), ((), ())), preferred_element_type=F32
            ).astype(BF16)
        eighth = sums_s.shape[0] // MEMBERS
        half = eighth // 2
        sums_out, first_out, last_out = sums_outs
        copies = [(sums_s, sums_out)]
        for i in range(2):
            at = (4 + i) * eighth
            here = slice(i * half, (i + 1) * half)
            copies.append((sums_s.at[at : at + half], first_out.at[here]))
            copies.append((sums_s.at[at + half : at + eighth], last_out.at[here]))
        fetch(copies, sums_sem)()
    for _, _, _, _, each in todo:
        for _, _, _, _, stage, sem, targets in each:
            for j in range(stage.shape[0]):
                pltpu.make_async_copy(stage.at[j], targets[0].at[0], sem.at[j]).wait()


def grad_blocks(jobs, sums=()):
    block = 200
    specs, ins, outs, scratch = [], [], [], []
    for slots, left, left_got, right, right_got, parts in jobs:
        width, rows = left.shape
        specs += [SMEM] + [HBM] * 4
        ins += [slots, left, left_got, right, right_got]
        scratch += [
            pltpu.VMEM((width, 2 * rows), BF16),
            pltpu.SemaphoreType.DMA((width // 800, 2)),
            pltpu.SemaphoreType.DMA((len(parts), 2)),
        ]
        for _, cols, sizes in parts:
            outs += [jax.ShapeDtypeStruct((size, block, cols), BF16) for size in sizes]
            scratch += [
                pltpu.VMEM((-(-cols // 256) * 256, 2 * rows), BF16),
                pltpu.VMEM((width // block, block, cols), BF16),
                pltpu.SemaphoreType.DMA((width // block,)),
            ]
    lists = [job[-1] for job in jobs]
    if sums:
        (hidden, rows), width = sums[0].shape, sums[1].shape[1]
        specs += [HBM] * 4
        ins += list(sums)
        outs.append(jax.ShapeDtypeStruct((rows, width), BF16))
        outs += [jax.ShapeDtypeStruct((rows // MEMBERS, width), BF16)] * 2
        scratch += [
            pltpu.VMEM((hidden, rows), BF16),
            pltpu.VMEM((hidden, width), BF16),
            pltpu.VMEM((rows, width), BF16),
            pltpu.VMEM((4, *sums[2].shape[1:]), BF16),
            pltpu.SemaphoreType.DMA((2,)),
            pltpu.SemaphoreType.DMA((5,)),
            pltpu.SemaphoreType.DMA((4,)),
        ]

    def kernel(*refs):
        blocks_kernel(lists, bool(sums), *refs)

    return pl.pallas_call(
        kernel,
        out_shape=outs,
        in_specs=specs,
        out_specs=[HBM] * len(outs),
        scratch_shapes=scratch,
        compiler_params=params(52),
        cost_estimate=cost(10**10, 10**7),
    )(*ins)


def z_order(z, xl):
    pairs = [(2, 0), (1, 1), (2, 1), (3, 0), (1, 0), (3, 1), (0, 0), (0, 1)]
    return [((z + dz) % Z) * XL + x for dz, x in pairs]


def x_order(z, xl):
    pairs = [(dz, dx) for dx in (1, 0) for dz in (2, 1, 3, 0)]
    return [((z + dz) % Z) * XL + (xl + dx) % XL for dz, dx in pairs]


def slots_of(order):
    order = jnp.stack(order).astype(jnp.int32)
    index = jnp.arange(order.shape[0], dtype=jnp.int32)
    return jnp.sum(jnp.where(order[None, :] == index[:, None], index[None, :], 0), 1)


def beside(*parts):
    return jnp.concatenate(parts, 1)


def below(*parts):
    return jnp.concatenate(parts, 0)


def on_device(
    lm_grad, encoder_row, patch_count, hidden_in, norm_gain, layer_scale, up_weight, down_weight
):
    tok_rows, width = hidden_in.shape
    rest = up_weight.shape[1] - CUT
    up_turned, down_turned = up_weight.T, down_weight.T
    group_len = tok_rows * MEMBERS
    per_pair = tok_rows // BLOCKS
    half = tok_rows // 2
    z, xl, core = lax.axis_index("z"), lax.axis_index("xl"), lax.axis_index("core")
    y, xh = lax.axis_index("y"), lax.axis_index("xh")
    group = (z * XL + xl) * CORE + core
    core_at = core.reshape(1).astype(jnp.int32)
    z_slots, x_slots = slots_of(z_order(z, xl)), slots_of(x_order(z, xl))

    inputs = hidden_in.astype(F32)
    inverse_rms = lax.rsqrt(jnp.mean(inputs * inputs, -1, keepdims=True) + 1e-06)
    normed_own = (inputs * inverse_rms * norm_gain).astype(BF16)

    n_prev = shift(normed_own, "y", Y, 1)
    n_next = shift(normed_own, "y", Y, -1)
    n_other = shift(normed_own, "xh", XH, 1)

    image, place = encoder_row // group_len, encoder_row % group_len
    index = jnp.arange(tok_rows, dtype=jnp.int32)
    same = (image[:, None] == image[None, :]) & (index[None, :] < index[:, None])
    slot = image * per_pair + jnp.sum(same.astype(jnp.int32), 1)
    sorter = (slot[None, :] == index[:, None]).astype(BF16)
    column = jnp.arange(ID_COLS, dtype=jnp.int32)[None, :]
    tags = jnp.where(
        column == 0,
        (place // ID_BASE)[:, None],
        jnp.where(column == 1, (place % ID_BASE)[:, None], 0),
    ).astype(BF16)
    ordered = jnp.dot(sorter, beside(lm_grad, tags), preferred_element_type=F32).astype(BF16)
    arrived = lax.all_to_all(
        ordered.reshape(BLOCKS, per_pair, width + ID_COLS),
        ("z", "xl", "core"),
        split_axis=0,
        concat_axis=0,
    ).reshape(tok_rows, width + ID_COLS)

    n_prev, n_next, n_other = together(n_prev, n_next, n_other)
    mix_prev = shift(below(n_other, n_prev[:half]), "y", Y, 1)
    mix_next = shift(below(n_other, n_next[half:]), "y", Y, -1)
    g_other = shift(arrived, "xh", XH, 1)
    block = jnp.arange(MEMBERS, dtype=jnp.int32)
    member = ((block // XH + y) % Y) * XH + (block % XH + xh) % XH
    positions = (member[:, None] * tok_rows + index[None, :]).reshape(group_len, 1)
    limit = lax.dynamic_index_in_dim(patch_count, group, 0, keepdims=False)
    positions = jnp.where(positions < limit, positions, -1).astype(F32)
    scale_column = jnp.broadcast_to(layer_scale[:, None], (width, 128))
    mix_prev, mix_next, g_other, arrived, positions, scale_column = together(
        mix_prev, mix_next, g_other, arrived, positions, scale_column
    )

    far_a = shift(mix_prev[:half], "y", Y, 1)
    far_b = shift(mix_next[half:tok_rows], "y", Y, -1)
    order = jnp.stack(z_order(z, xl)).astype(jnp.int32)
    g_1, g_2 = prepare(order, arrived, g_other, width)
    far_a, far_b, g_1, g_2 = together(far_a, far_b, g_1, g_2)

    g_prev_1, g_next_1 = shift(g_1, "y", Y, 1), shift(g_1, "y", Y, -1)
    g_prev_2, g_next_2 = shift(g_2, "y", Y, 1), shift(g_2, "y", Y, -1)
    act, slope, n_keep, n_give = assemble_normed(
        core_at, (normed_own, n_other, n_next, n_prev, mix_prev, mix_next, far_a, far_b), up_turned
    )
    g_prev_1, g_next_1, g_prev_2, g_next_2, act, n_give = together(
        g_prev_1, g_next_1, g_prev_2, g_next_2, act, n_give
    )

    f_prev_1 = shift(g_prev_1[:tok_rows], "y", Y, 1)
    f_next_1 = shift(g_next_1[tok_rows:], "y", Y, -1)
    f_prev_2 = shift(g_prev_2[:tok_rows], "y", Y, 1)
    f_next_2 = shift(g_next_2[tok_rows:], "y", Y, -1)
    act_got = shift(act, "core", CORE, 1)
    n_got = shift(n_give, "core", CORE, 1)
    s_1, d_keep_1, d_give_1, own_first, chooser = route_first(
        core_at, order, scale_column, positions, (g_1, g_prev_1, g_next_1, f_prev_1, f_next_1)
    )
    d_got_1 = shift(d_give_1, "core", CORE, 1)
    here = xl == 0
    straight = jnp.arange(4, dtype=jnp.int32)
    slots_1 = jnp.stack([straight, jnp.where(here, jnp.array([2, 1, 0, 3]), jnp.array([0, 3, 2, 1]))])
    slots_2 = jnp.stack([straight, jnp.where(here, jnp.array([2, 0, 3, 1]), jnp.array([0, 2, 1, 3]))])
    slots_1, slots_2 = slots_1.astype(jnp.int32), slots_2.astype(jnp.int32)
    d_got_1, act_got, n_got = together(d_got_1, act_got, n_got)
    d_up, d_down, d_out_1, d_mine_1 = grad_blocks(
        [(slots_1, d_keep_1, d_got_1, act, act_got, ((0, CUT, (2, 2)), (CUT, rest, (2, 2))))]
    )
    d_prev, d_next = shift(d_up, "z", Z, 1), shift(d_down, "z", Z, -1)
    d_x_1 = shift(d_out_1, "xl", XL, 1)
    f_prev_2, f_next_2, d_mine_1 = together(f_prev_2, f_next_2, d_mine_1)

    d_keep_2, d_give_2, own_grad, pre = middle(
        core_at, order, scale_column, chooser, own_first, s_1, slope, down_turned,
        (g_2, g_prev_2, g_next_2, f_prev_2, f_next_2),
    )
    d_got_2 = shift(d_give_2, "core", CORE, 1)
    d_got_2, d_prev, d_next = together(d_got_2, d_prev, d_next)
    pre_got = shift(pre, "core", CORE, 1)
    d_acc_prev, d_acc_next, d_kept, d_out_2, d_mine_2, parts, p_prev, p_next = grad_blocks(
        [(slots_2, d_keep_2, d_got_2, act, act_got, ((0, CUT, (1, 1, 2)), (CUT, rest, (2, 2))))],
        (pre, up_turned, d_prev, d_next),
    )
    pre_got, parts = together(pre_got, parts)

    d_acc_prev, d_acc_next = shift(d_acc_prev, "z", Z, 1), shift(d_acc_next, "z", Z, -1)
    d_x_2 = shift(d_out_2, "xl", XL, 1)
    u_up, u_down, u_kept, u_out, u_mine = grad_blocks(
        [
            (
                jnp.stack([z_slots, x_slots]), n_keep, n_got, pre, pre_got,
                ((0, UP_CUT, (2, 2, 4)), (UP_CUT, rest + CUT - UP_CUT, (4, 4))),
            )
        ]
    )
    d_acc_prev, d_acc_next, d_x_1, d_x_2, u_mine, parts, p_prev, p_next = together(
        d_acc_prev, d_acc_next, d_x_1, d_x_2, u_mine, parts, p_prev, p_next
    )

    u_prev, u_next = shift(u_up, "z", Z, 1), shift(u_down, "z", Z, -1)
    u_x = shift(u_out, "xl", XL, 1)
    blocks = parts.reshape(MEMBERS, tok_rows, width)
    p_prev, p_next = shift(p_prev, "y", Y, 1), shift(p_next, "y", Y, -1)
    sum_0, sum_1 = add(d_kept[0], d_acc_prev[0]), add(d_kept[1], d_acc_next[0])
    d_own, d_give = jnp.where(here, sum_0, sum_1), jnp.where(here, sum_1, sum_0)
    o_prev, o_next = (
        below(add(blocks[3][:half], p_prev[half:]), blocks[3][half:]),
        below(blocks[7][:half], add(blocks[7][half:], p_next[half:])),
    )
    d_give, u_x, _, _ = together(d_give, u_x, o_prev, o_next)
    o_prev, o_next = shift(o_prev, "y", Y, 1), shift(o_next, "y", Y, -1)
    d_other = shift(d_give, "xl", XL, 1)

    m_prev = shift(add(u_kept[0], u_prev[0]), "z", Z, 1)
    m_next = shift(add(u_kept[1], u_next[0]), "z", Z, -1)
    r_other = shift(add(blocks[1], o_prev, o_next), "xh", XH, 1)
    d_other, p_prev, p_next, o_prev, o_next = together(d_other, p_prev, p_next, o_prev, o_next)
    r_prev = shift(below(add(blocks[2][:half], p_prev[:half]), blocks[2][half:]), "y", Y, 1)
    r_next = shift(below(blocks[6][:half], add(blocks[6][half:], p_next[:half])), "y", Y, -1)

    sum_0 = add(u_kept[2], u_next[1], m_prev)
    sum_1 = add(u_kept[3], u_prev[1], m_next)
    u_own, u_give = jnp.where(here, sum_0, sum_1), jnp.where(here, sum_1, sum_0)
    u_other = shift(u_give, "xl", XL, 1)
    cut = -(-d_x_1.shape[1] // 16) * 8
    u_x, d_x_2, r_prev, r_next, u_own, d_other = together(
        u_x, d_x_2, r_prev, r_next, u_own, d_other
    )
    two, side_1, side_2 = (
        add(d_mine_1[0], d_x_1[0]), add(d_mine_1[1], d_x_1[1]), add(d_mine_2[0], d_x_2[0])
    )
    one, three = jnp.where(here, side_2, side_1), jnp.where(here, side_1, side_2)
    two, one, three = (
        beside(both, add(u_mine[i], u_x[i])) for i, both in enumerate((two, one, three))
    )
    b_here = beside(add32(d_mine_2[1], d_x_2[1]), add32(u_mine[3], u_x[3]))
    b_prev = shift(below(two[:cut], one[cut:]), "z", Z, 1)
    b_next = shift(below(three[:cut], two[cut:]), "z", Z, -1)
    c_prev = shift(add(one[:cut], b_prev[:cut]), "z", Z, 1)
    c_next = shift(add(three[cut:], b_next[cut:]), "z", Z, -1)
    r_prev, r_next, r_other, b_prev = together(r_prev, r_next, r_other, b_prev)
    down_a, up_a = add32(d_own, d_other), add32(u_own, u_other)
    b_total = below(
        add32(b_here[:cut], b_next[:cut], c_prev), add32(b_here[cut:], b_prev[cut:], c_next)
    )
    down_b, up_b = b_total[:, :rest], b_total[:, rest:]
    normed_grad = add32(blocks[0], r_prev, r_next, r_other)
    weighted = norm_gain * normed_grad
    input_grad = (
        own_grad.astype(F32)
        + inverse_rms * weighted
        - inputs * inverse_rms**3 * jnp.mean(weighted * inputs, -1, keepdims=True)
    ).astype(BF16)
    grad_scale = 1.0 / math.sqrt(group_len * BLOCKS)
    return (
        input_grad,
        (beside(up_a, up_b) * grad_scale).astype(BF16),
        (beside(down_a, down_b) * grad_scale).astype(BF16),
    )


def solution(mesh):
    fine = Mesh(mesh.devices.reshape(Z, XL, CORE, Y, XH), AXES)
    dp, tensor = AXES[:3], AXES[3:]
    in_specs = (
        P(AXES, None),
        P(AXES),
        P(),
        P(AXES, None),
        P(),
        P(),
        P(None, tensor),
        P(None, tensor),
    )
    out_specs = (P(AXES, None), P(dp, tensor), P(dp, tensor))
    return jax.shard_map(
        on_device, mesh=fine, in_specs=in_specs, out_specs=out_specs, check_vma=False
    )
```

```python
import math

import jax
import jax.numpy as jnp
from jax import lax
from jax.experimental import pallas as pl
from jax.experimental.pallas import tpu as pltpu
from jax.sharding import Mesh, PartitionSpec as P

F32 = jnp.float32
BF16 = jnp.bfloat16
Z, XL, CORE, Y, XH = 4, 2, 2, 4, 2
AXES = ("z", "xl", "core", "y", "xh")
MEMBERS = Y * XH
BLOCKS = Z * XL * CORE
ID_COLS = 128
ID_BASE = 32
CUT = 1152
UP_CUT = 1152
MIB = 1024 * 1024
VMEM = pl.BlockSpec(memory_space=pltpu.VMEM)
SMEM = pl.BlockSpec(memory_space=pltpu.SMEM)
ANY = pl.BlockSpec(memory_space=pl.ANY)
HBM = pl.BlockSpec(memory_space=pltpu.HBM)


def params(mib):
    return pltpu.CompilerParams(vmem_limit_bytes=mib * MIB)


def cost(flops, moved, special=0):
    return pl.CostEstimate(flops=flops, bytes_accessed=moved, transcendentals=special)


def shift(value, axis, size, step):
    return lax.ppermute(value, axis, [(i, (i + step) % size) for i in range(size)])


def add32(*terms):
    total = terms[0].astype(F32)
    for term in terms[1:]:
        total = total + term.astype(F32)
    return total


def add(*terms):
    return add32(*terms).astype(BF16)


def together(*values):
    return lax.optimization_barrier(values)


def fetch(pieces, sem):
    copies = [pltpu.make_async_copy(src, dst, sem.at[i]) for i, (src, dst) in enumerate(pieces)]
    for copy in copies:
        copy.start()

    def wait():
        for copy in copies:
            copy.wait()

    return wait


def pieces_of(listed, out):
    at, pieces = 0, []
    for ref, first, rows in listed:
        pieces.append((ref.at[first : first + rows], out.at[at : at + rows]))
        at += rows
    return pieces


def split_parity(turned, core, pairs, keep, give):
    rows = keep.shape[0] // pairs
    for two in range(pairs // 2):
        for out, parity in ((keep, core), (give, 1 - core)):
            blocks = [
                turned[pl.ds(pl.multiple_of((2 * b + parity) * rows, 8), rows), :]
                for b in (2 * two, 2 * two + 1)
            ]
            out[2 * two * rows : (2 * two + 2) * rows, :] = jnp.concatenate(blocks, 0).astype(BF16)


def by_last(left, right):
    return lax.dot_general(left, right, (((1,), (1,)), ((), ())), preferred_element_type=F32)


def normed_kernel(core, *refs):
    ins, weight, (act, slope, keep, give) = refs[:8], refs[8], refs[9:13]
    normed, turned, held, act_s, slope_s, keep_s, give_s, in_sem, w_sem, out_sem, sem = refs[13:]
    own, other, nxt, prev, mix_prev, mix_next, far_a, far_b = ins
    full = own.shape[0]
    half = full // 2
    listed = [(own, 0, full), (other, 0, full), (nxt, 0, full), (mix_next, 0, full)]
    listed += [(mix_prev, full, half), (mix_next, full, half), (far_a, 0, half), (far_b, 0, half)]
    listed += [(prev, 0, full), (mix_prev, 0, full)]
    fetched = fetch(pieces_of(listed, normed), in_sem)
    tile = held.shape[1]
    count = held.shape[0]
    tiles = [slice(n * tile, (n + 1) * tile) for n in range(count)]
    weights = [fetch([(weight.at[tiles[n]], held.at[n])], w_sem.at[n]) for n in range(count)]
    fetched()
    for t in range(normed.shape[1] // 128):
        cols = slice(t * 128, (t + 1) * 128)
        turned[cols, :] = normed[:, cols].astype(F32).T
    split_parity(turned, core[0], BLOCKS // 2, keep_s, give_s)
    waits = [fetch([(give_s, give), (keep_s, keep)], out_sem)]
    for n, rows in enumerate(tiles):
        weights[n]()
        value = by_last(held[n], normed[...])
        below = 0.5 * (1.0 + lax.erf(value * 0.7071067811865476))
        act_s[rows, :] = (value * below).astype(BF16)
        slope_s[rows, :] = (
            below + value * jnp.exp(-0.5 * value * value) * 0.3989422804014327
        ).astype(BF16)
        waits.append(
            fetch([(act_s.at[rows], act.at[rows]), (slope_s.at[rows], slope.at[rows])], sem.at[n])
        )
    for wait in waits:
        wait()


def assemble_normed(core, ins, weight):
    rows, width = ins[0].shape[0] * MEMBERS, ins[0].shape[1]
    hidden = weight.shape[0]
    count = 4
    outs = [((hidden, rows), BF16)] * 2 + [((width // 2, rows), BF16)] * 2
    return pl.pallas_call(
        normed_kernel,
        out_shape=[jax.ShapeDtypeStruct(shape, kind) for shape, kind in outs],
        in_specs=[SMEM] + [HBM] * (len(ins) + 1),
        out_specs=[HBM] * 4,
        scratch_shapes=[
            pltpu.VMEM((rows, width), BF16),
            pltpu.VMEM((width, rows), F32),
            pltpu.VMEM((count, hidden // count, width), BF16),
        ]
        + [pltpu.VMEM(shape, kind) for shape, kind in outs]
        + [pltpu.SemaphoreType.DMA((n,)) for n in (10,)]
        + [pltpu.SemaphoreType.DMA((count, 1)), pltpu.SemaphoreType.DMA((2,))]
        + [pltpu.SemaphoreType.DMA((count, 2))],
        compiler_params=params(52),
        cost_estimate=cost(10**10, 10**7),
    )(core, *ins, weight)


def prepare_kernel(order, own, other, first, second, rows_s, turned, sorted_s, *refs):
    outs_s, in_sem, sem = refs[:2], refs[2], refs[3]
    half = own.shape[0] // 2
    listed = [(own, 0, half), (other, 0, half), (own, half, half), (other, half, half)]
    fetch(pieces_of(listed, rows_s), in_sem)()
    width = turned.shape[0]
    pair = width // (BLOCKS // 2)
    for t in range(width // 128):
        cols = slice(t * 128, (t + 1) * 128)
        turned[cols, :] = rows_s[:, cols].astype(F32).T
    waits = []
    for h, out in enumerate((first, second)):
        for p in range(4):
            at = pl.ds(pl.multiple_of(order[4 * h + p] * pair, 8), pair)
            sorted_s[p * pair : (p + 1) * pair, :] = turned[at, :]
        cols = width // 2
        lead = 0 if h else ID_COLS
        for first_col in range(0, cols, 128):
            last = min(first_col + 128, cols)
            outs_s[h][:, lead + first_col : lead + last] = (
                sorted_s[first_col : first_col + 128, :].T[:, : last - first_col].astype(BF16)
            )
        if h == 0:
            outs_s[h][:, :lead] = rows_s[:, width : width + ID_COLS]
        waits.append(fetch([(outs_s[h], out)], sem.at[h]))
    for wait in waits:
        wait()


def prepare(order, own, other, width):
    rows = 2 * own.shape[0]
    cols = width // 2
    return pl.pallas_call(
        prepare_kernel,
        out_shape=[
            jax.ShapeDtypeStruct((rows, cols + ID_COLS), BF16),
            jax.ShapeDtypeStruct((rows, cols), BF16),
        ],
        in_specs=[SMEM, HBM, HBM],
        out_specs=[HBM, HBM],
        scratch_shapes=[
            pltpu.VMEM((rows, width + ID_COLS), BF16),
            pltpu.VMEM((width, rows), F32),
            pltpu.VMEM((-(-cols // 128) * 128, rows), F32),
            pltpu.VMEM((rows, cols + ID_COLS), BF16),
            pltpu.VMEM((rows, cols), BF16),
            pltpu.SemaphoreType.DMA((4,)),
            pltpu.SemaphoreType.DMA((2, 1)),
        ],
        compiler_params=params(52),
        cost_estimate=cost(10**8, 10**6),
    )(order, own, other)


def joined_pieces(ins, joined):
    at, pieces = 0, []
    for ref in ins:
        rows = ref.shape[0]
        pieces.append((ref, joined.at[at : at + rows]))
        at += rows
    return pieces


def to_image_order(chooser, joined, lead, scale, turned, own):
    cols = turned.shape[0]
    for first in range(0, cols, 640):
        last = min(first + 640, cols)
        grads = jnp.dot(
            chooser[...], joined[:, lead + first : lead + last], preferred_element_type=F32
        )
        own[first:last, :] = grads[:128].T
        turned[first:last, :] = (grads * scale[:, first:last]).T


def first_kernel(core, order, scales, positions, *refs):
    ins, (scaled, keep, give, own_turned, chooser_out) = refs[:5], refs[5:10]
    joined, turned, scaled_s, keep_s, give_s, chooser, own_s, in_sem, sem, give_sem = refs[10:]
    del order
    fetch(joined_pieces(ins, joined), in_sem)()
    tags = joined[:, :ID_COLS].astype(F32).T
    places = tags[0:1, :] * ID_BASE + tags[1:2, :]
    chooser[...] = (positions[...] == places).astype(F32).astype(BF16)
    to_image_order(chooser, joined, ID_COLS, scales[0:1, :], turned, own_s)
    waits = [fetch([(own_s, own_turned), (chooser, chooser_out)], sem)]
    scaled_s[...] = turned[...].astype(BF16)
    split_parity(turned, core[0], 4, keep_s, give_s)
    waits.append(fetch([(give_s, give), (keep_s, keep), (scaled_s, scaled)], give_sem))
    for wait in waits:
        wait()


def route_first(core, order, scales, positions, ins):
    rows, cols = positions.shape[0], scales.shape[1]
    turned = ((cols // 2, rows), BF16)
    outs = [((cols, rows), BF16), turned, turned, ((cols, 128), F32), ((rows, rows), BF16)]
    return pl.pallas_call(
        first_kernel,
        out_shape=[jax.ShapeDtypeStruct(shape, kind) for shape, kind in outs],
        in_specs=[SMEM, SMEM, VMEM, VMEM] + [HBM] * len(ins),
        out_specs=[HBM] * 5,
        scratch_shapes=[
            pltpu.VMEM((rows, cols + ID_COLS), BF16),
            pltpu.VMEM((cols, rows), F32),
            pltpu.VMEM((cols, rows), BF16),
            pltpu.VMEM((cols // 2, rows), BF16),
            pltpu.VMEM((cols // 2, rows), BF16),
            pltpu.VMEM((rows, rows), BF16),
            pltpu.VMEM((cols, 128), F32),
        ]
        + [pltpu.SemaphoreType.DMA((n,)) for n in (5, 2, 3)],
        compiler_params=params(52),
        cost_estimate=cost(10**9, 10**7),
    )(core, order, scales, positions, *ins)


def middle_kernel(core, order, *refs):
    scales, chooser_in, own_first, scaled_1, slope, down = refs[:6]
    ins, (keep, give, own_grad, pre) = refs[6:11], refs[11:15]
    joined, turned, scaled, keep_s, give_s, chooser, own_s, own_rows, own_out = refs[15:24]
    slope_s, down_s, pre_s = refs[24:27]
    in_sem, s_sem, d_sem, give_sem, own_sem, pre_sem = refs[27:]
    cols = joined.shape[1]
    pair = cols // 4
    got = fetch(
        joined_pieces(ins, joined)
        + [(chooser_in, chooser), (own_first, own_s.at[0])],
        in_sem,
    )
    more = [(slope, slope_s)]
    for p in range(4):
        at = pl.ds(pl.multiple_of(order[p] * pair, 16), pair)
        more.append((scaled_1.at[p * pair : (p + 1) * pair], scaled.at[at]))
    got_more = fetch(more, s_sem)
    count = 2
    tile = down.shape[0] // count
    tiles = [slice(n * tile, (n + 1) * tile) for n in range(count)]
    got_down = [fetch([(down.at[rows], down_s.at[rows])], d_sem.at[n]) for n, rows in enumerate(tiles)]
    got()
    to_image_order(chooser, joined, 0, scales[1:2, :], turned, own_s.at[1])
    got_more()
    for p in range(4):
        here = slice(p * pair, (p + 1) * pair)
        place = order[4 + p] * pair
        scaled[pl.ds(pl.multiple_of(place, 16), pair), :] = turned[here, :].astype(BF16)
    split_parity(turned, core[0], 4, keep_s, give_s)
    waits = [fetch([(give_s, give), (keep_s, keep)], give_sem)]
    for n, rows in enumerate(tiles):
        got_down[n]()
        value = jnp.dot(down_s[rows, :], scaled[...], preferred_element_type=F32)
        pre_s[rows, :] = (value * slope_s[rows, :].astype(F32)).astype(BF16)
        waits.append(fetch([(pre_s.at[rows], pre.at[rows])], pre_sem.at[n]))
    for p in range(8):
        at = pl.ds(pl.multiple_of(order[p] * pair, 8), pair)
        own_rows[at, :] = own_s[p // 4, (p % 4) * pair : (p % 4 + 1) * pair, :]
    for t in range(own_rows.shape[0] // 128):
        here = slice(t * 128, (t + 1) * 128)
        own_out[:, here] = own_rows[here, :].T[: own_out.shape[0]].astype(BF16)
    waits.append(fetch([(own_out, own_grad)], own_sem))
    for wait in waits:
        wait()


def middle(core, order, scales, chooser, own_first, scaled_1, slope, down, ins):
    hidden, width = down.shape
    rows, cols = chooser.shape[0], width // 2
    turned = ((cols // 2, rows), BF16)
    outs = [turned, turned, ((rows // MEMBERS, width), BF16), ((hidden, rows), BF16)]
    return pl.pallas_call(
        middle_kernel,
        out_shape=[jax.ShapeDtypeStruct(shape, kind) for shape, kind in outs],
        in_specs=[SMEM, SMEM, VMEM] + [HBM] * (5 + len(ins)),
        out_specs=[HBM] * 4,
        scratch_shapes=[
            pltpu.VMEM((rows, cols), BF16),
            pltpu.VMEM((cols, rows), F32),
            pltpu.VMEM((width, rows), BF16),
            pltpu.VMEM((cols // 2, rows), BF16),
            pltpu.VMEM((cols // 2, rows), BF16),
            pltpu.VMEM((rows, rows), BF16),
            pltpu.VMEM((2, cols, 128), F32),
            pltpu.VMEM((width, 128), F32),
            pltpu.VMEM((rows // MEMBERS, width), BF16),
            pltpu.VMEM((hidden, rows), BF16),
            pltpu.VMEM((hidden, width), BF16),
            pltpu.VMEM((hidden, rows), BF16),
        ]
        + [pltpu.SemaphoreType.DMA((n,)) for n in (7, 5)]
        + [pltpu.SemaphoreType.DMA((2, 1))]
        + [pltpu.SemaphoreType.DMA((n,)) for n in (2, 1)]
        + [pltpu.SemaphoreType.DMA((2, 1))],
        compiler_params=params(52),
        cost_estimate=cost(10**10, 10**7),
    )(core, order, scales, chooser, own_first, scaled_1, slope, down, *ins)


def blocks_kernel(jobs, sums, *refs):
    group = 800
    count = len(jobs)
    if sums:
        refs, (pre_s, up_s, sums_s, more_s, up_sem, sums_sem, more_sem) = refs[:-7], refs[-7:]
        pre, up, more_up, more_down = refs[5 * count : 5 * count + 4]
        refs = refs[: 5 * count] + refs[5 * count + 4 :]
    ins, refs = refs[: 5 * count], refs[5 * count :]
    total = sum(len(sizes) for parts in jobs for _, _, sizes in parts)
    pieces = sum(len(parts) for parts in jobs)
    scratch = refs[-(3 * count + 3 * pieces) :]
    outs, sums_outs = refs[:total], refs[total : total + 3]
    todo = []
    at_out = at = 0
    for k, parts in enumerate(jobs):
        slots, left, left_got, right, right_got = ins[5 * k : 5 * k + 5]
        left_s, l_sem, r_sem = scratch[at : at + 3]
        at += 3
        rows_in = left.shape[1]
        waits_r = []
        each = []
        for i, (first, cols, sizes) in enumerate(parts):
            right_s, stage, sem = scratch[at : at + 3]
            at += 3
            here = slice(first, first + cols)
            waits_r.append(
                fetch(
                    [
                        (right.at[here], right_s.at[:cols, :rows_in]),
                        (right_got.at[here], right_s.at[:cols, rows_in:]),
                    ],
                    r_sem.at[i],
                )
            )
            each.append((i, cols, sizes, right_s, stage, sem, outs[at_out : at_out + len(sizes)]))
            at_out += len(sizes)
        waits_l = []
        for g in range(left.shape[0] // group):
            here = slice(g * group, (g + 1) * group)
            waits_l.append(
                fetch(
                    [
                        (left.at[here], left_s.at[here, :rows_in]),
                        (left_got.at[here], left_s.at[here, rows_in:]),
                    ],
                    l_sem.at[g],
                )
            )
        todo.append((slots, left_s, waits_l, waits_r, each))
    if sums:
        got_more = fetch(
            [
                (more_up.at[0], more_s.at[0]),
                (more_down.at[0], more_s.at[1]),
                (more_down.at[1], more_s.at[2]),
                (more_up.at[1], more_s.at[3]),
            ],
            more_sem,
        )
        got_up = fetch([(pre, pre_s), (up, up_s)], up_sem)
    for slots, left_s, waits_l, waits_r, each in todo:
        for i, cols, sizes, right_s, stage, sem, targets in each:
            waits_r[i]()
            block = stage.shape[1]
            per = group // block
            for g in range(len(waits_l)):
                if i == 0:
                    waits_l[g]()
                product = by_last(left_s[g * group : (g + 1) * group, :], right_s[...])
                for b in range(per):
                    j = g * per + b
                    value = product[b * block : (b + 1) * block, :cols]
                    if sums and i == 0:
                        if j == 0:
                            got_more()
                        value = value + more_s[j].astype(F32)
                    stage[j] = value.astype(BF16)
                    slot = slots[i, j]
                    first = 0
                    for out, size in zip(targets, sizes):

                        @pl.when((slot >= first) & (slot < first + size))
                        def _(out=out, first=first, j=j, slot=slot, stage=stage, sem=sem):
                            pltpu.make_async_copy(
                                stage.at[j], out.at[slot - first], sem.at[j]
                            ).start()

                        first += size
    if sums:
        got_up()
        for first in range(0, up.shape[1], 512):
            here = slice(first, min(first + 512, up.shape[1]))
            sums_s[:, here] = lax.dot_general(
                pre_s[...], up_s[:, here], (((0,), (0,)), ((), ())), preferred_element_type=F32
            ).astype(BF16)
        eighth = sums_s.shape[0] // MEMBERS
        half = eighth // 2
        sums_out, first_out, last_out = sums_outs
        copies = [(sums_s, sums_out)]
        for i in range(2):
            at = (4 + i) * eighth
            here = slice(i * half, (i + 1) * half)
            copies.append((sums_s.at[at : at + half], first_out.at[here]))
            copies.append((sums_s.at[at + half : at + eighth], last_out.at[here]))
        fetch(copies, sums_sem)()
    for _, _, _, _, each in todo:
        for _, _, _, _, stage, sem, targets in each:
            for j in range(stage.shape[0]):
                pltpu.make_async_copy(stage.at[j], targets[0].at[0], sem.at[j]).wait()


def grad_blocks(jobs, sums=()):
    block = 200
    specs, ins, outs, scratch = [], [], [], []
    for slots, left, left_got, right, right_got, parts in jobs:
        width, rows = left.shape
        specs += [SMEM] + [HBM] * 4
        ins += [slots, left, left_got, right, right_got]
        scratch += [
            pltpu.VMEM((width, 2 * rows), BF16),
            pltpu.SemaphoreType.DMA((width // 800, 2)),
            pltpu.SemaphoreType.DMA((len(parts), 2)),
        ]
        for _, cols, sizes in parts:
            outs += [jax.ShapeDtypeStruct((size, block, cols), BF16) for size in sizes]
            scratch += [
                pltpu.VMEM((-(-cols // 256) * 256, 2 * rows), BF16),
                pltpu.VMEM((width // block, block, cols), BF16),
                pltpu.SemaphoreType.DMA((width // block,)),
            ]
    lists = [job[-1] for job in jobs]
    if sums:
        (hidden, rows), width = sums[0].shape, sums[1].shape[1]
        specs += [HBM] * 4
        ins += list(sums)
        outs.append(jax.ShapeDtypeStruct((rows, width), BF16))
        outs += [jax.ShapeDtypeStruct((rows // MEMBERS, width), BF16)] * 2
        scratch += [
            pltpu.VMEM((hidden, rows), BF16),
            pltpu.VMEM((hidden, width), BF16),
            pltpu.VMEM((rows, width), BF16),
            pltpu.VMEM((4, *sums[2].shape[1:]), BF16),
            pltpu.SemaphoreType.DMA((2,)),
            pltpu.SemaphoreType.DMA((5,)),
            pltpu.SemaphoreType.DMA((4,)),
        ]

    def kernel(*refs):
        blocks_kernel(lists, bool(sums), *refs)

    return pl.pallas_call(
        kernel,
        out_shape=outs,
        in_specs=specs,
        out_specs=[HBM] * len(outs),
        scratch_shapes=scratch,
        compiler_params=params(52),
        cost_estimate=cost(10**10, 10**7),
    )(*ins)


def z_order(z, xl):
    pairs = [(2, 0), (1, 1), (2, 1), (3, 0), (1, 0), (3, 1), (0, 0), (0, 1)]
    return [((z + dz) % Z) * XL + x for dz, x in pairs]


def x_order(z, xl):
    pairs = [(dz, dx) for dx in (1, 0) for dz in (2, 1, 3, 0)]
    return [((z + dz) % Z) * XL + (xl + dx) % XL for dz, dx in pairs]


def slots_of(order):
    order = jnp.stack(order).astype(jnp.int32)
    index = jnp.arange(order.shape[0], dtype=jnp.int32)
    return jnp.sum(jnp.where(order[None, :] == index[:, None], index[None, :], 0), 1)


def beside(*parts):
    return jnp.concatenate(parts, 1)


def below(*parts):
    return jnp.concatenate(parts, 0)


def on_device(
    lm_grad, encoder_row, patch_count, hidden_in, norm_gain, layer_scale, up_weight, down_weight
):
    tok_rows, width = hidden_in.shape
    rest = up_weight.shape[1] - CUT
    up_turned, down_turned = up_weight.T, down_weight.T
    group_len = tok_rows * MEMBERS
    per_pair = tok_rows // BLOCKS
    half = tok_rows // 2
    z, xl, core = lax.axis_index("z"), lax.axis_index("xl"), lax.axis_index("core")
    y, xh = lax.axis_index("y"), lax.axis_index("xh")
    group = (z * XL + xl) * CORE + core
    core_at = core.reshape(1).astype(jnp.int32)
    z_slots, x_slots = slots_of(z_order(z, xl)), slots_of(x_order(z, xl))

    inputs = hidden_in.astype(F32)
    inverse_rms = lax.rsqrt(jnp.mean(inputs * inputs, -1, keepdims=True) + 1e-06)
    normed_own = (inputs * inverse_rms * norm_gain).astype(BF16)

    n_prev = shift(normed_own, "y", Y, 1)
    n_next = shift(normed_own, "y", Y, -1)
    n_other = shift(normed_own, "xh", XH, 1)

    image, place = encoder_row // group_len, encoder_row % group_len
    index = jnp.arange(tok_rows, dtype=jnp.int32)
    same = (image[:, None] == image[None, :]) & (index[None, :] < index[:, None])
    slot = image * per_pair + jnp.sum(same.astype(jnp.int32), 1)
    sorter = (slot[None, :] == index[:, None]).astype(BF16)
    column = jnp.arange(ID_COLS, dtype=jnp.int32)[None, :]
    tags = jnp.where(
        column == 0,
        (place // ID_BASE)[:, None],
        jnp.where(column == 1, (place % ID_BASE)[:, None], 0),
    ).astype(BF16)
    ordered = jnp.dot(sorter, beside(lm_grad, tags), preferred_element_type=F32).astype(BF16)
    arrived = lax.all_to_all(
        ordered.reshape(BLOCKS, per_pair, width + ID_COLS),
        ("z", "xl", "core"),
        split_axis=0,
        concat_axis=0,
    ).reshape(tok_rows, width + ID_COLS)

    n_prev, n_next, n_other = together(n_prev, n_next, n_other)
    mix_prev = shift(below(n_other, n_prev[:half]), "y", Y, 1)
    mix_next = shift(below(n_other, n_next[half:]), "y", Y, -1)
    g_other = shift(arrived, "xh", XH, 1)
    block = jnp.arange(MEMBERS, dtype=jnp.int32)
    member = ((block // XH + y) % Y) * XH + (block % XH + xh) % XH
    positions = (member[:, None] * tok_rows + index[None, :]).reshape(group_len, 1)
    limit = lax.dynamic_index_in_dim(patch_count, group, 0, keepdims=False)
    positions = jnp.where(positions < limit, positions, -1).astype(F32)
    order = jnp.stack(z_order(z, xl)).astype(jnp.int32)
    scale_rows = layer_scale.reshape(BLOCKS // 2, -1)[order].reshape(2, width // 2)
    mix_prev, mix_next, g_other, arrived, positions, scale_rows = together(
        mix_prev, mix_next, g_other, arrived, positions, scale_rows
    )

    far_a = shift(mix_prev[:half], "y", Y, 1)
    far_b = shift(mix_next[half:tok_rows], "y", Y, -1)
    g_1, g_2 = prepare(order, arrived, g_other, width)
    far_a, far_b, g_1, g_2 = together(far_a, far_b, g_1, g_2)

    g_prev_1, g_next_1 = shift(g_1, "y", Y, 1), shift(g_1, "y", Y, -1)
    g_prev_2, g_next_2 = shift(g_2, "y", Y, 1), shift(g_2, "y", Y, -1)
    act, slope, n_keep, n_give = assemble_normed(
        core_at, (normed_own, n_other, n_next, n_prev, mix_prev, mix_next, far_a, far_b), up_turned
    )
    g_prev_1, g_next_1, g_prev_2, g_next_2, act, n_give = together(
        g_prev_1, g_next_1, g_prev_2, g_next_2, act, n_give
    )

    f_prev_1 = shift(g_prev_1[:tok_rows], "y", Y, 1)
    f_next_1 = shift(g_next_1[tok_rows:], "y", Y, -1)
    f_prev_2 = shift(g_prev_2[:tok_rows], "y", Y, 1)
    f_next_2 = shift(g_next_2[tok_rows:], "y", Y, -1)
    s_1, d_keep_1, d_give_1, own_first, chooser = route_first(
        core_at, order, scale_rows, positions, (g_1, g_prev_1, g_next_1, f_prev_1, f_next_1)
    )
    d_give_1, act = together(d_give_1, act)
    d_got_1 = shift(d_give_1, "core", CORE, 1)
    act_got = shift(act, "core", CORE, 1)
    here = xl == 0
    straight = jnp.arange(4, dtype=jnp.int32)
    slots_1 = jnp.stack([straight, jnp.where(here, jnp.array([2, 1, 0, 3]), jnp.array([0, 3, 2, 1]))])
    slots_2 = jnp.stack([straight, jnp.where(here, jnp.array([2, 0, 3, 1]), jnp.array([0, 2, 1, 3]))])
    slots_1, slots_2 = slots_1.astype(jnp.int32), slots_2.astype(jnp.int32)
    d_got_1, act_got, n_give = together(d_got_1, act_got, n_give)
    d_up, d_down, d_out_1, d_mine_1 = grad_blocks(
        [(slots_1, d_keep_1, d_got_1, act, act_got, ((0, CUT, (2, 2)), (CUT, rest, (2, 2))))]
    )
    d_prev, d_next = shift(d_up, "z", Z, 1), shift(d_down, "z", Z, -1)
    d_x_1 = shift(d_out_1, "xl", XL, 1)
    d_out_1, n_give = together(d_out_1, n_give)
    n_got = shift(n_give, "core", CORE, 1)
    f_prev_2, f_next_2, d_mine_1 = together(f_prev_2, f_next_2, d_mine_1)

    d_keep_2, d_give_2, own_grad, pre = middle(
        core_at, order, scale_rows, chooser, own_first, s_1, slope, down_turned,
        (g_2, g_prev_2, g_next_2, f_prev_2, f_next_2),
    )
    d_got_2 = shift(d_give_2, "core", CORE, 1)
    d_got_2, d_prev, d_next = together(d_got_2, d_prev, d_next)
    pre_got = shift(pre, "core", CORE, 1)
    d_acc_prev, d_acc_next, d_kept, d_out_2, d_mine_2, parts, p_prev, p_next = grad_blocks(
        [(slots_2, d_keep_2, d_got_2, act, act_got, ((0, CUT, (1, 1, 2)), (CUT, rest, (2, 2))))],
        (pre, up_turned, d_prev, d_next),
    )
    pre_got, parts = together(pre_got, parts)

    d_acc_prev, d_acc_next = shift(d_acc_prev, "z", Z, 1), shift(d_acc_next, "z", Z, -1)
    d_x_2 = shift(d_out_2, "xl", XL, 1)
    u_up, u_down, u_kept, u_out, u_mine = grad_blocks(
        [
            (
                jnp.stack([z_slots, x_slots]), n_keep, n_got, pre, pre_got,
                ((0, UP_CUT, (2, 2, 4)), (UP_CUT, rest + CUT - UP_CUT, (4, 4))),
            )
        ]
    )
    d_acc_prev, d_acc_next, d_x_1, d_x_2, u_mine, parts, p_prev, p_next = together(
        d_acc_prev, d_acc_next, d_x_1, d_x_2, u_mine, parts, p_prev, p_next
    )

    u_prev, u_next = shift(u_up, "z", Z, 1), shift(u_down, "z", Z, -1)
    u_x = shift(u_out, "xl", XL, 1)
    blocks = parts.reshape(MEMBERS, tok_rows, width)
    p_prev = shift(below(blocks[4][:half], blocks[5][:half]), "y", Y, 1)
    p_next = shift(below(blocks[4][half:], blocks[5][half:]), "y", Y, -1)
    sum_0, sum_1 = add(d_kept[0], d_acc_prev[0]), add(d_kept[1], d_acc_next[0])
    d_own, d_give = jnp.where(here, sum_0, sum_1), jnp.where(here, sum_1, sum_0)
    o_prev, o_next = (
        below(add(blocks[3][:half], p_prev[half:]), blocks[3][half:]),
        below(blocks[7][:half], add(blocks[7][half:], p_next[half:])),
    )
    d_give, u_x, _, _ = together(d_give, u_x, o_prev, o_next)
    o_prev, o_next = shift(o_prev, "y", Y, 1), shift(o_next, "y", Y, -1)
    d_other = shift(d_give, "xl", XL, 1)

    m_prev = shift(add(u_kept[0], u_prev[0]), "z", Z, 1)
    m_next = shift(add(u_kept[1], u_next[0]), "z", Z, -1)
    d_other, p_prev, p_next, o_prev, o_next = together(d_other, p_prev, p_next, o_prev, o_next)
    r_other = shift(add(blocks[1], o_prev, o_next), "xh", XH, 1)
    r_prev = shift(below(add(blocks[2][:half], p_prev[:half]), blocks[2][half:]), "y", Y, 1)
    r_next = shift(below(blocks[6][:half], add(blocks[6][half:], p_next[:half])), "y", Y, -1)

    sum_0 = add(u_kept[2], u_next[1], m_prev)
    sum_1 = add(u_kept[3], u_prev[1], m_next)
    u_own, u_give = jnp.where(here, sum_0, sum_1), jnp.where(here, sum_1, sum_0)
    u_other = shift(u_give, "xl", XL, 1)
    cut = -(-d_x_1.shape[1] // 16) * 8
    u_x, d_x_2, r_prev, r_next, u_own, d_other = together(
        u_x, d_x_2, r_prev, r_next, u_own, d_other
    )
    two, side_1, side_2 = (
        add(d_mine_1[0], d_x_1[0]), add(d_mine_1[1], d_x_1[1]), add(d_mine_2[0], d_x_2[0])
    )
    one, three = jnp.where(here, side_2, side_1), jnp.where(here, side_1, side_2)
    two, one, three = (
        beside(both, add(u_mine[i], u_x[i])) for i, both in enumerate((two, one, three))
    )
    b_here = beside(add32(d_mine_2[1], d_x_2[1]), add32(u_mine[3], u_x[3]))
    b_prev = shift(below(two[:cut], one[cut:]), "z", Z, 1)
    b_next = shift(below(three[:cut], two[cut:]), "z", Z, -1)
    c_prev = shift(add(one[:cut], b_prev[:cut]), "z", Z, 1)
    c_next = shift(add(three[cut:], b_next[cut:]), "z", Z, -1)
    r_prev, r_next, r_other, b_prev = together(r_prev, r_next, r_other, b_prev)
    down_a, up_a = add32(d_own, d_other), add32(u_own, u_other)
    b_total = below(
        add32(b_here[:cut], b_next[:cut], c_prev), add32(b_here[cut:], b_prev[cut:], c_next)
    )
    down_b, up_b = b_total[:, :rest], b_total[:, rest:]
    normed_grad = add32(blocks[0], r_prev, r_next, r_other)
    weighted = norm_gain * normed_grad
    input_grad = (
        own_grad.astype(F32)
        + inverse_rms * weighted
        - inputs * inverse_rms**3 * jnp.mean(weighted * inputs, -1, keepdims=True)
    ).astype(BF16)
    grad_scale = 1.0 / math.sqrt(group_len * BLOCKS)
    return (
        input_grad,
        (beside(up_a, up_b) * grad_scale).astype(BF16),
        (beside(down_a, down_b) * grad_scale).astype(BF16),
    )


def solution(mesh):
    fine = Mesh(mesh.devices.reshape(Z, XL, CORE, Y, XH), AXES)
    dp, tensor = AXES[:3], AXES[3:]
    in_specs = (
        P(AXES, None),
        P(AXES),
        P(),
        P(AXES, None),
        P(),
        P(),
        P(None, tensor),
        P(None, tensor),
    )
    out_specs = (P(AXES, None), P(dp, tensor), P(dp, tensor))
    return jax.shard_map(
        on_device, mesh=fine, in_specs=in_specs, out_specs=out_specs, check_vma=False
    )
```

```python
import math

import jax
import jax.numpy as jnp
from jax import lax
from jax.experimental import pallas as pl
from jax.experimental.pallas import tpu as pltpu
from jax.sharding import Mesh, PartitionSpec as P

F32 = jnp.float32
BF16 = jnp.bfloat16
Z, XL, CORE, Y, XH = 4, 2, 2, 4, 2
AXES = ("z", "xl", "core", "y", "xh")
MEMBERS = Y * XH
BLOCKS = Z * XL * CORE
ID_COLS = 128
ID_BASE = 32
CUT = 1152
UP_CUT = 1152
MIB = 1024 * 1024
VMEM = pl.BlockSpec(memory_space=pltpu.VMEM)
SMEM = pl.BlockSpec(memory_space=pltpu.SMEM)
ANY = pl.BlockSpec(memory_space=pl.ANY)
HBM = pl.BlockSpec(memory_space=pltpu.HBM)


def params(mib):
    return pltpu.CompilerParams(vmem_limit_bytes=mib * MIB)


def cost(flops, moved, special=0):
    return pl.CostEstimate(flops=flops, bytes_accessed=moved, transcendentals=special)


def shift(value, axis, size, step):
    return lax.ppermute(value, axis, [(i, (i + step) % size) for i in range(size)])


def add32(*terms):
    total = terms[0].astype(F32)
    for term in terms[1:]:
        total = total + term.astype(F32)
    return total


def add(*terms):
    return add32(*terms).astype(BF16)


def together(*values):
    return lax.optimization_barrier(values)


def fetch(pieces, sem):
    copies = [pltpu.make_async_copy(src, dst, sem.at[i]) for i, (src, dst) in enumerate(pieces)]
    for copy in copies:
        copy.start()

    def wait():
        for copy in copies:
            copy.wait()

    return wait


def pieces_of(listed, out):
    at, pieces = 0, []
    for ref, first, rows in listed:
        pieces.append((ref.at[first : first + rows], out.at[at : at + rows]))
        at += rows
    return pieces


def split_parity(turned, core, pairs, keep, give):
    rows = keep.shape[0] // pairs
    for two in range(pairs // 2):
        for out, parity in ((keep, core), (give, 1 - core)):
            blocks = [
                turned[pl.ds(pl.multiple_of((2 * b + parity) * rows, 8), rows), :]
                for b in (2 * two, 2 * two + 1)
            ]
            out[2 * two * rows : (2 * two + 2) * rows, :] = jnp.concatenate(blocks, 0).astype(BF16)


def by_last(left, right):
    return lax.dot_general(left, right, (((1,), (1,)), ((), ())), preferred_element_type=F32)


def normed_kernel(core, *refs):
    ins, weight, (act, slope, keep, give) = refs[:8], refs[8], refs[9:13]
    normed, turned, held, act_s, slope_s, keep_s, give_s, in_sem, w_sem, out_sem, sem = refs[13:]
    own, other, nxt, prev, mix_prev, mix_next, far_a, far_b = ins
    full = own.shape[0]
    half = full // 2
    listed = [(own, 0, full), (other, 0, full), (nxt, 0, full), (mix_next, 0, full)]
    listed += [(mix_prev, full, half), (mix_next, full, half), (far_a, 0, half), (far_b, 0, half)]
    listed += [(prev, 0, full), (mix_prev, 0, full)]
    fetched = fetch(pieces_of(listed, normed), in_sem)
    tile = held.shape[1]
    count = held.shape[0]
    tiles = [slice(n * tile, (n + 1) * tile) for n in range(count)]
    weights = [fetch([(weight.at[tiles[n]], held.at[n])], w_sem.at[n]) for n in range(count)]
    fetched()
    for t in range(normed.shape[1] // 128):
        cols = slice(t * 128, (t + 1) * 128)
        turned[cols, :] = normed[:, cols].astype(F32).T
    split_parity(turned, core[0], BLOCKS // 2, keep_s, give_s)
    waits = [fetch([(give_s, give), (keep_s, keep)], out_sem)]
    for n, rows in enumerate(tiles):
        weights[n]()
        value = by_last(held[n], normed[...])
        below = 0.5 * (1.0 + lax.erf(value * 0.7071067811865476))
        act_s[rows, :] = (value * below).astype(BF16)
        slope_s[rows, :] = (
            below + value * jnp.exp(-0.5 * value * value) * 0.3989422804014327
        ).astype(BF16)
        waits.append(
            fetch([(act_s.at[rows], act.at[rows]), (slope_s.at[rows], slope.at[rows])], sem.at[n])
        )
    for wait in waits:
        wait()


def assemble_normed(core, ins, weight):
    rows, width = ins[0].shape[0] * MEMBERS, ins[0].shape[1]
    hidden = weight.shape[0]
    count = 4
    outs = [((hidden, rows), BF16)] * 2 + [((width // 2, rows), BF16)] * 2
    return pl.pallas_call(
        normed_kernel,
        out_shape=[jax.ShapeDtypeStruct(shape, kind) for shape, kind in outs],
        in_specs=[SMEM] + [HBM] * (len(ins) + 1),
        out_specs=[HBM] * 4,
        scratch_shapes=[
            pltpu.VMEM((rows, width), BF16),
            pltpu.VMEM((width, rows), F32),
            pltpu.VMEM((count, hidden // count, width), BF16),
        ]
        + [pltpu.VMEM(shape, kind) for shape, kind in outs]
        + [pltpu.SemaphoreType.DMA((n,)) for n in (10,)]
        + [pltpu.SemaphoreType.DMA((count, 1)), pltpu.SemaphoreType.DMA((2,))]
        + [pltpu.SemaphoreType.DMA((count, 2))],
        compiler_params=params(52),
        cost_estimate=cost(10**10, 10**7),
    )(core, *ins, weight)


def prepare_kernel(order, own, other, first, second, rows_s, turned, sorted_s, *refs):
    outs_s, in_sem, sem = refs[:2], refs[2], refs[3]
    half = own.shape[0] // 2
    listed = [(own, 0, half), (other, 0, half), (own, half, half), (other, half, half)]
    fetch(pieces_of(listed, rows_s), in_sem)()
    width = turned.shape[0]
    pair = width // (BLOCKS // 2)
    for t in range(width // 128):
        cols = slice(t * 128, (t + 1) * 128)
        turned[cols, :] = rows_s[:, cols].astype(F32).T
    waits = []
    for h, out in enumerate((first, second)):
        for p in range(4):
            at = pl.ds(pl.multiple_of(order[4 * h + p] * pair, 8), pair)
            sorted_s[p * pair : (p + 1) * pair, :] = turned[at, :]
        cols = width // 2
        lead = 0 if h else ID_COLS
        for first_col in range(0, cols, 128):
            last = min(first_col + 128, cols)
            outs_s[h][:, lead + first_col : lead + last] = (
                sorted_s[first_col : first_col + 128, :].T[:, : last - first_col].astype(BF16)
            )
        if h == 0:
            outs_s[h][:, :lead] = rows_s[:, width : width + ID_COLS]
        waits.append(fetch([(outs_s[h], out)], sem.at[h]))
    for wait in waits:
        wait()


def prepare(order, own, other, width):
    rows = 2 * own.shape[0]
    cols = width // 2
    return pl.pallas_call(
        prepare_kernel,
        out_shape=[
            jax.ShapeDtypeStruct((rows, cols + ID_COLS), BF16),
            jax.ShapeDtypeStruct((rows, cols), BF16),
        ],
        in_specs=[SMEM, HBM, HBM],
        out_specs=[HBM, HBM],
        scratch_shapes=[
            pltpu.VMEM((rows, width + ID_COLS), BF16),
            pltpu.VMEM((width, rows), F32),
            pltpu.VMEM((-(-cols // 128) * 128, rows), F32),
            pltpu.VMEM((rows, cols + ID_COLS), BF16),
            pltpu.VMEM((rows, cols), BF16),
            pltpu.SemaphoreType.DMA((4,)),
            pltpu.SemaphoreType.DMA((2, 1)),
        ],
        compiler_params=params(52),
        cost_estimate=cost(10**8, 10**6),
    )(order, own, other)


def joined_pieces(ins, joined):
    at, pieces = 0, []
    for ref in ins:
        rows = ref.shape[0]
        pieces.append((ref, joined.at[at : at + rows]))
        at += rows
    return pieces


def to_image_order(chooser, joined, lead, scale, turned, own):
    cols = turned.shape[0]
    for first in range(0, cols, 640):
        last = min(first + 640, cols)
        grads = jnp.dot(
            chooser[...], joined[:, lead + first : lead + last], preferred_element_type=F32
        )
        own[first:last, :] = grads[:128].T
        turned[first:last, :] = (grads * scale[:, first:last]).T


def first_kernel(core, order, scales, positions, *refs):
    ins, (scaled, keep, give, own_turned, chooser_out) = refs[:5], refs[5:10]
    joined, turned, scaled_s, keep_s, give_s, chooser, own_s, in_sem, sem, give_sem = refs[10:]
    del order
    fetch(joined_pieces(ins, joined), in_sem)()
    tags = joined[:, :ID_COLS].astype(F32).T
    places = tags[0:1, :] * ID_BASE + tags[1:2, :]
    chooser[...] = (positions[...] == places).astype(F32).astype(BF16)
    to_image_order(chooser, joined, ID_COLS, scales[0:1, :], turned, own_s)
    waits = [fetch([(own_s, own_turned), (chooser, chooser_out)], sem)]
    scaled_s[...] = turned[...].astype(BF16)
    split_parity(turned, core[0], 4, keep_s, give_s)
    waits.append(fetch([(give_s, give), (keep_s, keep), (scaled_s, scaled)], give_sem))
    for wait in waits:
        wait()


def route_first(core, order, scales, positions, ins):
    rows, cols = positions.shape[0], scales.shape[1]
    turned = ((cols // 2, rows), BF16)
    outs = [((cols, rows), BF16), turned, turned, ((cols, 128), F32), ((rows, rows), BF16)]
    return pl.pallas_call(
        first_kernel,
        out_shape=[jax.ShapeDtypeStruct(shape, kind) for shape, kind in outs],
        in_specs=[SMEM, SMEM, VMEM, VMEM] + [HBM] * len(ins),
        out_specs=[HBM] * 5,
        scratch_shapes=[
            pltpu.VMEM((rows, cols + ID_COLS), BF16),
            pltpu.VMEM((cols, rows), F32),
            pltpu.VMEM((cols, rows), BF16),
            pltpu.VMEM((cols // 2, rows), BF16),
            pltpu.VMEM((cols // 2, rows), BF16),
            pltpu.VMEM((rows, rows), BF16),
            pltpu.VMEM((cols, 128), F32),
        ]
        + [pltpu.SemaphoreType.DMA((n,)) for n in (5, 2, 3)],
        compiler_params=params(52),
        cost_estimate=cost(10**9, 10**7),
    )(core, order, scales, positions, *ins)


def middle_kernel(core, order, *refs):
    scales, chooser_in, own_first, scaled_1, slope, down = refs[:6]
    ins, (keep, give, own_grad, pre) = refs[6:11], refs[11:15]
    joined, turned, scaled, keep_s, give_s, chooser, own_s, own_rows, own_out = refs[15:24]
    slope_s, down_s, pre_s = refs[24:27]
    in_sem, s_sem, d_sem, give_sem, own_sem, pre_sem = refs[27:]
    cols = joined.shape[1]
    pair = cols // 4
    got = fetch(
        joined_pieces(ins, joined)
        + [(chooser_in, chooser), (own_first, own_s.at[0])],
        in_sem,
    )
    more = [(slope, slope_s)]
    for p in range(4):
        at = pl.ds(pl.multiple_of(order[p] * pair, 16), pair)
        more.append((scaled_1.at[p * pair : (p + 1) * pair], scaled.at[at]))
    got_more = fetch(more, s_sem)
    count = 2
    tile = down.shape[0] // count
    tiles = [slice(n * tile, (n + 1) * tile) for n in range(count)]
    got_down = [fetch([(down.at[rows], down_s.at[rows])], d_sem.at[n]) for n, rows in enumerate(tiles)]
    got()
    to_image_order(chooser, joined, 0, scales[1:2, :], turned, own_s.at[1])
    got_more()
    for p in range(4):
        here = slice(p * pair, (p + 1) * pair)
        place = order[4 + p] * pair
        scaled[pl.ds(pl.multiple_of(place, 16), pair), :] = turned[here, :].astype(BF16)
    split_parity(turned, core[0], 4, keep_s, give_s)
    waits = [fetch([(give_s, give), (keep_s, keep)], give_sem)]
    for n, rows in enumerate(tiles):
        got_down[n]()
        value = jnp.dot(down_s[rows, :], scaled[...], preferred_element_type=F32)
        pre_s[rows, :] = (value * slope_s[rows, :].astype(F32)).astype(BF16)
        waits.append(fetch([(pre_s.at[rows], pre.at[rows])], pre_sem.at[n]))
    for p in range(8):
        at = pl.ds(pl.multiple_of(order[p] * pair, 8), pair)
        own_rows[at, :] = own_s[p // 4, (p % 4) * pair : (p % 4 + 1) * pair, :]
    for t in range(own_rows.shape[0] // 128):
        here = slice(t * 128, (t + 1) * 128)
        own_out[:, here] = own_rows[here, :].T[: own_out.shape[0]].astype(BF16)
    waits.append(fetch([(own_out, own_grad)], own_sem))
    for wait in waits:
        wait()


def middle(core, order, scales, chooser, own_first, scaled_1, slope, down, ins):
    hidden, width = down.shape
    rows, cols = chooser.shape[0], width // 2
    turned = ((cols // 2, rows), BF16)
    outs = [turned, turned, ((rows // MEMBERS, width), BF16), ((hidden, rows), BF16)]
    return pl.pallas_call(
        middle_kernel,
        out_shape=[jax.ShapeDtypeStruct(shape, kind) for shape, kind in outs],
        in_specs=[SMEM, SMEM, VMEM] + [HBM] * (5 + len(ins)),
        out_specs=[HBM] * 4,
        scratch_shapes=[
            pltpu.VMEM((rows, cols), BF16),
            pltpu.VMEM((cols, rows), F32),
            pltpu.VMEM((width, rows), BF16),
            pltpu.VMEM((cols // 2, rows), BF16),
            pltpu.VMEM((cols // 2, rows), BF16),
            pltpu.VMEM((rows, rows), BF16),
            pltpu.VMEM((2, cols, 128), F32),
            pltpu.VMEM((width, 128), F32),
            pltpu.VMEM((rows // MEMBERS, width), BF16),
            pltpu.VMEM((hidden, rows), BF16),
            pltpu.VMEM((hidden, width), BF16),
            pltpu.VMEM((hidden, rows), BF16),
        ]
        + [pltpu.SemaphoreType.DMA((n,)) for n in (7, 5)]
        + [pltpu.SemaphoreType.DMA((2, 1))]
        + [pltpu.SemaphoreType.DMA((n,)) for n in (2, 1)]
        + [pltpu.SemaphoreType.DMA((2, 1))],
        compiler_params=params(52),
        cost_estimate=cost(10**10, 10**7),
    )(core, order, scales, chooser, own_first, scaled_1, slope, down, *ins)


def blocks_kernel(jobs, sums, *refs):
    group = 800
    count = len(jobs)
    if sums:
        refs, (pre_s, up_s, sums_s, more_s, up_sem, sums_sem, more_sem) = refs[:-7], refs[-7:]
        pre, up, more_up, more_down = refs[5 * count : 5 * count + 4]
        refs = refs[: 5 * count] + refs[5 * count + 4 :]
    ins, refs = refs[: 5 * count], refs[5 * count :]
    total = sum(len(sizes) for parts in jobs for _, _, sizes in parts)
    pieces = sum(len(parts) for parts in jobs)
    scratch = refs[-(3 * count + 3 * pieces) :]
    outs, sums_outs = refs[:total], refs[total : total + 3]
    todo = []
    at_out = at = 0
    for k, parts in enumerate(jobs):
        slots, left, left_got, right, right_got = ins[5 * k : 5 * k + 5]
        left_s, l_sem, r_sem = scratch[at : at + 3]
        at += 3
        rows_in = left.shape[1]
        waits_r = []
        each = []
        for i, (first, cols, sizes) in enumerate(parts):
            right_s, stage, sem = scratch[at : at + 3]
            at += 3
            here = slice(first, first + cols)
            waits_r.append(
                fetch(
                    [
                        (right.at[here], right_s.at[:cols, :rows_in]),
                        (right_got.at[here], right_s.at[:cols, rows_in:]),
                    ],
                    r_sem.at[i],
                )
            )
            each.append((i, cols, sizes, right_s, stage, sem, outs[at_out : at_out + len(sizes)]))
            at_out += len(sizes)
        waits_l = []
        for g in range(left.shape[0] // group):
            here = slice(g * group, (g + 1) * group)
            waits_l.append(
                fetch(
                    [
                        (left.at[here], left_s.at[here, :rows_in]),
                        (left_got.at[here], left_s.at[here, rows_in:]),
                    ],
                    l_sem.at[g],
                )
            )
        todo.append((slots, left_s, waits_l, waits_r, each))
    if sums:
        got_more = fetch(
            [
                (more_up.at[0], more_s.at[0]),
                (more_down.at[0], more_s.at[1]),
                (more_down.at[1], more_s.at[2]),
                (more_up.at[1], more_s.at[3]),
            ],
            more_sem,
        )
        got_up = fetch([(pre, pre_s), (up, up_s)], up_sem)
    for slots, left_s, waits_l, waits_r, each in todo:
        for i, cols, sizes, right_s, stage, sem, targets in each:
            waits_r[i]()
            block = stage.shape[1]
            per = group // block
            for g in range(len(waits_l)):
                if i == 0:
                    waits_l[g]()
                product = by_last(left_s[g * group : (g + 1) * group, :], right_s[...])
                for b in range(per):
                    j = g * per + b
                    value = product[b * block : (b + 1) * block, :cols]
                    if sums and i == 0:
                        if j == 0:
                            got_more()
                        value = value + more_s[j].astype(F32)
                    stage[j] = value.astype(BF16)
                    slot = slots[i, j]
                    first = 0
                    for out, size in zip(targets, sizes):

                        @pl.when((slot >= first) & (slot < first + size))
                        def _(out=out, first=first, j=j, slot=slot, stage=stage, sem=sem):
                            pltpu.make_async_copy(
                                stage.at[j], out.at[slot - first], sem.at[j]
                            ).start()

                        first += size
    if sums:
        got_up()
        for first in range(0, up.shape[1], 512):
            here = slice(first, min(first + 512, up.shape[1]))
            sums_s[:, here] = lax.dot_general(
                pre_s[...], up_s[:, here], (((0,), (0,)), ((), ())), preferred_element_type=F32
            ).astype(BF16)
        eighth = sums_s.shape[0] // MEMBERS
        half = eighth // 2
        sums_out, first_out, last_out = sums_outs
        copies = [(sums_s, sums_out)]
        for i in range(2):
            at = (4 + i) * eighth
            here = slice(i * half, (i + 1) * half)
            copies.append((sums_s.at[at : at + half], first_out.at[here]))
            copies.append((sums_s.at[at + half : at + eighth], last_out.at[here]))
        fetch(copies, sums_sem)()
    for _, _, _, _, each in todo:
        for _, _, _, _, stage, sem, targets in each:
            for j in range(stage.shape[0]):
                pltpu.make_async_copy(stage.at[j], targets[0].at[0], sem.at[j]).wait()


def grad_blocks(jobs, sums=()):
    block = 200
    specs, ins, outs, scratch = [], [], [], []
    for slots, left, left_got, right, right_got, parts in jobs:
        width, rows = left.shape
        specs += [SMEM] + [HBM] * 4
        ins += [slots, left, left_got, right, right_got]
        scratch += [
            pltpu.VMEM((width, 2 * rows), BF16),
            pltpu.SemaphoreType.DMA((width // 800, 2)),
            pltpu.SemaphoreType.DMA((len(parts), 2)),
        ]
        for _, cols, sizes in parts:
            outs += [jax.ShapeDtypeStruct((size, block, cols), BF16) for size in sizes]
            scratch += [
                pltpu.VMEM((-(-cols // 256) * 256, 2 * rows), BF16),
                pltpu.VMEM((width // block, block, cols), BF16),
                pltpu.SemaphoreType.DMA((width // block,)),
            ]
    lists = [job[-1] for job in jobs]
    if sums:
        (hidden, rows), width = sums[0].shape, sums[1].shape[1]
        specs += [HBM] * 4
        ins += list(sums)
        outs.append(jax.ShapeDtypeStruct((rows, width), BF16))
        outs += [jax.ShapeDtypeStruct((rows // MEMBERS, width), BF16)] * 2
        scratch += [
            pltpu.VMEM((hidden, rows), BF16),
            pltpu.VMEM((hidden, width), BF16),
            pltpu.VMEM((rows, width), BF16),
            pltpu.VMEM((4, *sums[2].shape[1:]), BF16),
            pltpu.SemaphoreType.DMA((2,)),
            pltpu.SemaphoreType.DMA((5,)),
            pltpu.SemaphoreType.DMA((4,)),
        ]

    def kernel(*refs):
        blocks_kernel(lists, bool(sums), *refs)

    return pl.pallas_call(
        kernel,
        out_shape=outs,
        in_specs=specs,
        out_specs=[HBM] * len(outs),
        scratch_shapes=scratch,
        compiler_params=params(52),
        cost_estimate=cost(10**10, 10**7),
    )(*ins)


def z_order(z, xl):
    pairs = [(2, 0), (1, 1), (2, 1), (3, 0), (1, 0), (3, 1), (0, 0), (0, 1)]
    return [((z + dz) % Z) * XL + x for dz, x in pairs]


def x_order(z, xl):
    pairs = [(dz, dx) for dx in (1, 0) for dz in (2, 1, 3, 0)]
    return [((z + dz) % Z) * XL + (xl + dx) % XL for dz, dx in pairs]


def slots_of(order):
    order = jnp.stack(order).astype(jnp.int32)
    index = jnp.arange(order.shape[0], dtype=jnp.int32)
    return jnp.sum(jnp.where(order[None, :] == index[:, None], index[None, :], 0), 1)


def beside(*parts):
    return jnp.concatenate(parts, 1)


def below(*parts):
    return jnp.concatenate(parts, 0)


def on_device(
    lm_grad, encoder_row, patch_count, hidden_in, norm_gain, layer_scale, up_weight, down_weight
):
    tok_rows, width = hidden_in.shape
    rest = up_weight.shape[1] - CUT
    up_turned, down_turned = up_weight.T, down_weight.T
    group_len = tok_rows * MEMBERS
    per_pair = tok_rows // BLOCKS
    half = tok_rows // 2
    z, xl, core = lax.axis_index("z"), lax.axis_index("xl"), lax.axis_index("core")
    y, xh = lax.axis_index("y"), lax.axis_index("xh")
    group = (z * XL + xl) * CORE + core
    core_at = core.reshape(1).astype(jnp.int32)
    z_slots, x_slots = slots_of(z_order(z, xl)), slots_of(x_order(z, xl))

    inputs = hidden_in.astype(F32)
    inverse_rms = lax.rsqrt(jnp.mean(inputs * inputs, -1, keepdims=True) + 1e-06)
    normed_own = (inputs * inverse_rms * norm_gain).astype(BF16)

    n_prev = shift(normed_own, "y", Y, 1)
    n_next = shift(normed_own, "y", Y, -1)
    n_other = shift(normed_own, "xh", XH, 1)

    image, place = encoder_row // group_len, encoder_row % group_len
    index = jnp.arange(tok_rows, dtype=jnp.int32)
    same = (image[:, None] == image[None, :]) & (index[None, :] < index[:, None])
    slot = image * per_pair + jnp.sum(same.astype(jnp.int32), 1)
    sorter = (slot[None, :] == index[:, None]).astype(BF16)
    column = jnp.arange(ID_COLS, dtype=jnp.int32)[None, :]
    tags = jnp.where(
        column == 0,
        (place // ID_BASE)[:, None],
        jnp.where(column == 1, (place % ID_BASE)[:, None], 0),
    ).astype(BF16)
    ordered = jnp.dot(sorter, beside(lm_grad, tags), preferred_element_type=F32).astype(BF16)
    arrived = lax.all_to_all(
        ordered.reshape(BLOCKS, per_pair, width + ID_COLS),
        ("z", "xl", "core"),
        split_axis=0,
        concat_axis=0,
    ).reshape(tok_rows, width + ID_COLS)

    n_prev, n_next, n_other = together(n_prev, n_next, n_other)
    mix_prev = shift(below(n_other, n_prev[:half]), "y", Y, 1)
    mix_next = shift(below(n_other, n_next[half:]), "y", Y, -1)
    g_other = shift(arrived, "xh", XH, 1)
    block = jnp.arange(MEMBERS, dtype=jnp.int32)
    member = ((block // XH + y) % Y) * XH + (block % XH + xh) % XH
    positions = (member[:, None] * tok_rows + index[None, :]).reshape(group_len, 1)
    limit = lax.dynamic_index_in_dim(patch_count, group, 0, keepdims=False)
    positions = jnp.where(positions < limit, positions, -1).astype(F32)
    order = jnp.stack(z_order(z, xl)).astype(jnp.int32)
    scale_rows = layer_scale.reshape(BLOCKS // 2, -1)[order].reshape(2, width // 2)
    mix_prev, mix_next, g_other, arrived, positions, scale_rows = together(
        mix_prev, mix_next, g_other, arrived, positions, scale_rows
    )

    far_a, far_b, arrived, g_other = together(
        mix_prev[:half], mix_next[half:tok_rows], arrived, g_other
    )
    far_a, far_b = shift(far_a, "y", Y, 1), shift(far_b, "y", Y, -1)
    g_1, g_2 = prepare(order, arrived, g_other, width)

    g_prev_1, g_next_1 = shift(g_1, "y", Y, 1), shift(g_1, "y", Y, -1)
    g_prev_2, g_next_2 = shift(g_2, "y", Y, 1), shift(g_2, "y", Y, -1)
    act, slope, n_keep, n_give = assemble_normed(
        core_at, (normed_own, n_other, n_next, n_prev, mix_prev, mix_next, far_a, far_b), up_turned
    )
    g_prev_1, g_next_1, g_prev_2, g_next_2, act, n_give = together(
        g_prev_1, g_next_1, g_prev_2, g_next_2, act, n_give
    )

    f_prev_1 = shift(g_prev_1[:tok_rows], "y", Y, 1)
    f_next_1 = shift(g_next_1[tok_rows:], "y", Y, -1)
    f_prev_2 = shift(g_prev_2[:tok_rows], "y", Y, 1)
    f_next_2 = shift(g_next_2[tok_rows:], "y", Y, -1)
    s_1, d_keep_1, d_give_1, own_first, chooser = route_first(
        core_at, order, scale_rows, positions, (g_1, g_prev_1, g_next_1, f_prev_1, f_next_1)
    )
    d_give_1, act = together(d_give_1, act)
    d_got_1 = shift(d_give_1, "core", CORE, 1)
    act_got = shift(act, "core", CORE, 1)
    here = xl == 0
    straight = jnp.arange(4, dtype=jnp.int32)
    slots_1 = jnp.stack([straight, jnp.where(here, jnp.array([2, 1, 0, 3]), jnp.array([0, 3, 2, 1]))])
    slots_2 = jnp.stack([straight, jnp.where(here, jnp.array([2, 0, 3, 1]), jnp.array([0, 2, 1, 3]))])
    slots_1, slots_2 = slots_1.astype(jnp.int32), slots_2.astype(jnp.int32)
    d_got_1, act_got, n_give = together(d_got_1, act_got, n_give)
    d_up, d_down, d_out_1, d_mine_1 = grad_blocks(
        [(slots_1, d_keep_1, d_got_1, act, act_got, ((0, CUT, (2, 2)), (CUT, rest, (2, 2))))]
    )
    d_prev, d_next = shift(d_up, "z", Z, 1), shift(d_down, "z", Z, -1)
    d_x_1 = shift(d_out_1, "xl", XL, 1)
    d_out_1, n_give = together(d_out_1, n_give)
    n_got = shift(n_give, "core", CORE, 1)
    f_prev_2, f_next_2, d_mine_1 = together(f_prev_2, f_next_2, d_mine_1)

    d_keep_2, d_give_2, own_grad, pre = middle(
        core_at, order, scale_rows, chooser, own_first, s_1, slope, down_turned,
        (g_2, g_prev_2, g_next_2, f_prev_2, f_next_2),
    )
    d_got_2 = shift(d_give_2, "core", CORE, 1)
    d_got_2, d_prev, d_next = together(d_got_2, d_prev, d_next)
    pre_got = shift(pre, "core", CORE, 1)
    d_acc_prev, d_acc_next, d_kept, d_out_2, d_mine_2, parts, p_prev, p_next = grad_blocks(
        [(slots_2, d_keep_2, d_got_2, act, act_got, ((0, CUT, (1, 1, 2)), (CUT, rest, (2, 2))))],
        (pre, up_turned, d_prev, d_next),
    )
    pre_got, parts = together(pre_got, parts)

    d_acc_prev, d_acc_next = shift(d_acc_prev, "z", Z, 1), shift(d_acc_next, "z", Z, -1)
    d_x_2 = shift(d_out_2, "xl", XL, 1)
    u_up, u_down, u_kept, u_out, u_mine = grad_blocks(
        [
            (
                jnp.stack([z_slots, x_slots]), n_keep, n_got, pre, pre_got,
                ((0, UP_CUT, (2, 2, 4)), (UP_CUT, rest + CUT - UP_CUT, (4, 4))),
            )
        ]
    )
    d_acc_prev, d_acc_next, d_x_1, d_x_2, u_mine, parts, p_prev, p_next = together(
        d_acc_prev, d_acc_next, d_x_1, d_x_2, u_mine, parts, p_prev, p_next
    )

    u_prev, u_next = shift(u_up, "z", Z, 1), shift(u_down, "z", Z, -1)
    u_x = shift(u_out, "xl", XL, 1)
    blocks = parts.reshape(MEMBERS, tok_rows, width)
    p_prev = shift(below(blocks[4][:half], blocks[5][:half]), "y", Y, 1)
    p_next = shift(below(blocks[4][half:], blocks[5][half:]), "y", Y, -1)
    sum_0, sum_1 = add(d_kept[0], d_acc_prev[0]), add(d_kept[1], d_acc_next[0])
    d_own, d_give = jnp.where(here, sum_0, sum_1), jnp.where(here, sum_1, sum_0)
    o_prev, o_next = (
        below(add(blocks[3][:half], p_prev[half:]), blocks[3][half:]),
        below(blocks[7][:half], add(blocks[7][half:], p_next[half:])),
    )
    d_give, u_x, _, _ = together(d_give, u_x, o_prev, o_next)
    o_prev, o_next = shift(o_prev, "y", Y, 1), shift(o_next, "y", Y, -1)
    d_other = shift(d_give, "xl", XL, 1)

    m_prev = shift(add(u_kept[0], u_prev[0]), "z", Z, 1)
    m_next = shift(add(u_kept[1], u_next[0]), "z", Z, -1)
    d_other, p_prev, p_next, o_prev, o_next = together(d_other, p_prev, p_next, o_prev, o_next)
    r_other = shift(add(blocks[1], o_prev, o_next), "xh", XH, 1)
    r_prev = shift(below(add(blocks[2][:half], p_prev[:half]), blocks[2][half:]), "y", Y, 1)
    r_next = shift(below(blocks[6][:half], add(blocks[6][half:], p_next[:half])), "y", Y, -1)

    sum_0 = add(u_kept[2], u_next[1], m_prev)
    sum_1 = add(u_kept[3], u_prev[1], m_next)
    u_own, u_give = jnp.where(here, sum_0, sum_1), jnp.where(here, sum_1, sum_0)
    u_other = shift(u_give, "xl", XL, 1)
    cut = -(-d_x_1.shape[1] // 16) * 8
    u_x, d_x_2, r_prev, r_next, u_own, d_other = together(
        u_x, d_x_2, r_prev, r_next, u_own, d_other
    )
    two, side_1, side_2 = (
        add(d_mine_1[0], d_x_1[0]), add(d_mine_1[1], d_x_1[1]), add(d_mine_2[0], d_x_2[0])
    )
    one, three = jnp.where(here, side_2, side_1), jnp.where(here, side_1, side_2)
    two, one, three = (
        beside(both, add(u_mine[i], u_x[i])) for i, both in enumerate((two, one, three))
    )
    b_here = beside(add32(d_mine_2[1], d_x_2[1]), add32(u_mine[3], u_x[3]))
    b_prev = shift(below(two[:cut], one[cut:]), "z", Z, 1)
    b_next = shift(below(three[:cut], two[cut:]), "z", Z, -1)
    c_prev = shift(add(one[:cut], b_prev[:cut]), "z", Z, 1)
    c_next = shift(add(three[cut:], b_next[cut:]), "z", Z, -1)
    r_prev, r_next, r_other, b_prev = together(r_prev, r_next, r_other, b_prev)
    down_a, up_a = add32(d_own, d_other), add32(u_own, u_other)
    b_total = below(
        add32(b_here[:cut], b_next[:cut], c_prev), add32(b_here[cut:], b_prev[cut:], c_next)
    )
    down_b, up_b = b_total[:, :rest], b_total[:, rest:]
    normed_grad = add32(blocks[0], r_prev, r_next, r_other)
    weighted = norm_gain * normed_grad
    input_grad = (
        own_grad.astype(F32)
        + inverse_rms * weighted
        - inputs * inverse_rms**3 * jnp.mean(weighted * inputs, -1, keepdims=True)
    ).astype(BF16)
    grad_scale = 1.0 / math.sqrt(group_len * BLOCKS)
    return (
        input_grad,
        (beside(up_a, up_b) * grad_scale).astype(BF16),
        (beside(down_a, down_b) * grad_scale).astype(BF16),
    )


def solution(mesh):
    fine = Mesh(mesh.devices.reshape(Z, XL, CORE, Y, XH), AXES)
    dp, tensor = AXES[:3], AXES[3:]
    in_specs = (
        P(AXES, None),
        P(AXES),
        P(),
        P(AXES, None),
        P(),
        P(),
        P(None, tensor),
        P(None, tensor),
    )
    out_specs = (P(AXES, None), P(dp, tensor), P(dp, tensor))
    return jax.shard_map(
        on_device, mesh=fine, in_specs=in_specs, out_specs=out_specs, check_vma=False
    )
```

```python
import math

import jax
import jax.numpy as jnp
from jax import lax
from jax.experimental import pallas as pl
from jax.experimental.pallas import tpu as pltpu
from jax.sharding import Mesh, PartitionSpec as P

F32 = jnp.float32
BF16 = jnp.bfloat16
Z, XL, CORE, Y, XH = 4, 2, 2, 4, 2
AXES = ("z", "xl", "core", "y", "xh")
MEMBERS = Y * XH
BLOCKS = Z * XL * CORE
ID_COLS = 128
ID_BASE = 32
CUT = 1152
UP_CUT = 1152
MIB = 1024 * 1024
VMEM = pl.BlockSpec(memory_space=pltpu.VMEM)
SMEM = pl.BlockSpec(memory_space=pltpu.SMEM)
ANY = pl.BlockSpec(memory_space=pl.ANY)
HBM = pl.BlockSpec(memory_space=pltpu.HBM)


def params(mib):
    return pltpu.CompilerParams(vmem_limit_bytes=mib * MIB)


def cost(flops, moved, special=0):
    return pl.CostEstimate(flops=flops, bytes_accessed=moved, transcendentals=special)


def shift(value, axis, size, step):
    return lax.ppermute(value, axis, [(i, (i + step) % size) for i in range(size)])


def add32(*terms):
    total = terms[0].astype(F32)
    for term in terms[1:]:
        total = total + term.astype(F32)
    return total


def add(*terms):
    return add32(*terms).astype(BF16)


def together(*values):
    return lax.optimization_barrier(values)


def fetch(pieces, sem):
    copies = [pltpu.make_async_copy(src, dst, sem.at[i]) for i, (src, dst) in enumerate(pieces)]
    for copy in copies:
        copy.start()

    def wait():
        for copy in copies:
            copy.wait()

    return wait


def pieces_of(listed, out):
    at, pieces = 0, []
    for ref, first, rows in listed:
        pieces.append((ref.at[first : first + rows], out.at[at : at + rows]))
        at += rows
    return pieces


def split_parity(turned, core, pairs, keep, give):
    rows = keep.shape[0] // pairs
    for two in range(pairs // 2):
        for out, parity in ((keep, core), (give, 1 - core)):
            blocks = [
                turned[pl.ds(pl.multiple_of((2 * b + parity) * rows, 8), rows), :]
                for b in (2 * two, 2 * two + 1)
            ]
            out[2 * two * rows : (2 * two + 2) * rows, :] = jnp.concatenate(blocks, 0).astype(BF16)


def by_last(left, right):
    return lax.dot_general(left, right, (((1,), (1,)), ((), ())), preferred_element_type=F32)


def normed_kernel(core, *refs):
    ins, weight, (act, slope, keep, give) = refs[:8], refs[8], refs[9:13]
    normed, turned, held, act_s, slope_s, keep_s, give_s, in_sem, w_sem, out_sem, sem = refs[13:]
    own, other, nxt, prev, mix_prev, mix_next, far_a, far_b = ins
    full = own.shape[0]
    half = full // 2
    listed = [(own, 0, full), (other, 0, full), (nxt, 0, full), (mix_next, 0, full)]
    listed += [(mix_prev, full, half), (mix_next, full, half), (far_a, 0, half), (far_b, 0, half)]
    listed += [(prev, 0, full), (mix_prev, 0, full)]
    fetched = fetch(pieces_of(listed, normed), in_sem)
    tile = held.shape[1]
    count = held.shape[0]
    tiles = [slice(n * tile, (n + 1) * tile) for n in range(count)]
    weights = [fetch([(weight.at[tiles[n]], held.at[n])], w_sem.at[n]) for n in range(count)]
    fetched()
    for t in range(normed.shape[1] // 128):
        cols = slice(t * 128, (t + 1) * 128)
        turned[cols, :] = normed[:, cols].astype(F32).T
    split_parity(turned, core[0], BLOCKS // 2, keep_s, give_s)
    waits = [fetch([(give_s, give), (keep_s, keep)], out_sem)]
    for n, rows in enumerate(tiles):
        weights[n]()
        value = by_last(held[n], normed[...])
        below = 0.5 * (1.0 + lax.erf(value * 0.7071067811865476))
        act_s[rows, :] = (value * below).astype(BF16)
        slope_s[rows, :] = (
            below + value * jnp.exp(-0.5 * value * value) * 0.3989422804014327
        ).astype(BF16)
        waits.append(
            fetch([(act_s.at[rows], act.at[rows]), (slope_s.at[rows], slope.at[rows])], sem.at[n])
        )
    for wait in waits:
        wait()


def assemble_normed(core, ins, weight):
    rows, width = ins[0].shape[0] * MEMBERS, ins[0].shape[1]
    hidden = weight.shape[0]
    count = 4
    outs = [((hidden, rows), BF16)] * 2 + [((width // 2, rows), BF16)] * 2
    return pl.pallas_call(
        normed_kernel,
        out_shape=[jax.ShapeDtypeStruct(shape, kind) for shape, kind in outs],
        in_specs=[SMEM] + [HBM] * (len(ins) + 1),
        out_specs=[HBM] * 4,
        scratch_shapes=[
            pltpu.VMEM((rows, width), BF16),
            pltpu.VMEM((width, rows), F32),
            pltpu.VMEM((count, hidden // count, width), BF16),
        ]
        + [pltpu.VMEM(shape, kind) for shape, kind in outs]
        + [pltpu.SemaphoreType.DMA((n,)) for n in (10,)]
        + [pltpu.SemaphoreType.DMA((count, 1)), pltpu.SemaphoreType.DMA((2,))]
        + [pltpu.SemaphoreType.DMA((count, 2))],
        compiler_params=params(52),
        cost_estimate=cost(10**10, 10**7),
    )(core, *ins, weight)


def prepare_kernel(order, own, other, first, second, rows_s, turned, sorted_s, *refs):
    outs_s, in_sem, sem = refs[:2], refs[2], refs[3]
    half = own.shape[0] // 2
    listed = [(own, 0, half), (other, 0, half), (own, half, half), (other, half, half)]
    fetch(pieces_of(listed, rows_s), in_sem)()
    width = turned.shape[0]
    pair = width // (BLOCKS // 2)
    for t in range(width // 128):
        cols = slice(t * 128, (t + 1) * 128)
        turned[cols, :] = rows_s[:, cols].astype(F32).T
    waits = []
    for h, out in enumerate((first, second)):
        for p in range(4):
            at = pl.ds(pl.multiple_of(order[4 * h + p] * pair, 8), pair)
            sorted_s[p * pair : (p + 1) * pair, :] = turned[at, :]
        cols = width // 2
        lead = 0 if h else ID_COLS
        for first_col in range(0, cols, 128):
            last = min(first_col + 128, cols)
            outs_s[h][:, lead + first_col : lead + last] = (
                sorted_s[first_col : first_col + 128, :].T[:, : last - first_col].astype(BF16)
            )
        if h == 0:
            outs_s[h][:, :lead] = rows_s[:, width : width + ID_COLS]
        waits.append(fetch([(outs_s[h], out)], sem.at[h]))
    for wait in waits:
        wait()


def prepare(order, own, other, width):
    rows = 2 * own.shape[0]
    cols = width // 2
    return pl.pallas_call(
        prepare_kernel,
        out_shape=[
            jax.ShapeDtypeStruct((rows, cols + ID_COLS), BF16),
            jax.ShapeDtypeStruct((rows, cols), BF16),
        ],
        in_specs=[SMEM, HBM, HBM],
        out_specs=[HBM, HBM],
        scratch_shapes=[
            pltpu.VMEM((rows, width + ID_COLS), BF16),
            pltpu.VMEM((width, rows), F32),
            pltpu.VMEM((-(-cols // 128) * 128, rows), F32),
            pltpu.VMEM((rows, cols + ID_COLS), BF16),
            pltpu.VMEM((rows, cols), BF16),
            pltpu.SemaphoreType.DMA((4,)),
            pltpu.SemaphoreType.DMA((2, 1)),
        ],
        compiler_params=params(52),
        cost_estimate=cost(10**8, 10**6),
    )(order, own, other)


def joined_pieces(ins, joined):
    at, pieces = 0, []
    for ref in ins:
        rows = ref.shape[0]
        pieces.append((ref, joined.at[at : at + rows]))
        at += rows
    return pieces


def to_image_order(chooser, joined, lead, scale, turned, own):
    cols = turned.shape[0]
    for first in range(0, cols, 640):
        last = min(first + 640, cols)
        grads = jnp.dot(
            chooser[...], joined[:, lead + first : lead + last], preferred_element_type=F32
        )
        own[first:last, :] = grads[:128].T
        turned[first:last, :] = (grads * scale[:, first:last]).T


def first_kernel(core, order, scales, positions, *refs):
    ins, (scaled, keep, give, own_turned, chooser_out) = refs[:5], refs[5:10]
    joined, turned, scaled_s, keep_s, give_s, chooser, own_s, in_sem, sem, give_sem = refs[10:]
    del order
    fetch(joined_pieces(ins, joined), in_sem)()
    tags = joined[:, :ID_COLS].astype(F32).T
    places = tags[0:1, :] * ID_BASE + tags[1:2, :]
    chooser[...] = (positions[...] == places).astype(F32).astype(BF16)
    to_image_order(chooser, joined, ID_COLS, scales[0:1, :], turned, own_s)
    waits = [fetch([(own_s, own_turned), (chooser, chooser_out)], sem)]
    scaled_s[...] = turned[...].astype(BF16)
    split_parity(turned, core[0], 4, keep_s, give_s)
    waits.append(fetch([(give_s, give), (keep_s, keep), (scaled_s, scaled)], give_sem))
    for wait in waits:
        wait()


def route_first(core, order, scales, positions, ins):
    rows, cols = positions.shape[0], scales.shape[1]
    turned = ((cols // 2, rows), BF16)
    outs = [((cols, rows), BF16), turned, turned, ((cols, 128), F32), ((rows, rows), BF16)]
    return pl.pallas_call(
        first_kernel,
        out_shape=[jax.ShapeDtypeStruct(shape, kind) for shape, kind in outs],
        in_specs=[SMEM, SMEM, VMEM, VMEM] + [HBM] * len(ins),
        out_specs=[HBM] * 5,
        scratch_shapes=[
            pltpu.VMEM((rows, cols + ID_COLS), BF16),
            pltpu.VMEM((cols, rows), F32),
            pltpu.VMEM((cols, rows), BF16),
            pltpu.VMEM((cols // 2, rows), BF16),
            pltpu.VMEM((cols // 2, rows), BF16),
            pltpu.VMEM((rows, rows), BF16),
            pltpu.VMEM((cols, 128), F32),
        ]
        + [pltpu.SemaphoreType.DMA((n,)) for n in (5, 2, 3)],
        compiler_params=params(52),
        cost_estimate=cost(10**9, 10**7),
    )(core, order, scales, positions, *ins)


def middle_kernel(core, order, *refs):
    scales, chooser_in, own_first, scaled_1, slope, down = refs[:6]
    ins, (keep, give, own_grad, pre) = refs[6:11], refs[11:15]
    joined, turned, scaled, keep_s, give_s, chooser, own_s, own_rows, own_out = refs[15:24]
    slope_s, down_s, pre_s = refs[24:27]
    in_sem, s_sem, d_sem, give_sem, own_sem, pre_sem = refs[27:]
    cols = joined.shape[1]
    pair = cols // 4
    got = fetch(
        joined_pieces(ins, joined)
        + [(chooser_in, chooser), (own_first, own_s.at[0])],
        in_sem,
    )
    more = [(slope, slope_s)]
    for p in range(4):
        at = pl.ds(pl.multiple_of(order[p] * pair, 16), pair)
        more.append((scaled_1.at[p * pair : (p + 1) * pair], scaled.at[at]))
    got_more = fetch(more, s_sem)
    count = 2
    tile = down.shape[0] // count
    tiles = [slice(n * tile, (n + 1) * tile) for n in range(count)]
    got_down = [fetch([(down.at[rows], down_s.at[rows])], d_sem.at[n]) for n, rows in enumerate(tiles)]
    got()
    to_image_order(chooser, joined, 0, scales[1:2, :], turned, own_s.at[1])
    got_more()
    for p in range(4):
        here = slice(p * pair, (p + 1) * pair)
        place = order[4 + p] * pair
        scaled[pl.ds(pl.multiple_of(place, 16), pair), :] = turned[here, :].astype(BF16)
    split_parity(turned, core[0], 4, keep_s, give_s)
    waits = [fetch([(give_s, give), (keep_s, keep)], give_sem)]
    for n, rows in enumerate(tiles):
        got_down[n]()
        value = jnp.dot(down_s[rows, :], scaled[...], preferred_element_type=F32)
        pre_s[rows, :] = (value * slope_s[rows, :].astype(F32)).astype(BF16)
        waits.append(fetch([(pre_s.at[rows], pre.at[rows])], pre_sem.at[n]))
    for p in range(8):
        at = pl.ds(pl.multiple_of(order[p] * pair, 8), pair)
        own_rows[at, :] = own_s[p // 4, (p % 4) * pair : (p % 4 + 1) * pair, :]
    for t in range(own_rows.shape[0] // 128):
        here = slice(t * 128, (t + 1) * 128)
        own_out[:, here] = own_rows[here, :].T[: own_out.shape[0]].astype(BF16)
    waits.append(fetch([(own_out, own_grad)], own_sem))
    for wait in waits:
        wait()


def middle(core, order, scales, chooser, own_first, scaled_1, slope, down, ins):
    hidden, width = down.shape
    rows, cols = chooser.shape[0], width // 2
    turned = ((cols // 2, rows), BF16)
    outs = [turned, turned, ((rows // MEMBERS, width), BF16), ((hidden, rows), BF16)]
    return pl.pallas_call(
        middle_kernel,
        out_shape=[jax.ShapeDtypeStruct(shape, kind) for shape, kind in outs],
        in_specs=[SMEM, SMEM, VMEM] + [HBM] * (5 + len(ins)),
        out_specs=[HBM] * 4,
        scratch_shapes=[
            pltpu.VMEM((rows, cols), BF16),
            pltpu.VMEM((cols, rows), F32),
            pltpu.VMEM((width, rows), BF16),
            pltpu.VMEM((cols // 2, rows), BF16),
            pltpu.VMEM((cols // 2, rows), BF16),
            pltpu.VMEM((rows, rows), BF16),
            pltpu.VMEM((2, cols, 128), F32),
            pltpu.VMEM((width, 128), F32),
            pltpu.VMEM((rows // MEMBERS, width), BF16),
            pltpu.VMEM((hidden, rows), BF16),
            pltpu.VMEM((hidden, width), BF16),
            pltpu.VMEM((hidden, rows), BF16),
        ]
        + [pltpu.SemaphoreType.DMA((n,)) for n in (7, 5)]
        + [pltpu.SemaphoreType.DMA((2, 1))]
        + [pltpu.SemaphoreType.DMA((n,)) for n in (2, 1)]
        + [pltpu.SemaphoreType.DMA((2, 1))],
        compiler_params=params(52),
        cost_estimate=cost(10**10, 10**7),
    )(core, order, scales, chooser, own_first, scaled_1, slope, down, *ins)


def blocks_kernel(jobs, sums, *refs):
    group = 800
    count = len(jobs)
    if sums:
        refs, (pre_s, up_s, sums_s, more_s, up_sem, sums_sem, more_sem) = refs[:-7], refs[-7:]
        pre, up, more_up, more_down = refs[5 * count : 5 * count + 4]
        refs = refs[: 5 * count] + refs[5 * count + 4 :]
    ins, refs = refs[: 5 * count], refs[5 * count :]
    total = sum(len(sizes) for parts in jobs for _, _, sizes in parts)
    pieces = sum(len(parts) for parts in jobs)
    scratch = refs[-(3 * count + 3 * pieces) :]
    outs, sums_outs = refs[:total], refs[total : total + 3]
    todo = []
    at_out = at = 0
    for k, parts in enumerate(jobs):
        slots, left, left_got, right, right_got = ins[5 * k : 5 * k + 5]
        left_s, l_sem, r_sem = scratch[at : at + 3]
        at += 3
        rows_in = left.shape[1]
        waits_r, waits_l, each = [], [], []

        def fetch_left(g, left=left, left_got=left_got, left_s=left_s, l_sem=l_sem):
            here = slice(g * group, (g + 1) * group)
            return fetch(
                [
                    (left.at[here], left_s.at[here, :rows_in]),
                    (left_got.at[here], left_s.at[here, rows_in:]),
                ],
                l_sem.at[g],
            )

        for i, (first, cols, sizes) in enumerate(parts):
            right_s, stage, sem = scratch[at : at + 3]
            at += 3
            here = slice(first, first + cols)
            waits_r.append(
                fetch(
                    [
                        (right.at[here], right_s.at[:cols, :rows_in]),
                        (right_got.at[here], right_s.at[:cols, rows_in:]),
                    ],
                    r_sem.at[i],
                )
            )
            if i == 0:
                waits_l = [fetch_left(g) for g in range(left.shape[0] // group)]
            each.append((i, cols, sizes, right_s, stage, sem, outs[at_out : at_out + len(sizes)]))
            at_out += len(sizes)
        todo.append((slots, left_s, waits_l, waits_r, each))
    if sums:
        got_more = fetch(
            [
                (more_up.at[0], more_s.at[0]),
                (more_down.at[0], more_s.at[1]),
                (more_down.at[1], more_s.at[2]),
                (more_up.at[1], more_s.at[3]),
            ],
            more_sem,
        )
        got_up = fetch([(pre, pre_s), (up, up_s)], up_sem)
    for slots, left_s, waits_l, waits_r, each in todo:
        for i, cols, sizes, right_s, stage, sem, targets in each:
            waits_r[i]()
            block = stage.shape[1]
            per = group // block
            for g in range(len(waits_l)):
                if i == 0:
                    waits_l[g]()
                product = by_last(left_s[g * group : (g + 1) * group, :], right_s[...])
                for b in range(per):
                    j = g * per + b
                    value = product[b * block : (b + 1) * block, :cols]
                    if sums and i == 0:
                        if j == 0:
                            got_more()
                        value = value + more_s[j].astype(F32)
                    stage[j] = value.astype(BF16)
                    slot = slots[i, j]
                    first = 0
                    for out, size in zip(targets, sizes):

                        @pl.when((slot >= first) & (slot < first + size))
                        def _(out=out, first=first, j=j, slot=slot, stage=stage, sem=sem):
                            pltpu.make_async_copy(
                                stage.at[j], out.at[slot - first], sem.at[j]
                            ).start()

                        first += size
    if sums:
        got_up()
        for first in range(0, up.shape[1], 512):
            here = slice(first, min(first + 512, up.shape[1]))
            sums_s[:, here] = lax.dot_general(
                pre_s[...], up_s[:, here], (((0,), (0,)), ((), ())), preferred_element_type=F32
            ).astype(BF16)
        eighth = sums_s.shape[0] // MEMBERS
        half = eighth // 2
        sums_out, first_out, last_out = sums_outs
        copies = [(sums_s, sums_out)]
        for i in range(2):
            at = (4 + i) * eighth
            here = slice(i * half, (i + 1) * half)
            copies.append((sums_s.at[at : at + half], first_out.at[here]))
            copies.append((sums_s.at[at + half : at + eighth], last_out.at[here]))
        fetch(copies, sums_sem)()
    for _, _, _, _, each in todo:
        for _, _, _, _, stage, sem, targets in each:
            for j in range(stage.shape[0]):
                pltpu.make_async_copy(stage.at[j], targets[0].at[0], sem.at[j]).wait()


def grad_blocks(jobs, sums=()):
    block = 200
    specs, ins, outs, scratch = [], [], [], []
    for slots, left, left_got, right, right_got, parts in jobs:
        width, rows = left.shape
        specs += [SMEM] + [HBM] * 4
        ins += [slots, left, left_got, right, right_got]
        scratch += [
            pltpu.VMEM((width, 2 * rows), BF16),
            pltpu.SemaphoreType.DMA((width // 800, 2)),
            pltpu.SemaphoreType.DMA((len(parts), 2)),
        ]
        for _, cols, sizes in parts:
            outs += [jax.ShapeDtypeStruct((size, block, cols), BF16) for size in sizes]
            scratch += [
                pltpu.VMEM((-(-cols // 256) * 256, 2 * rows), BF16),
                pltpu.VMEM((width // block, block, cols), BF16),
                pltpu.SemaphoreType.DMA((width // block,)),
            ]
    lists = [job[-1] for job in jobs]
    if sums:
        (hidden, rows), width = sums[0].shape, sums[1].shape[1]
        specs += [HBM] * 4
        ins += list(sums)
        outs.append(jax.ShapeDtypeStruct((rows, width), BF16))
        outs += [jax.ShapeDtypeStruct((rows // MEMBERS, width), BF16)] * 2
        scratch += [
            pltpu.VMEM((hidden, rows), BF16),
            pltpu.VMEM((hidden, width), BF16),
            pltpu.VMEM((rows, width), BF16),
            pltpu.VMEM((4, *sums[2].shape[1:]), BF16),
            pltpu.SemaphoreType.DMA((2,)),
            pltpu.SemaphoreType.DMA((5,)),
            pltpu.SemaphoreType.DMA((4,)),
        ]

    def kernel(*refs):
        blocks_kernel(lists, bool(sums), *refs)

    return pl.pallas_call(
        kernel,
        out_shape=outs,
        in_specs=specs,
        out_specs=[HBM] * len(outs),
        scratch_shapes=scratch,
        compiler_params=params(52),
        cost_estimate=cost(10**10, 10**7),
    )(*ins)


def z_order(z, xl):
    pairs = [(2, 0), (1, 1), (2, 1), (3, 0), (1, 0), (3, 1), (0, 0), (0, 1)]
    return [((z + dz) % Z) * XL + x for dz, x in pairs]


def x_order(z, xl):
    pairs = [(dz, dx) for dx in (1, 0) for dz in (2, 1, 3, 0)]
    return [((z + dz) % Z) * XL + (xl + dx) % XL for dz, dx in pairs]


def slots_of(order):
    order = jnp.stack(order).astype(jnp.int32)
    index = jnp.arange(order.shape[0], dtype=jnp.int32)
    return jnp.sum(jnp.where(order[None, :] == index[:, None], index[None, :], 0), 1)


def beside(*parts):
    return jnp.concatenate(parts, 1)


def below(*parts):
    return jnp.concatenate(parts, 0)


def on_device(
    lm_grad, encoder_row, patch_count, hidden_in, norm_gain, layer_scale, up_weight, down_weight
):
    tok_rows, width = hidden_in.shape
    rest = up_weight.shape[1] - CUT
    up_turned, down_turned = up_weight.T, down_weight.T
    group_len = tok_rows * MEMBERS
    per_pair = tok_rows // BLOCKS
    half = tok_rows // 2
    z, xl, core = lax.axis_index("z"), lax.axis_index("xl"), lax.axis_index("core")
    y, xh = lax.axis_index("y"), lax.axis_index("xh")
    group = (z * XL + xl) * CORE + core
    core_at = core.reshape(1).astype(jnp.int32)
    z_slots, x_slots = slots_of(z_order(z, xl)), slots_of(x_order(z, xl))

    inputs = hidden_in.astype(F32)
    inverse_rms = lax.rsqrt(jnp.mean(inputs * inputs, -1, keepdims=True) + 1e-06)
    normed_own = (inputs * inverse_rms * norm_gain).astype(BF16)

    n_prev = shift(normed_own, "y", Y, 1)
    n_next = shift(normed_own, "y", Y, -1)
    n_other = shift(normed_own, "xh", XH, 1)

    image, place = encoder_row // group_len, encoder_row % group_len
    index = jnp.arange(tok_rows, dtype=jnp.int32)
    same = (image[:, None] == image[None, :]) & (index[None, :] < index[:, None])
    slot = image * per_pair + jnp.sum(same.astype(jnp.int32), 1)
    sorter = (slot[None, :] == index[:, None]).astype(BF16)
    column = jnp.arange(ID_COLS, dtype=jnp.int32)[None, :]
    tags = jnp.where(
        column == 0,
        (place // ID_BASE)[:, None],
        jnp.where(column == 1, (place % ID_BASE)[:, None], 0),
    ).astype(BF16)
    ordered = jnp.dot(sorter, beside(lm_grad, tags), preferred_element_type=F32).astype(BF16)
    arrived = lax.all_to_all(
        ordered.reshape(BLOCKS, per_pair, width + ID_COLS),
        ("z", "xl", "core"),
        split_axis=0,
        concat_axis=0,
    ).reshape(tok_rows, width + ID_COLS)

    n_prev, n_next, n_other = together(n_prev, n_next, n_other)
    mix_prev = shift(below(n_other, n_prev[:half]), "y", Y, 1)
    mix_next = shift(below(n_other, n_next[half:]), "y", Y, -1)
    g_other = shift(arrived, "xh", XH, 1)
    block = jnp.arange(MEMBERS, dtype=jnp.int32)
    member = ((block // XH + y) % Y) * XH + (block % XH + xh) % XH
    positions = (member[:, None] * tok_rows + index[None, :]).reshape(group_len, 1)
    limit = lax.dynamic_index_in_dim(patch_count, group, 0, keepdims=False)
    positions = jnp.where(positions < limit, positions, -1).astype(F32)
    order = jnp.stack(z_order(z, xl)).astype(jnp.int32)
    scale_rows = layer_scale.reshape(BLOCKS // 2, -1)[order].reshape(2, width // 2)
    mix_prev, mix_next, g_other, arrived, positions, scale_rows = together(
        mix_prev, mix_next, g_other, arrived, positions, scale_rows
    )

    far_a, far_b, arrived, g_other = together(
        mix_prev[:half], mix_next[half:tok_rows], arrived, g_other
    )
    far_a, far_b = shift(far_a, "y", Y, 1), shift(far_b, "y", Y, -1)
    g_1, g_2 = prepare(order, arrived, g_other, width)

    g_prev_1, g_next_1 = shift(g_1, "y", Y, 1), shift(g_1, "y", Y, -1)
    g_prev_2, g_next_2 = shift(g_2, "y", Y, 1), shift(g_2, "y", Y, -1)
    act, slope, n_keep, n_give = assemble_normed(
        core_at, (normed_own, n_other, n_next, n_prev, mix_prev, mix_next, far_a, far_b), up_turned
    )
    g_prev_1, g_next_1, g_prev_2, g_next_2, act, n_give = together(
        g_prev_1, g_next_1, g_prev_2, g_next_2, act, n_give
    )

    f_prev_1 = shift(g_prev_1[:tok_rows], "y", Y, 1)
    f_next_1 = shift(g_next_1[tok_rows:], "y", Y, -1)
    f_prev_2 = shift(g_prev_2[:tok_rows], "y", Y, 1)
    f_next_2 = shift(g_next_2[tok_rows:], "y", Y, -1)
    s_1, d_keep_1, d_give_1, own_first, chooser = route_first(
        core_at, order, scale_rows, positions, (g_1, g_prev_1, g_next_1, f_prev_1, f_next_1)
    )
    d_give_1, act = together(d_give_1, act)
    d_got_1 = shift(d_give_1, "core", CORE, 1)
    act_got = shift(act, "core", CORE, 1)
    here = xl == 0
    straight = jnp.arange(4, dtype=jnp.int32)
    slots_1 = jnp.stack([straight, jnp.where(here, jnp.array([2, 1, 0, 3]), jnp.array([0, 3, 2, 1]))])
    slots_2 = jnp.stack([straight, jnp.where(here, jnp.array([2, 0, 3, 1]), jnp.array([0, 2, 1, 3]))])
    slots_1, slots_2 = slots_1.astype(jnp.int32), slots_2.astype(jnp.int32)
    d_got_1, act_got, n_give = together(d_got_1, act_got, n_give)
    d_up, d_down, d_out_1, d_mine_1 = grad_blocks(
        [(slots_1, d_keep_1, d_got_1, act, act_got, ((0, CUT, (2, 2)), (CUT, rest, (2, 2))))]
    )
    d_prev, d_next = shift(d_up, "z", Z, 1), shift(d_down, "z", Z, -1)
    d_x_1 = shift(d_out_1, "xl", XL, 1)
    d_out_1, n_give = together(d_out_1, n_give)
    n_got = shift(n_give, "core", CORE, 1)
    f_prev_2, f_next_2, d_mine_1 = together(f_prev_2, f_next_2, d_mine_1)

    d_keep_2, d_give_2, own_grad, pre = middle(
        core_at, order, scale_rows, chooser, own_first, s_1, slope, down_turned,
        (g_2, g_prev_2, g_next_2, f_prev_2, f_next_2),
    )
    d_got_2 = shift(d_give_2, "core", CORE, 1)
    d_got_2, d_prev, d_next = together(d_got_2, d_prev, d_next)
    pre_got = shift(pre, "core", CORE, 1)
    d_acc_prev, d_acc_next, d_kept, d_out_2, d_mine_2, parts, p_prev, p_next = grad_blocks(
        [(slots_2, d_keep_2, d_got_2, act, act_got, ((0, CUT, (1, 1, 2)), (CUT, rest, (2, 2))))],
        (pre, up_turned, d_prev, d_next),
    )
    pre_got, parts = together(pre_got, parts)

    d_acc_prev, d_acc_next = shift(d_acc_prev, "z", Z, 1), shift(d_acc_next, "z", Z, -1)
    d_x_2 = shift(d_out_2, "xl", XL, 1)
    u_up, u_down, u_kept, u_out, u_mine = grad_blocks(
        [
            (
                jnp.stack([z_slots, x_slots]), n_keep, n_got, pre, pre_got,
                ((0, UP_CUT, (2, 2, 4)), (UP_CUT, rest + CUT - UP_CUT, (4, 4))),
            )
        ]
    )
    d_acc_prev, d_acc_next, d_x_1, d_x_2, u_mine, parts, p_prev, p_next = together(
        d_acc_prev, d_acc_next, d_x_1, d_x_2, u_mine, parts, p_prev, p_next
    )

    u_prev, u_next = shift(u_up, "z", Z, 1), shift(u_down, "z", Z, -1)
    u_x = shift(u_out, "xl", XL, 1)
    blocks = parts.reshape(MEMBERS, tok_rows, width)
    p_prev = shift(below(blocks[4][:half], blocks[5][:half]), "y", Y, 1)
    p_next = shift(below(blocks[4][half:], blocks[5][half:]), "y", Y, -1)
    sum_0, sum_1 = add(d_kept[0], d_acc_prev[0]), add(d_kept[1], d_acc_next[0])
    d_own, d_give = jnp.where(here, sum_0, sum_1), jnp.where(here, sum_1, sum_0)
    o_prev, o_next = (
        below(add(blocks[3][:half], p_prev[half:]), blocks[3][half:]),
        below(blocks[7][:half], add(blocks[7][half:], p_next[half:])),
    )
    d_give, u_x, _, _ = together(d_give, u_x, o_prev, o_next)
    o_prev, o_next = shift(o_prev, "y", Y, 1), shift(o_next, "y", Y, -1)
    d_other = shift(d_give, "xl", XL, 1)

    m_prev = shift(add(u_kept[0], u_prev[0]), "z", Z, 1)
    m_next = shift(add(u_kept[1], u_next[0]), "z", Z, -1)
    d_other, p_prev, p_next, o_prev, o_next = together(d_other, p_prev, p_next, o_prev, o_next)
    r_other = shift(add(blocks[1], o_prev, o_next), "xh", XH, 1)
    r_prev = shift(below(add(blocks[2][:half], p_prev[:half]), blocks[2][half:]), "y", Y, 1)
    r_next = shift(below(blocks[6][:half], add(blocks[6][half:], p_next[:half])), "y", Y, -1)

    sum_0 = add(u_kept[2], u_next[1], m_prev)
    sum_1 = add(u_kept[3], u_prev[1], m_next)
    u_own, u_give = jnp.where(here, sum_0, sum_1), jnp.where(here, sum_1, sum_0)
    u_other = shift(u_give, "xl", XL, 1)
    cut = -(-d_x_1.shape[1] // 16) * 8
    u_x, d_x_2, r_prev, r_next, u_own, d_other = together(
        u_x, d_x_2, r_prev, r_next, u_own, d_other
    )
    two, side_1, side_2 = (
        add(d_mine_1[0], d_x_1[0]), add(d_mine_1[1], d_x_1[1]), add(d_mine_2[0], d_x_2[0])
    )
    one, three = jnp.where(here, side_2, side_1), jnp.where(here, side_1, side_2)
    two, one, three = (
        beside(both, add(u_mine[i], u_x[i])) for i, both in enumerate((two, one, three))
    )
    b_here = beside(add32(d_mine_2[1], d_x_2[1]), add32(u_mine[3], u_x[3]))
    b_prev = shift(below(two[:cut], one[cut:]), "z", Z, 1)
    b_next = shift(below(three[:cut], two[cut:]), "z", Z, -1)
    c_prev = shift(add(one[:cut], b_prev[:cut]), "z", Z, 1)
    c_next = shift(add(three[cut:], b_next[cut:]), "z", Z, -1)
    r_prev, r_next, r_other, b_prev = together(r_prev, r_next, r_other, b_prev)
    down_a, up_a = add32(d_own, d_other), add32(u_own, u_other)
    b_total = below(
        add32(b_here[:cut], b_next[:cut], c_prev), add32(b_here[cut:], b_prev[cut:], c_next)
    )
    down_b, up_b = b_total[:, :rest], b_total[:, rest:]
    normed_grad = add32(blocks[0], r_prev, r_next, r_other)
    weighted = norm_gain * normed_grad
    input_grad = (
        own_grad.astype(F32)
        + inverse_rms * weighted
        - inputs * inverse_rms**3 * jnp.mean(weighted * inputs, -1, keepdims=True)
    ).astype(BF16)
    grad_scale = 1.0 / math.sqrt(group_len * BLOCKS)
    return (
        input_grad,
        (beside(up_a, up_b) * grad_scale).astype(BF16),
        (beside(down_a, down_b) * grad_scale).astype(BF16),
    )


def solution(mesh):
    fine = Mesh(mesh.devices.reshape(Z, XL, CORE, Y, XH), AXES)
    dp, tensor = AXES[:3], AXES[3:]
    in_specs = (
        P(AXES, None),
        P(AXES),
        P(),
        P(AXES, None),
        P(),
        P(),
        P(None, tensor),
        P(None, tensor),
    )
    out_specs = (P(AXES, None), P(dp, tensor), P(dp, tensor))
    return jax.shard_map(
        on_device, mesh=fine, in_specs=in_specs, out_specs=out_specs, check_vma=False
    )
```
